32 devices in a mesh: dp: 16 (over z, y, x), mp: 2 (over core).
Axes of the slice: x: 2, y: 2, z: 4, core: 2. Of those that a mesh axis runs over, the one named last changes fastest.
Arguments:
- patches: bfloat16 [12544, 768], P(('dp', 'mp')), may hold values from -6 to 6
- cotangent: bfloat16 [12544, 768], P(('dp', 'mp')), may hold values from -6 to 6
- patch_counts: int32 [64], P('dp'), may hold values from 0 to 576, as said below
- qkv_weight: float32 [2, 768, 3, 768], P(None, 'dp', None, 'mp'), may hold values from -0.21875 to 0.21875
- out_weight: float32 [2, 768, 768], P(None, 'mp', 'dp'), may hold values from -1.5 to 1.5
- up_weight: float32 [2, 768, 3072], P(None, 'dp', 'mp'), may hold values from -0.21875 to 0.21875
- down_weight: float32 [2, 3072, 768], P(None, 'mp', 'dp'), may hold values from -0.109375 to 0.109375
- norms: float32 [2, 4, 768], replicated
- qkv_rows: float32 [2, 768], P(None, 'dp'), may hold values from 1568 to 25088
- qkv_cols: float32 [2, 3, 768], P(None, None, 'mp'), may hold values from 1568 to 25088
- out_rows: float32 [2, 768], P(None, 'mp'), may hold values from 1568 to 50176
- out_cols: float32 [2, 768], P(None, 'dp'), may hold values from 1568 to 50176
- up_rows: float32 [2, 768], P(None, 'dp'), may hold values from 196 to 3136
- up_cols: float32 [2, 3072], P(None, 'mp'), may hold values from 196 to 3136
- down_rows: float32 [2, 3072], P(None, 'mp'), may hold values from 1045 to 12544
- down_cols: float32 [2, 768], P(None, 'dp'), may hold values from 1045 to 12544
- norm_state: float32 [2, 4, 768], P(None, None, 'dp'), may hold values from 1568 to 25088
Outputs:
- activations: bfloat16 [12544, 768], P(('dp', 'mp'))
- input_grad: float32 [12544, 768], P(('dp', 'mp'))
- qkv_grad: float32 [2, 768, 3, 768], P(None, 'dp', None, 'mp')
- out_grad: float32 [2, 768, 768], P(None, 'mp', 'dp')
- up_grad: float32 [2, 768, 3072], P(None, 'dp', 'mp')
- down_grad: float32 [2, 3072, 768], P(None, 'mp', 'dp')
- norm_grad: float32 [2, 4, 768], P(None, None, 'dp')
- qkv_new: float32 [2, 768, 3, 768], P(None, 'dp', None, 'mp')
- out_new: float32 [2, 768, 768], P(None, 'mp', 'dp')
- up_new: float32 [2, 768, 3072], P(None, 'dp', 'mp')
- down_new: float32 [2, 3072, 768], P(None, 'mp', 'dp')
- norm_new: float32 [2, 4, 768], P(None, None, 'dp')
- qkv_copy: bfloat16 [2, 768, 3, 768], P(None, 'dp', None, 'mp')
- out_copy: bfloat16 [2, 768, 768], P(None, 'mp', 'dp')
- up_copy: bfloat16 [2, 768, 3072], P(None, 'dp', 'mp')
- down_copy: bfloat16 [2, 3072, 768], P(None, 'mp', 'dp')
- qkv_rows_new: float32 [2, 768], P(None, 'dp')
- qkv_cols_new: float32 [2, 3, 768], P(None, None, 'mp')
- out_rows_new: float32 [2, 768], P(None, 'mp')
- out_cols_new: float32 [2, 768], P(None, 'dp')
- up_rows_new: float32 [2, 768], P(None, 'dp')
- up_cols_new: float32 [2, 3072], P(None, 'mp')
- down_rows_new: float32 [2, 3072], P(None, 'mp')
- down_cols_new: float32 [2, 768], P(None, 'dp')
- attention_moments: float32 [2, 2, 768], P(None, None, 'dp')
- feedforward_moments: float32 [2, 2, 768], P(None, None, 'dp')
- update_rms: float32 [2, 8], replicated
The draws below stay inside these ranges and needn't reach their ends.
Inputs may be any that keep to these rules, and one draw needn't show every extreme that they name: `patch_counts`: each index of dp owns 4 slots in a row; they list its 384 px images (576 patches) first, then its 224 px images (196 patches), then empty slots (0). The patches of one index of dp total at most 784, exactly 784 on some index in every draw, and half of 784 or more on every index; some index holds a 384 px image in every draw.
All inputs are finite; a program needn't handle non-finite values.
Results may differ from the reference program's by a relative error of at most 0.028.
Values may be sent and summed in bfloat16 or wider, within the bound.
A program may use at most 256 MiB of HBM per device.

```python
import math
import jax
import jax.numpy as jnp
from jax import lax

D = 768
HEADS = 12
HEAD_DIM = 64
FF = 3072
LAYERS = 2
SMALL_PATCHES = 196
LARGE_PATCHES = 576
SLOTS = 4
TOK_DEV = 784
TOKENS = 12544
IMAGES = 64
N_DP = 16


def draw_patch_counts(key, part):
    key = jax.random.fold_in(key, 5)
    keys = jax.random.split(key, 4)
    devices = IMAGES // SLOTS
    capacity = SLOTS * SMALL_PATCHES
    most_large = capacity // LARGE_PATCHES
    places = jnp.arange(devices, dtype=jnp.int32)
    large = jax.random.randint(keys[0], (devices,), 0, most_large + 1)
    filled = jax.random.randint(keys[1], (), 0, devices)
    holder = (filled + 1 + jax.random.randint(keys[2], (), 0, devices - 1)) % devices
    large = jnp.where(places == holder, jnp.maximum(large, 1), large)
    room = (capacity - large * LARGE_PATCHES) // SMALL_PATCHES
    fewest = jnp.where(large > 0, 0, (room + 1) // 2)
    small = jax.random.randint(keys[3], (devices,), fewest, room + 1)
    large = jnp.where(places == filled, 0, large)
    small = jnp.where(places == filled, SLOTS, small)
    slot = jnp.arange(SLOTS, dtype=jnp.int32)[None, :]
    counts = jnp.where(slot < large[:, None], LARGE_PATCHES, jnp.where(slot < (large + small)[:, None], SMALL_PATCHES, 0))
    return counts.reshape(-1).astype(jnp.int32)


def draw_norms(key, part):
    key = jax.random.fold_in(key, 11)
    first, second = jax.random.split(key)
    rise = 0.5 + jnp.arange(D, dtype=jnp.float32) / D
    rough = jnp.exp(jax.random.uniform(first, (LAYERS, 2, D), jnp.float32, -0.5, 0.5))
    shift = 0.3 * jax.random.normal(second, (LAYERS, 2, D), jnp.float32)
    gains = rough * rise
    return jnp.stack([gains[:, 0], shift[:, 0], gains[:, 1], shift[:, 1]], axis=1).astype(jnp.float32)


def spiked(entries, key, source, target, blocks, factor):
    owner, partner = [(jnp.arange(entries.shape[dim]) // (entries.shape[dim] // blocks)).reshape([-1 if axis == dim else 1 for axis in range(entries.ndim)]) for dim in (source, target)]
    chosen = jax.random.permutation(key, blocks)[partner]
    strong = (owner == chosen) | (owner == (partner + blocks // 2) % blocks)
    return jnp.where(strong, factor * entries, entries)


def block_scale(own_key, extent, cuts, smallest, largest):
    level, own = 1.0, jax.random.fold_in(own_key, 6)
    for dim, shards_of in cuts:
        steps = jnp.exp(jax.random.uniform(jax.random.fold_in(own, dim), (shards_of,), jnp.float32, smallest / len(cuts), largest / len(cuts)))
        level = level * jnp.repeat(steps, extent[dim] // shards_of).reshape([-1 if axis == dim else 1 for axis in range(len(extent))])
    return level


def gaussian(own_key, extent, scale, limit, shards=(), held_as=jnp.bfloat16):
    loudness = block_scale(own_key, extent, shards, -0.22, 0.18) if shards else 1.0
    values = jax.random.normal(own_key, extent, jnp.float32) * scale * loudness
    return jnp.minimum(jnp.maximum(values, -limit), limit).astype(held_as)


def noise_with(rng, shape, scale, most, shards, heavy, kind=jnp.bfloat16):
    entries = scale * jax.random.normal(rng, shape, jnp.float32)
    if shards:
        entries = entries * block_scale(rng, shape, shards, -0.22, 0.18)
    return jnp.clip(spiked(entries, jax.random.fold_in(rng, 3), *heavy), -most, most).astype(kind)


def setup_inputs(seed: int = 0) -> dict:
    key_list = jax.random.split(jax.random.key(seed), 18)
    patches = noise_with(key_list[0], (TOKENS, D), 1.0, 6.0, ((0, 32),), (0, 1, 32, 2.75))
    cotangent = gaussian(key_list[1], (TOKENS, D), 1.0, 6.0, ((0, 32),))
    patch_counts = draw_patch_counts(jax.random.fold_in(key_list[17], 71), 0)
    qkv_weight = gaussian(key_list[3], (LAYERS, D, 3, D), D ** -0.5, 0.21875, ((1, 16), (3, 2)), jnp.float32)
    out_weight = gaussian(key_list[4], (LAYERS, D, D), (12 * D // LARGE_PATCHES) ** -0.5, 1.5, ((1, 2), (2, 16)), jnp.float32)
    up_weight = gaussian(key_list[5], (LAYERS, D, FF), D ** -0.5, 0.21875, ((1, 16), (2, 2)), jnp.float32)
    down_weight = gaussian(key_list[6], (LAYERS, FF, D), FF ** -0.5, 0.109375, ((1, 2), (2, 16)), jnp.float32)
    norms = draw_norms(jax.random.fold_in(key_list[17], 71), 0)
    qkv_rows = jnp.clip(jnp.exp(math.log(25088.0) - 2.7725887 * jax.random.uniform(key_list[8], (LAYERS, D), jnp.float32) ** block_scale(key_list[8], (LAYERS, D), ((1, 16),), -0.2, 0.2)), 1568.0, 25088.0)
    qkv_cols = jnp.clip(jnp.exp(math.log(25088.0) - 2.7725887 * jax.random.uniform(key_list[9], (LAYERS, 3, D), jnp.float32) ** block_scale(key_list[9], (LAYERS, 3, D), ((2, 2),), -0.2, 0.2)), 1568.0, 25088.0)
    out_rows = jnp.clip(jnp.exp(math.log(50176.0) - 3.465736 * jax.random.uniform(key_list[10], (LAYERS, D), jnp.float32) ** block_scale(key_list[10], (LAYERS, D), ((1, 2),), -0.2, 0.2)), 1568.0, 50176.0)
    out_cols = jnp.clip(jnp.exp(math.log(50176.0) - 3.465736 * jax.random.uniform(key_list[11], (LAYERS, D), jnp.float32) ** block_scale(key_list[11], (LAYERS, D), ((1, 16),), -0.2, 0.2)), 1568.0, 50176.0)
    up_rows = jnp.clip(jnp.exp(math.log(3136.0) - 2.7725887 * jax.random.uniform(key_list[12], (LAYERS, D), jnp.float32) ** block_scale(key_list[12], (LAYERS, D), ((1, 16),), -0.2, 0.2)), 196.0, 3136.0)
    up_cols = jnp.clip(jnp.exp(math.log(3136.0) - 2.7725887 * jax.random.uniform(key_list[13], (LAYERS, FF), jnp.float32) ** block_scale(key_list[13], (LAYERS, FF), ((1, 2),), -0.2, 0.2)), 196.0, 3136.0)
    down_rows = jnp.clip(jnp.exp(math.log(12544.0) - 2.4852256 * jax.random.uniform(key_list[14], (LAYERS, FF), jnp.float32) ** block_scale(key_list[14], (LAYERS, FF), ((1, 2),), -0.2, 0.2)), 1045.0, 12544.0)
    down_cols = jnp.clip(jnp.exp(math.log(12544.0) - 2.4852256 * jax.random.uniform(key_list[15], (LAYERS, D), jnp.float32) ** block_scale(key_list[15], (LAYERS, D), ((1, 16),), -0.2, 0.2)), 1045.0, 12544.0)
    norm_state = jnp.clip(jnp.exp(math.log(25088.0) - 2.7725887 * jax.random.uniform(key_list[16], (LAYERS, 4, D), jnp.float32) ** block_scale(key_list[16], (LAYERS, 4, D), ((2, 16),), -0.2, 0.2)), 1568.0, 25088.0)
    return dict(patches=patches, cotangent=cotangent, patch_counts=patch_counts, qkv_weight=qkv_weight, out_weight=out_weight, up_weight=up_weight, down_weight=down_weight, norms=norms, qkv_rows=qkv_rows, qkv_cols=qkv_cols, out_rows=out_rows, out_cols=out_cols, up_rows=up_rows, up_cols=up_cols, down_rows=down_rows, down_cols=down_cols, norm_state=norm_state)


@jax.custom_vjp
def low(v):
    return lax.optimization_barrier(v.astype(jnp.bfloat16)).astype(jnp.float32)

@jax.custom_vjp
def low_back(v):
    return v

def low_keep(v):
    return (low(v), None)

def low_pass(kept, grad):
    return (grad,)

def back_keep(v):
    return (v, None)

def back_low(kept, grad):
    return (low(grad),)
low.defvjp(low_keep, low_pass)
low_back.defvjp(back_keep, back_low)
DECAY = 0.5
EPS_SQUARE = 1e-30
CLIP = 0.25
RATE = 2.0
MASKED = -1e+30
HIGH = lax.Precision.HIGHEST

def matmul(left, right):
    return jnp.dot(left, right, precision=HIGH, preferred_element_type=jnp.float32)

def layer_norm(rows, gain, shift):
    centre = rows - lax.optimization_barrier(jnp.mean(rows, axis=-1, keepdims=True))
    spread = lax.optimization_barrier(jnp.mean(centre * centre, axis=-1, keepdims=True))
    return centre * lax.rsqrt(spread + 1e-06) * gain + shift

def segments(counts):
    bounds = jnp.cumsum(counts)
    places = jnp.arange(TOK_DEV, dtype=jnp.int32)
    image = lax.optimization_barrier(jnp.sum((places[:, None] >= bounds[None, :]).astype(jnp.int32), axis=1))
    live = (places < bounds[-1]).astype(jnp.float32)
    return (image[:, None] == image[None, :], live)

def attention(qkv, same):
    query, keys, values = (qkv[:, 0], qkv[:, 1], qkv[:, 2])
    scores = jnp.einsum('qhd,khd->hqk', query, keys, precision=HIGH) * HEAD_DIM ** (-0.5)
    scores = low_back(jnp.where(same[None], scores, MASKED))
    top = lax.optimization_barrier(jnp.max(scores, axis=-1, keepdims=True))
    raised = jnp.exp(scores - top)
    probs = low(raised / lax.optimization_barrier(jnp.sum(raised, axis=-1, keepdims=True)))
    mixed = jnp.einsum('hqk,khd->qhd', probs, values, precision=HIGH)
    return mixed.reshape(mixed.shape[0], D)

def two_layers(rows, params, same):
    qkv_weight, out_weight, up_weight, down_weight, norms = params
    for layer in range(LAYERS):
        normed = low(layer_norm(rows, norms[layer, 0], norms[layer, 1]))
        qkv = matmul(normed, low(qkv_weight[layer]).reshape(D, 3 * D))
        qkv = low(low_back(qkv)).reshape(rows.shape[0], 3, HEADS, HEAD_DIM)
        mixed = low(low_back(attention(qkv, same)))
        rows = rows + low_back(matmul(mixed, low(out_weight[layer])))
        normed = low(layer_norm(rows, norms[layer, 2], norms[layer, 3]))
        hidden = low_back(matmul(normed, low(up_weight[layer])))
        active = low(jax.nn.gelu(hidden, approximate=False))
        rows = rows + low_back(matmul(active, low(down_weight[layer])))
    return rows

def factored(weight, grad, row_state, col_state):
    count = weight.shape[0]
    matrix = grad.reshape(count, -1)
    square = matrix * matrix + EPS_SQUARE
    row_new = DECAY * row_state + (1.0 - DECAY) * lax.optimization_barrier(jnp.mean(square, axis=1))
    col_new = DECAY * col_state.reshape(-1) + (1.0 - DECAY) * lax.optimization_barrier(jnp.mean(square, axis=0))
    second = row_new[:, None] * col_new[None, :] / jnp.mean(row_new)
    step = matrix * lax.rsqrt(second)
    size = jnp.sqrt(jnp.mean(step * step))
    step = step / jnp.maximum(1.0, size / CLIP)
    scale = jnp.sqrt(jnp.mean(weight * weight) + 1e-06)
    new = weight - RATE * scale * step.reshape(weight.shape)
    return (new, row_new, col_new.reshape(col_state.shape), size)

def plain(param, grad, state):
    state_new = DECAY * state + (1.0 - DECAY) * (grad * grad + EPS_SQUARE)
    step = grad * lax.rsqrt(state_new)
    size = jnp.sqrt(jnp.mean(step * step))
    step = step / jnp.maximum(1.0, size / CLIP)
    scale = jnp.sqrt(jnp.mean(param * param) + 1e-06)
    return (param - RATE * scale * step, state_new, size)

def reference(patches, cotangent, patch_counts, qkv_weight, out_weight, up_weight, down_weight, norms, qkv_rows, qkv_cols, out_rows, out_cols, up_rows, up_cols, down_rows, down_cols, norm_state):
    params = (qkv_weight, out_weight, up_weight, down_weight, norms)
    blocks = (patches.astype(jnp.float32).reshape(N_DP, TOK_DEV, D), cotangent.astype(jnp.float32).reshape(N_DP, TOK_DEV, D), patch_counts.reshape(N_DP, SLOTS))

    def one_block(totals, block):
        rows, grad, counts = block
        same, live = segments(counts)
        result, back = jax.vjp(lambda values, weights: two_layers(values, weights, same), rows, params)
        d_rows, d_params = back(grad * live[:, None])
        totals = jax.tree.map(lambda left, right: left + right, totals, d_params)
        return (totals, (result.astype(jnp.bfloat16), d_rows))
    grads, (outs, d_rows) = lax.scan(one_block, jax.tree.map(jnp.zeros_like, params), blocks)
    activations = outs.reshape(TOKENS, D)
    input_grad = d_rows.reshape(TOKENS, D)
    row_states = (qkv_rows, out_rows, up_rows, down_rows)
    col_states = (qkv_cols, out_cols, up_cols, down_cols)
    news, row_news, col_news, sizes = ([], [], [], [])
    for which in range(4):
        results = [factored(params[which][layer], grads[which][layer], row_states[which][layer], col_states[which][layer]) for layer in range(LAYERS)]
        news.append(jnp.stack([item[0] for item in results]))
        row_news.append(jnp.stack([item[1] for item in results]))
        col_news.append(jnp.stack([item[2] for item in results]))
        sizes.append(jnp.stack([item[3] for item in results]))
    norm_news, norm_states, norm_sizes = ([], [], [])
    for layer in range(LAYERS):
        results = [plain(norms[layer, kind], grads[4][layer, kind], norm_state[layer, kind]) for kind in range(4)]
        norm_news.append(jnp.stack([item[0] for item in results]))
        norm_states.append(jnp.stack([item[1] for item in results]))
        norm_sizes.append(jnp.stack([item[2] for item in results]))
    update_rms = jnp.concatenate([jnp.stack(sizes, axis=1), jnp.stack(norm_sizes)], axis=1)
    moments = jnp.stack(norm_states)
    return (activations, input_grad, grads[0], grads[1], grads[2], grads[3], grads[4], news[0], news[1], news[2], news[3], jnp.stack(norm_news), news[0].astype(jnp.bfloat16), news[1].astype(jnp.bfloat16), news[2].astype(jnp.bfloat16), news[3].astype(jnp.bfloat16), row_news[0], col_news[0], row_news[1], col_news[1], row_news[2], col_news[2], row_news[3], col_news[3], moments[:, 0:2], moments[:, 2:4], update_rms)
```

```python
import functools

import jax
import jax.numpy as jnp
from jax import lax
from jax.experimental import pallas as pl
from jax.experimental.pallas import tpu as pltpu
from jax.sharding import PartitionSpec as P

D = 768
HEAD_DIM = 64
FF = 3072


DECAY = 0.5
EPS_SQUARE = 1e-30
CLIP = 0.25
RATE = 2.0
MASKED = -1e30


def for_sending(value):
    return jax.tree.map(lambda a: a.astype(jnp.bfloat16) if a.dtype == jnp.float32 else a, value)


def layer_norm(rows, gain, shift):
    centre = rows - jnp.mean(rows, axis=-1, keepdims=True)
    spread = jnp.mean(centre * centre, axis=-1, keepdims=True)
    return centre * lax.rsqrt(spread + 1e-06) * gain + shift


def norm_back(rows, gain, shift, grad):
    result, back = jax.vjp(layer_norm, rows, gain, shift)
    return back(grad)


def exact_gelu(values):
    return jax.nn.gelu(values, approximate=False)


def segments(counts, length):
    bounds = jnp.cumsum(counts)
    places = jnp.arange(length, dtype=jnp.int32)
    image = jnp.sum((places[:, None] >= bounds[None, :]).astype(jnp.int32), axis=1)
    live = (places < bounds[-1]).astype(jnp.float32)
    return (image[:, None] == image[None, :], live)


def attention_scores(query, keys, same):
    scale = query.shape[-1] ** (-0.5)
    scores = jnp.einsum("qhd,khd->hqk", query, keys, preferred_element_type=jnp.float32) * scale
    return jnp.where(same[None], scores, MASKED)


def attend(qkv, same):
    scores = attention_scores(qkv[:, 0], qkv[:, 1], same)
    top = jnp.max(scores, axis=-1, keepdims=True)
    raised = jnp.exp(scores - top)
    total = jnp.sum(raised, axis=-1, keepdims=True)
    probs = (raised / total).astype(jnp.bfloat16)
    mixed = jnp.einsum("hqk,khd->qhd", probs, qkv[:, 2], preferred_element_type=jnp.float32)
    return (mixed.reshape(mixed.shape[0], -1), top + jnp.log(total))


def attend_back(qkv, same, log_total, grad_mixed):
    query, keys, values = (qkv[:, 0], qkv[:, 1], qkv[:, 2])
    scale = query.shape[-1] ** (-0.5)
    probs = jnp.exp(attention_scores(query, keys, same) - log_total)
    d_values = jnp.einsum(
        "hqk,qhd->khd", probs.astype(jnp.bfloat16), grad_mixed, preferred_element_type=jnp.float32
    )
    d_probs = jnp.einsum("qhd,khd->hqk", grad_mixed, values, preferred_element_type=jnp.float32)
    d_scores = (probs * (d_probs - jnp.sum(probs * d_probs, axis=-1, keepdims=True))).astype(
        jnp.bfloat16
    )
    d_query = jnp.einsum("hqk,khd->qhd", d_scores, keys, preferred_element_type=jnp.float32) * scale
    d_keys = jnp.einsum("hqk,qhd->khd", d_scores, query, preferred_element_type=jnp.float32) * scale
    return jnp.stack([d_query, d_keys, d_values], axis=1).astype(jnp.bfloat16)


def spread_rows(values):
    return lax.all_gather(values, "mp", axis=0, tiled=True)


def size_of(name):
    return lax.axis_size("dp") if name == "dp" else lax.axis_size("mp")


TILE = 112
VMEM_BYTES = 64 << 20
GROUP = 768
BIG = 1e30
MESH = pl.DeviceIdType.MESH
F32 = jnp.float32
BF16 = jnp.bfloat16
NN = ((1,), (0,))
NT = ((1,), (1,))


def dot(left, right, dims):
    return lax.dot_general(left, right, (dims, ((), ())), preferred_element_type=F32)


class Place:
    def __init__(self, n_dp):
        self.nz = n_dp // 4
        me = lax.axis_index("dp")
        self.core = lax.axis_index("mp")
        self.z, self.y, self.x = me // 4, (me // 2) % 2, me % 2

    def at(self, z, y, x, core):
        return (z * 4 + y * 2 + x, core)

    def over_x(self):
        return self.at(self.z, self.y, 1 - self.x, self.core)

    def over_y(self):
        return self.at(self.z, 1 - self.y, self.x, self.core)

    def over_z(self, step):
        return self.at((self.z + step) % self.nz, self.y, self.x, self.core)

    def over_core(self):
        return self.at(self.z, self.y, self.x, 1 - self.core)

    def barrier(self):
        sem = pltpu.get_barrier_semaphore()
        others = [self.over_core(), self.over_x(), self.over_y()]
        others += [self.over_z(step) for step in range(1, self.nz)]
        for other in others:
            pl.semaphore_signal(sem, inc=1, device_id=other, device_id_type=MESH)
        pl.semaphore_wait(sem, len(others))


class Sender:
    def __init__(self, send_sems, recv_sems):
        self.send_sems, self.recv_sems = send_sems, recv_sems
        self.count = 0
        self.sent = []

    def start(self, src, dst, device):
        copy = pltpu.make_async_remote_copy(
            src_ref=src,
            dst_ref=dst,
            send_sem=self.send_sems.at[self.count],
            recv_sem=self.recv_sems.at[self.count],
            device_id=device,
            device_id_type=MESH,
        )
        self.count += 1
        copy.start()
        self.sent.append(copy)
        return copy

    def drain(self):
        for copy in self.sent:
            copy.wait_send()
        self.sent = []


class Gather:
    def __init__(self, place, sender, weights, groups):
        self.p, self.sender, self.weights, self.groups = place, sender, weights, groups
        self.first, self.second, self.third = {}, {}, {}
        self.tick_at = 0

    def cut(self, k):
        layer, low = self.groups[k]
        return self.weights[layer], low, low + GROUP // 2, low + GROUP

    def s1(self, k):
        if k >= len(self.groups):
            return
        w, low, mid, high = self.cut(k)
        p = self.p
        own = w.at[p.z, p.y, p.x, :, low:high]
        self.first[k] = [
            self.sender.start(own, own, p.over_z(step)) for step in range(1, p.nz)
        ]

    def s2(self, k):
        if k >= len(self.groups):
            return
        w, low, mid, high = self.cut(k)
        p = self.p
        for copy in self.first[k]:
            copy.wait_recv()
        a, b = w.at[:, p.y, p.x, :, low:mid], w.at[:, p.y, p.x, :, mid:high]
        self.second[k] = [
            self.sender.start(a, a, p.over_y()),
            self.sender.start(b, b, p.over_x()),
        ]

    def s3(self, k):
        if k < 0 or k >= len(self.groups):
            return
        w, low, mid, high = self.cut(k)
        p = self.p
        for copy in self.second[k]:
            copy.wait_recv()
        a, b = w.at[:, :, p.x, :, low:mid], w.at[:, p.y, :, :, mid:high]
        self.third[k] = [
            self.sender.start(a, a, p.over_x()),
            self.sender.start(b, b, p.over_y()),
        ]

    def tick(self):
        k = self.tick_at
        if k > len(self.groups):
            return
        self.s2(k)
        self.s1(k + 3)
        self.s3(k - 1)
        self.tick_at += 1

    def ready(self, k):
        while self.tick_at < k + 2:
            self.tick()
        for copy in self.third.pop(k, ()):
            copy.wait_recv()


class Scatter:
    def __init__(self, place, sender, grads, groups, r1a, r1b, r2a, r2b, r3, result):
        self.p, self.sender, self.grads, self.groups = place, sender, grads, groups
        self.r1a, self.r1b, self.r2a, self.r2b, self.r3 = r1a, r1b, r2a, r2b, r3
        self.result = result
        self.first, self.second, self.third = {}, {}, {}
        self.started = 0
        self.tick_at = 0

    def cut(self, k):
        layer, low = self.groups[k]
        return self.grads[layer], low, low + GROUP // 2, low + GROUP

    def s1(self):
        k = self.started
        self.started += 1
        g, low, mid, high = self.cut(k)
        p = self.p
        self.first[k] = [
            self.sender.start(g.at[:, :, 1 - p.x, :, low:mid], self.r1a.at[k % self.r1a.shape[0]], p.over_x()),
            self.sender.start(g.at[:, 1 - p.y, :, :, mid:high], self.r1b.at[k % self.r1b.shape[0]], p.over_y()),
        ]

    def s2(self, k):
        g, low, mid, high = self.cut(k)
        p = self.p
        for copy in self.first[k]:
            copy.wait_recv()
        a, b = g.at[:, :, p.x, :, low:mid], g.at[:, p.y, :, :, mid:high]
        for z in range(p.nz):
            a[z] = (a[z].astype(F32) + self.r1a[k % self.r1a.shape[0], z].astype(F32)).astype(BF16)
            b[z] = (b[z].astype(F32) + self.r1b[k % self.r1b.shape[0], z].astype(F32)).astype(BF16)
        self.second[k] = [
            self.sender.start(g.at[:, 1 - p.y, p.x, :, low:mid], self.r2a.at[k % 4], p.over_y()),
            self.sender.start(g.at[:, p.y, 1 - p.x, :, mid:high], self.r2b.at[k % 4], p.over_x()),
        ]

    def s3(self, k):
        g, low, mid, high = self.cut(k)
        p = self.p
        for copy in self.second[k]:
            copy.wait_recv()
        a, b = g.at[:, p.y, p.x, :, low:mid], g.at[:, p.y, p.x, :, mid:high]
        a[...] = (a[...].astype(F32) + self.r2a[k % 4].astype(F32)).astype(BF16)
        b[...] = (b[...].astype(F32) + self.r2b[k % 4].astype(F32)).astype(BF16)
        self.third[k] = [
            self.sender.start(
                g.at[(p.z + step) % p.nz, p.y, p.x, :, low:high],
                self.r3.at[k % 4, step - 1],
                p.over_z(step),
            )
            for step in range(1, p.nz)
        ]

    def finish(self, k):
        layer, low = self.groups[k]
        g, low, mid, high = self.cut(k)
        p = self.p
        for copy in self.third[k]:
            copy.wait_recv()
        total = g[p.z, p.y, p.x, :, low:high].astype(F32)
        for step in range(1, p.nz):
            total = total + self.r3[k % 4, step - 1].astype(F32)
        self.result[layer, :, low:high] = total

    def tick(self):
        k = self.tick_at
        if k >= self.started + 2:
            return
        if k < self.started:
            self.s2(k)
        if 0 <= k - 1 < self.started:
            self.s3(k - 1)
        if 0 <= k - 2 < self.started:
            self.finish(k - 2)
        self.tick_at += 1


def row_tiles(length, body):
    def step(i, carry):
        body(pl.ds(pl.multiple_of(i * TILE, TILE), TILE))
        return carry

    lax.fori_loop(0, length // TILE, step, 0)


def normalised(rows):
    centre = rows - jnp.mean(rows, axis=-1, keepdims=True)
    spread = jnp.mean(centre * centre, axis=-1, keepdims=True)
    rise = lax.rsqrt(spread + 1e-06)
    return centre * rise, rise


def encode_segments(counts, slots, qe, ke):
    length = qe.shape[0]
    place = lax.broadcasted_iota(jnp.int32, (length, 128), 0)
    lane = lax.broadcasted_iota(jnp.int32, (length, 128), 1) % HEAD_DIM
    image = jnp.zeros((length, 128), jnp.int32)
    total = jnp.int32(0)
    for slot in range(slots):
        total = total + counts[slot]
        image = image + (place >= total).astype(jnp.int32)
    hit = image == lane
    ke[...] = jnp.where(hit, 1.0, 0.0).astype(BF16)
    qe[...] = jnp.where(jnp.logical_or(hit, lane > slots), 0.0, -BIG).astype(BF16)


def attention_forward(qkv, qe, ke, log_total, mixed, between=None):
    length, width = mixed.shape
    lane = lax.broadcasted_iota(jnp.int32, (length, 128), 1)

    def pair(at, carry):
        low = pl.multiple_of(at * 128, 128)
        query = qkv[:, pl.ds(low, 128)] * jnp.asarray(0.125, BF16)
        keys = qkv[:, pl.ds(width + low, 128)]
        values = qkv[:, pl.ds(2 * width + low, 128)].T
        outs = []
        for half in range(2):
            own = (lane < HEAD_DIM) if half == 0 else (lane >= HEAD_DIM)
            q = jnp.where(own, query, qe[...])
            k = jnp.where(own, keys, ke[...])
            scores = dot(k, q, NT)
            top = jnp.max(scores, axis=0, keepdims=True)
            raised = jnp.exp(scores - top)
            total = jnp.sum(raised, axis=0, keepdims=True)
            rows = slice(half * HEAD_DIM, (half + 1) * HEAD_DIM)
            outs.append(dot(values[rows], raised.astype(BF16), NN) / total)
            log_total[pl.ds(at * 2 + half, 1), :] = top + jnp.log(total)
        mixed[:, pl.ds(low, 128)] = jnp.concatenate(outs, axis=0).T.astype(BF16)
        return carry

    lax.fori_loop(0, width // 128, pair, 0)


def attention_backward(qkv, qe, ke, log_total, d_mixed):
    length, width = d_mixed.shape
    lane = lax.broadcasted_iota(jnp.int32, (length, 128), 1)

    def pair(at, carry):
        low = pl.multiple_of(at * 128, 128)
        query = qkv[:, pl.ds(low, 128)] * jnp.asarray(0.125, BF16)
        keys = qkv[:, pl.ds(width + low, 128)]
        values = qkv[:, pl.ds(2 * width + low, 128)]
        d_out = d_mixed[:, pl.ds(low, 128)]
        keys_t = keys.T
        d_query, d_keys, d_values = [], [], []
        for half in range(2):
            own = (lane < HEAD_DIM) if half == 0 else (lane >= HEAD_DIM)
            q = jnp.where(own, query, qe[...])
            k = jnp.where(own, keys, ke[...])
            v = jnp.where(own, values, jnp.zeros_like(values))
            probs = jnp.exp(dot(k, q, NT) - log_total[pl.ds(at * 2 + half, 1), :])
            d_probs = dot(v, d_out, NT)
            mean = jnp.sum(probs * d_probs, axis=0, keepdims=True)
            d_scores = (probs * (d_probs - mean)).astype(BF16)
            d_values.append(dot(probs.astype(BF16), d_out, NN))
            d_keys.append(dot(d_scores, query, NN))
            rows = slice(half * HEAD_DIM, (half + 1) * HEAD_DIM)
            d_query.append(dot(keys_t[rows], d_scores, NN))
        first = lane < HEAD_DIM
        d_q = jnp.concatenate(d_query, axis=0).T * 0.125
        qkv[:, pl.ds(low, 128)] = d_q.astype(BF16)
        qkv[:, pl.ds(width + low, 128)] = jnp.where(first, *d_keys).astype(BF16)
        qkv[:, pl.ds(2 * width + low, 128)] = jnp.where(first, *d_values).astype(BF16)
        return carry

    lax.fori_loop(0, width // 128, pair, 0)


class Exchange:
    def __init__(self, place, sender, out, into):
        self.p, self.sender, self.out, self.into = place, sender, out, into
        self.turn = 0
        self.copies = {}
        length = out.shape[1]
        cut = (length // TILE + 1) // 2 * TILE
        self.chunks = ((0, cut), (cut, length))

    def send(self, compute):
        slot = self.turn % 2
        for copy in self.copies.get(slot, ()):
            copy.wait_send()
            self.sender.sent = [item for item in self.sender.sent if item is not copy]
        self.copies[slot] = []
        for low, high in self.chunks:
            self.out[slot, low:high, :] = compute(low, high).astype(BF16)
            piece = self.out.at[slot, low:high, :]
            self.copies[slot].append(
                self.sender.start(piece, self.into.at[slot, low:high, :], self.p.over_core())
            )

    def take(self, body):
        slot = self.turn % 2
        self.turn += 1
        for (low, high), copy in zip(self.chunks, self.copies[slot]):
            copy.wait_recv()

            def step(i, carry, low=low):
                rows = pl.ds(pl.multiple_of(low + i * TILE, TILE), TILE)
                total = self.out[slot, rows, :].astype(F32) + self.into[slot, rows, :].astype(F32)
                body(rows, total)
                return carry

            lax.fori_loop(0, (high - low) // TILE, step, 0)


def flat(w, low, high):
    value = w[:, :, :, :, low:high]
    return value.reshape(-1, high - low)


def gelu_and_slope(hidden):
    cdf = 0.5 * (1.0 + lax.erf(hidden * (0.5**0.5)))
    slope = cdf + hidden * (jnp.exp(-0.5 * hidden * hidden) * 0.3989422804014327)
    return hidden * cdf, slope


def forward_kernel(
    n_dp, cuts, slots,
    counts, patches, pieces, norms,
    o_weights, o_rows, o_middle, o_normed_a, o_qkv, o_mixed, o_normed_b, o_active, o_slope, o_log,
    o_result,
    w0, w1, rows, middle, normed_a, qkv, mixed, normed_b, active, slope, log_total, final,
    x_out, x_in, qe, ke, send_sems, recv_sems, local_sems,
):
    layers, half = 2, patches.shape[0]
    length = 2 * half
    c_qkv, c_out, c_up, c_down = cuts
    p = Place(n_dp)
    sender = Sender(send_sems, recv_sems)
    local = []

    def move(src, dst):
        copy = pltpu.make_async_copy(src, dst, local_sems.at[len(local)])
        copy.start()
        local.append(copy)
        return copy

    weights = (w0, w1)
    loads = [move(pieces.at[l], weights[l].at[p.z, p.y, p.x]) for l in range(layers)]
    p.barrier()
    groups = [(l, low) for l in range(layers) for low in range(0, c_down[1], GROUP)]
    per = len(groups) // layers
    gather = Gather(p, sender, weights, groups)
    loads[0].wait()
    gather.s1(0)
    gather.s1(1)
    own_rows = pl.ds(pl.multiple_of(p.core * half, half), half)
    rows[0, own_rows, :] = patches[...].astype(F32)
    swap = sender.start(rows.at[0, own_rows, :], rows.at[0, own_rows, :], p.over_core())
    loads[1].wait()
    gather.s1(2)
    encode_segments(counts, slots, qe, ke)
    swap.wait_recv()
    exchange = Exchange(p, sender, x_out, x_in)

    def norm_into(target, layer, which, at, value):
        hat, _ = normalised(value)
        gain, shift = norms[layer, which : which + 1, :], norms[layer, which + 1 : which + 2, :]
        target[layer, at, :] = (hat * gain + shift).astype(BF16)

    row_tiles(length, lambda at: norm_into(normed_a, 0, 0, at, rows[0, at, :]))
    saves = [(rows, o_rows, 0), (normed_a, o_normed_a, 0)]

    def save(*items):
        for src, dst, layer in items:
            move(src.at[layer], dst.at[layer])

    save(*saves)
    for layer in range(layers):
        w, base = weights[layer], per * layer
        qkv_end = c_qkv[1]
        for k in range(-(-qkv_end // GROUP)):
            gather.ready(base + k)
            low, high = k * GROUP, min(qkv_end, (k + 1) * GROUP)
            qkv[layer, :, low:high] = dot(normed_a[layer], flat(w, low, high), NN).astype(BF16)
        gather.tick()
        attention_forward(qkv.at[layer], qe, ke, log_total.at[layer], mixed.at[layer])
        save((qkv, o_qkv, layer), (log_total, o_log, layer), (mixed, o_mixed, layer))
        gather.ready(base + (c_out[1] - 1) // GROUP)
        w_out = flat(w, *c_out)
        exchange.send(lambda low, high: dot(mixed[layer, low:high, :], w_out, NT))
        gather.tick()

        def mid_step(at, total):
            value = rows[layer, at, :] + total
            middle[layer, at, :] = value
            norm_into(normed_b, layer, 2, at, value)

        exchange.take(mid_step)
        save((middle, o_middle, layer), (normed_b, o_normed_b, layer))
        for k in range(c_up[0] // GROUP, c_up[1] // GROUP):
            gather.ready(base + k)
            low = k * GROUP - c_up[0]
            for at in range(0, GROUP, GROUP // 2):
                cols = slice(low + at, low + at + GROUP // 2)
                first = k * GROUP + at
                hidden = dot(normed_b[layer], flat(w, first, first + GROUP // 2), NN)
                act, rise = gelu_and_slope(hidden)
                active[layer, :, cols] = act.astype(BF16)
                slope[layer, :, cols] = rise.astype(BF16)
        save((active, o_active, layer), (slope, o_slope, layer))
        gather.tick()
        for k in range(c_down[0] // GROUP, c_down[1] // GROUP):
            gather.ready(base + k)
        if True:
            w_down = flat(w, *c_down)
            exchange.send(lambda low, high: dot(active[layer, low:high, :], w_down, NT))
        move(w, o_weights.at[layer])
        gather.tick()
        if layer + 1 < layers:

            def next_step(at, total):
                value = middle[layer, at, :] + total
                rows[layer + 1, at, :] = value
                norm_into(normed_a, layer + 1, 0, at, value)

            exchange.take(next_step)
            save((rows, o_rows, layer + 1), (normed_a, o_normed_a, layer + 1))
        else:

            def last_step(at, total):
                final[at, :] = middle[layer, at, :] + total

            exchange.take(last_step)
    o_result[...] = final[own_rows, :].astype(BF16)
    sender.drain()
    for copy in local[layers:]:
        copy.wait()


def backward_kernel(
    n_dp, cuts, slots,
    counts, cotangent, norms,
    i_weights, i_rows, i_middle, i_normed_a, i_qkv, i_mixed, i_normed_b, i_active, i_slope, i_log,
    o_input, o_pieces, o_norms,
    g0, g1, r1a, r1b, r2a, r2b, r3,
    w, kept, normed_a, qkv, mixed, normed_b, active, slope, log_total,
    grad, rounded, turned, x_out, x_in, qe, ke, send_sems, recv_sems, local_sems,
):
    layers, half = 2, cotangent.shape[0]
    length = 2 * half
    c_qkv, c_out, c_up, c_down = cuts
    p = Place(n_dp)
    sender = Sender(send_sems, recv_sems)
    count = [0]

    def load(src, dst):
        copy = pltpu.make_async_copy(src, dst, local_sems.at[count[0]])
        count[0] += 1
        copy.start()
        return copy

    def load_mlp(l):
        cols = slice(c_up[0], c_down[1])
        return dict(
            active=load(i_active.at[l], active),
            slope=load(i_slope.at[l], slope),
            weights=load(i_weights.at[l, :, :, :, :, cols], w.at[:, :, :, :, cols]),
            normed_b=load(i_normed_b.at[l], normed_b),
            middle=load(i_middle.at[l], kept),
        )

    def load_attention(l):
        cols = slice(c_qkv[0], c_out[1])
        return dict(
            mixed=load(i_mixed.at[l], mixed),
            weights=load(i_weights.at[l, :, :, :, :, cols], w.at[:, :, :, :, cols]),
            qkv=load(i_qkv.at[l], qkv),
            log=load(i_log.at[l], log_total),
            normed_a=load(i_normed_a.at[l], normed_a),
        )

    mlp = load_mlp(layers - 1)
    att = load_attention(layers - 1)
    p.barrier()
    own_rows = pl.ds(pl.multiple_of(p.core * half, half), half)
    total = jnp.int32(0)
    for slot in range(slots):
        total = total + counts[slot]
    place = lax.broadcasted_iota(jnp.int32, (half, 1), 0) + p.core * half
    grad[own_rows, :] = jnp.where(place < total, cotangent[...].astype(F32), 0.0)
    swap = sender.start(grad.at[own_rows, :], grad.at[own_rows, :], p.over_core())
    encode_segments(counts, slots, qe, ke)
    o_norms[...] = jnp.zeros_like(o_norms)
    exchange = Exchange(p, sender, x_out, x_in)
    grads = (g0, g1)
    per = c_down[1] // GROUP
    order = [k for k in range(c_down[0] // GROUP, per)]
    order += [k for k in range(c_up[0] // GROUP, c_up[1] // GROUP)]
    order += [k for k in reversed(range(0, c_up[0] // GROUP))]
    groups = [(l, k * GROUP) for l in reversed(range(layers)) for k in order]
    scatter = Scatter(p, sender, grads, groups, r1a, r1b, r2a, r2b, r3, o_pieces)
    swap.wait_recv()
    sender.drain()

    def store(layer, low, value):
        g = grads[layer]
        shape = g.shape[:4] + (value.shape[1],)
        g[:, :, :, :, low : low + value.shape[1]] = value.astype(BF16).reshape(shape)

    def norm_step(layer, which, at, total):
        hat, rise = normalised(kept[at, :])
        o_norms[layer, which : which + 1, :] += jnp.sum(total * hat, axis=0, keepdims=True)
        o_norms[layer, which + 1 : which + 2, :] += jnp.sum(total, axis=0, keepdims=True)
        d_hat = total * norms[layer, which : which + 1, :]
        flat_mean = jnp.mean(d_hat, axis=-1, keepdims=True)
        hat_mean = jnp.mean(d_hat * hat, axis=-1, keepdims=True)
        value = grad[at, :] + rise * (d_hat - flat_mean - hat * hat_mean)
        grad[at, :] = value
        rounded[at, :] = value.astype(BF16)

    def round_step(at):
        rounded[at, :] = grad[at, :].astype(BF16)

    row_tiles(length, round_step)
    for layer in reversed(range(layers)):
        turned[...] = rounded[...].T
        mlp["active"].wait()
        for k in range(c_down[0] // GROUP, c_down[1] // GROUP):
            low = k * GROUP - c_down[0]
            store(layer, k * GROUP, dot(turned[...], active[:, low : low + GROUP], NN))
            scatter.s1()
        mlp["weights"].wait()
        mlp["slope"].wait()
        step = GROUP // 2
        for at in range(0, c_down[1] - c_down[0], step):
            cols = slice(at, at + step)
            first = c_down[0] + at
            d_active = dot(rounded[...], flat(w, first, first + step), NN)
            slope[:, cols] = (d_active * slope[:, cols].astype(F32)).astype(BF16)
        scatter.tick()
        mlp["normed_b"].wait()
        turned[...] = normed_b[...].T
        for k in range(c_up[0] // GROUP, c_up[1] // GROUP):
            low = k * GROUP - c_up[0]
            store(layer, k * GROUP, dot(turned[...], slope[:, low : low + GROUP], NN))
            scatter.s1()
        w_up = flat(w, *c_up)
        exchange.send(lambda low, high: dot(slope[low:high, :], w_up, NT))
        scatter.tick()
        mlp["middle"].wait()
        exchange.take(lambda at, total: norm_step(layer, 2, at, total))
        rows_load = load(i_rows.at[layer], kept)
        if layer:
            mlp = load_mlp_next(load, layer - 1, i_active, i_slope, i_weights, i_normed_b,
                                active, slope, w, normed_b, slice(c_up[0], c_down[1]))
        turned[...] = rounded[...].T
        att["mixed"].wait()
        store(layer, c_out[0], dot(turned[...], mixed[...], NN))
        att["weights"].wait()
        mixed[...] = dot(rounded[...], flat(w, *c_out), NN).astype(BF16)
        scatter.tick()
        att["qkv"].wait()
        att["log"].wait()
        attention_backward(qkv, qe, ke, log_total, mixed)
        att["normed_a"].wait()
        turned[...] = normed_a[...].T
        for k in reversed(range(0, c_out[1] // GROUP)):
            low, high = k * GROUP, min(c_qkv[1], (k + 1) * GROUP)
            store(layer, low, dot(turned[...], qkv[:, low:high], NN))
            scatter.s1()
        w_qkv = flat(w, *c_qkv)
        exchange.send(lambda low, high: dot(qkv[low:high, :], w_qkv, NT))
        scatter.tick()
        rows_load.wait()
        exchange.take(lambda at, total: norm_step(layer, 0, at, total))
        if layer:
            mlp["middle"] = load(i_middle.at[layer - 1], kept)
            att = load_attention(layer - 1)
        scatter.tick()
    o_input[...] = grad[own_rows, :]
    while scatter.tick_at < len(groups) + 2:
        scatter.tick()
    sender.drain()


def load_mlp_next(load, l, i_active, i_slope, i_weights, i_normed_b, active, slope, w, normed_b, cols):
    return dict(
        active=load(i_active.at[l], active),
        slope=load(i_slope.at[l], slope),
        weights=load(i_weights.at[l, :, :, :, :, cols], w.at[:, :, :, :, cols]),
        normed_b=load(i_normed_b.at[l], normed_b),
    )


def passes_by_xla(
    patches,
    cotangent,
    patch_counts,
    qkv_weight,
    out_weight,
    up_weight,
    down_weight,
    norms,
):
    layers = qkv_weight.shape[0]
    half = patches.shape[0]
    length = half * lax.axis_size("mp")
    same, live_all = segments(patch_counts, length)
    live = lax.dynamic_slice_in_dim(live_all, lax.axis_index("mp") * half, half)
    rows = patches.astype(jnp.float32)
    kept = []
    for layer in range(layers):
        pieces = (
            qkv_weight[layer].astype(jnp.bfloat16),
            out_weight[layer].astype(jnp.bfloat16),
            up_weight[layer].astype(jnp.bfloat16),
            down_weight[layer].astype(jnp.bfloat16),
        )
        whole = (
            lax.all_gather(pieces[0], "dp", axis=0, tiled=True),
            lax.all_gather(pieces[1], "dp", axis=1, tiled=True),
            lax.all_gather(pieces[2], "dp", axis=0, tiled=True),
            lax.all_gather(pieces[3], "dp", axis=1, tiled=True),
        )
        w_qkv, w_out, w_up, w_down = whole
        local = w_qkv.shape[2]
        normed_a = spread_rows(
            layer_norm(rows, norms[layer, 0], norms[layer, 1]).astype(jnp.bfloat16)
        )
        qkv = jnp.dot(normed_a, w_qkv.reshape(D, 3 * local), preferred_element_type=jnp.float32)
        qkv = qkv.astype(jnp.bfloat16).reshape(length, 3, local // HEAD_DIM, HEAD_DIM)
        mixed, log_total = attend(qkv, same)
        mixed = mixed.astype(jnp.bfloat16)
        middle = rows + lax.psum_scatter(
            jnp.dot(mixed, w_out, preferred_element_type=jnp.float32).astype(jnp.bfloat16),
            "mp",
            scatter_dimension=0,
            tiled=True,
        ).astype(jnp.float32)
        normed_b = spread_rows(
            layer_norm(middle, norms[layer, 2], norms[layer, 3]).astype(jnp.bfloat16)
        )
        hidden = jnp.dot(normed_b, w_up, preferred_element_type=jnp.float32)
        active = exact_gelu(hidden).astype(jnp.bfloat16)
        after = middle + lax.psum_scatter(
            jnp.dot(active, w_down, preferred_element_type=jnp.float32).astype(jnp.bfloat16),
            "mp",
            scatter_dimension=0,
            tiled=True,
        ).astype(jnp.float32)
        stored = None
        kept.append(
            (
                rows,
                normed_a,
                qkv,
                log_total,
                mixed,
                middle,
                normed_b,
                hidden,
                active,
                stored,
                pieces,
            )
        )
        rows = after
    activations = rows.astype(jnp.bfloat16)
    grad = cotangent.astype(jnp.float32) * live[:, None]
    reduced = [None] * layers
    for layer in reversed(range(layers)):
        (
            rows_in,
            normed_a,
            qkv,
            log_total,
            mixed,
            middle,
            normed_b,
            hidden,
            active,
            stored,
            pieces,
        ) = kept[layer]
        whole = (
            lax.all_gather(pieces[0], "dp", axis=0, tiled=True),
            lax.all_gather(pieces[1], "dp", axis=1, tiled=True),
            lax.all_gather(pieces[2], "dp", axis=0, tiled=True),
            lax.all_gather(pieces[3], "dp", axis=1, tiled=True),
        )
        w_qkv, w_out, w_up, w_down = whole
        local = w_qkv.shape[2]
        grad_down = spread_rows(grad.astype(jnp.bfloat16))
        g_down = jnp.einsum("tf,td->fd", active, grad_down, preferred_element_type=jnp.float32)
        d_active = jnp.einsum("td,fd->tf", grad_down, w_down, preferred_element_type=jnp.float32)
        gelu_value, gelu_back = jax.vjp(exact_gelu, hidden)
        d_hidden = gelu_back(d_active)[0].astype(jnp.bfloat16)
        g_up = jnp.einsum("td,tf->df", normed_b, d_hidden, preferred_element_type=jnp.float32)
        d_normed_b = lax.psum_scatter(
            jnp.einsum("tf,df->td", d_hidden, w_up, preferred_element_type=jnp.float32).astype(
                jnp.bfloat16
            ),
            "mp",
            scatter_dimension=0,
            tiled=True,
        ).astype(jnp.float32)
        d_middle, g_gain_b, g_shift_b = norm_back(
            middle, norms[layer, 2], norms[layer, 3], d_normed_b
        )
        grad_mid = grad + d_middle
        grad_out = spread_rows(grad_mid.astype(jnp.bfloat16))
        g_out = jnp.einsum("tc,td->cd", mixed, grad_out, preferred_element_type=jnp.float32)
        d_mixed = jnp.einsum(
            "td,cd->tc", grad_out, w_out, preferred_element_type=jnp.float32
        ).astype(jnp.bfloat16)
        d_qkv = attend_back(
            qkv, same, log_total, d_mixed.reshape(length, local // HEAD_DIM, HEAD_DIM)
        )
        d_qkv = d_qkv.reshape(length, 3 * local)
        g_qkv = jnp.einsum(
            "td,tc->dc", normed_a, d_qkv, preferred_element_type=jnp.float32
        ).reshape(D, 3, local)
        d_normed_a = lax.psum_scatter(
            jnp.einsum(
                "tc,dc->td", d_qkv, w_qkv.reshape(D, 3 * local), preferred_element_type=jnp.float32
            ).astype(jnp.bfloat16),
            "mp",
            scatter_dimension=0,
            tiled=True,
        ).astype(jnp.float32)
        d_input, g_gain_a, g_shift_a = norm_back(
            rows_in, norms[layer, 0], norms[layer, 1], d_normed_a
        )
        grad = grad_mid + d_input
        norm_terms = jnp.stack([g_gain_a, g_shift_a, g_gain_b, g_shift_b])
        reduced[layer] = (
            lax.psum_scatter(g_qkv, "dp", scatter_dimension=0, tiled=True),
            lax.psum_scatter(g_out, "dp", scatter_dimension=1, tiled=True),
            lax.psum_scatter(g_up, "dp", scatter_dimension=0, tiled=True),
            lax.psum_scatter(g_down, "dp", scatter_dimension=1, tiled=True),
            lax.psum(norm_terms, "mp"),
        )
    return activations, grad, [item[:4] for item in reduced], jnp.stack([item[4] for item in reduced])


def passes_by_kernels(
    patches,
    cotangent,
    patch_counts,
    qkv_weight,
    out_weight,
    up_weight,
    down_weight,
    norms,
):
    layers, depth, _, local = qkv_weight.shape
    n_dp = lax.axis_size("dp")
    nz, half, wide = n_dp // 4, patches.shape[0], up_weight.shape[2]
    length, slots = 2 * half, patch_counts.shape[0]
    ends = [0, 3 * local, 4 * local, 4 * local + wide, 4 * local + 2 * wide]
    cuts = tuple(zip(ends[:-1], ends[1:]))
    columns, n_groups = ends[-1], layers * ends[-1] // GROUP
    pieces = jnp.concatenate(
        [
            qkv_weight.reshape(layers, depth, 3 * local),
            out_weight.transpose(0, 2, 1),
            up_weight,
            down_weight.transpose(0, 2, 1),
        ],
        axis=2,
    ).astype(BF16)
    vmem, smem, hbm = [
        pl.BlockSpec(memory_space=space) for space in (pltpu.VMEM, pltpu.SMEM, pl.ANY)
    ]
    shape = jax.ShapeDtypeStruct
    whole = (nz, 2, 2, depth, columns)
    rows_f32, rows_bf16 = ((length, D), F32), ((length, D), BF16)
    kept = [
        rows_f32,
        rows_f32,
        rows_bf16,
        ((length, 3 * local), BF16),
        ((length, local), BF16),
        rows_bf16,
        ((length, wide), BF16),
        ((length, wide), BF16),
        ((8, length), F32),
    ]
    saved = [shape((layers,) + dims, kind) for dims, kind in kept]
    sems = [
        pltpu.SemaphoreType.DMA((96,)),
        pltpu.SemaphoreType.DMA((96,)),
        pltpu.SemaphoreType.DMA((32,)),
    ]
    codes = [pltpu.VMEM((length, 128), BF16)] * 2
    swaps = [pltpu.VMEM((2, length, D), BF16)] * 2
    outs = pl.pallas_call(
        functools.partial(forward_kernel, n_dp, cuts, slots),
        out_shape=[shape((layers,) + whole, BF16)] + saved + [shape((half, D), BF16)],
        in_specs=[smem, vmem, hbm, vmem],
        out_specs=[hbm] * (1 + len(saved)) + [vmem],
        scratch_shapes=[pltpu.VMEM(whole, BF16)] * layers
        + [pltpu.VMEM((layers,) + dims, kind) for dims, kind in kept]
        + [pltpu.VMEM((length, D), F32)]
        + swaps
        + codes
        + sems,
        compiler_params=pltpu.CompilerParams(
            collective_id=0, has_side_effects=True, vmem_limit_bytes=VMEM_BYTES
        ),
        name="forward",
    )(patch_counts, patches, pieces, norms)
    saved, activations = outs[:-1], outs[-1]
    own = (nz, 2, depth, GROUP // 2)
    grad, sums, norm_terms = pl.pallas_call(
        functools.partial(backward_kernel, n_dp, cuts, slots),
        out_shape=[
            shape((half, D), F32),
            shape((layers, depth, columns), F32),
            shape((layers, 4, D), F32),
        ],
        in_specs=[smem, vmem, vmem] + [hbm] * len(saved),
        out_specs=[vmem, vmem, vmem],
        scratch_shapes=[pltpu.VMEM(whole, BF16)] * layers
        + [pltpu.VMEM((n_groups // 2,) + own, BF16)] * 2
        + [pltpu.VMEM((4, nz, depth, GROUP // 2), BF16)] * 2
        + [pltpu.VMEM((4, nz - 1, depth, GROUP), BF16)]
        + [pltpu.VMEM(whole, BF16)]
        + [pltpu.VMEM(dims, kind) for dims, kind in kept[1:]]
        + [
            pltpu.VMEM((length, D), F32),
            pltpu.VMEM((length, D), BF16),
            pltpu.VMEM((D, length), BF16),
        ]
        + swaps
        + codes
        + sems,
        compiler_params=pltpu.CompilerParams(
            collective_id=1, has_side_effects=True, vmem_limit_bytes=VMEM_BYTES
        ),
        name="backward",
    )(patch_counts, cotangent, norms, *saved)
    reduced = []
    for layer in range(layers):
        parts = [sums[layer, :, low:high] for low, high in cuts]
        reduced.append(
            (parts[0].reshape(depth, 3, local), parts[1].T, parts[2], parts[3].T)
        )
    return activations, grad, reduced, norm_terms


def kernels_fit(patches, qkv_weight):
    length = 2 * patches.shape[0]
    depth, local = qkv_weight.shape[1], qkv_weight.shape[3]
    return (
        lax.axis_size("mp") == 2
        and lax.axis_size("dp") % 4 == 0
        and depth % 16 == 0
        and length % TILE == 0
        and (4 * local) % GROUP == 0
    )


def per_device(
    patches,
    cotangent,
    patch_counts,
    qkv_weight,
    out_weight,
    up_weight,
    down_weight,
    norms,
    qkv_rows,
    qkv_cols,
    out_rows,
    out_cols,
    up_rows,
    up_cols,
    down_rows,
    down_cols,
    norm_state,
):
    layers = qkv_weight.shape[0]
    passes = passes_by_kernels if kernels_fit(patches, qkv_weight) else passes_by_xla
    activations, grad, reduced, norm_terms = passes(
        patches, cotangent, patch_counts, qkv_weight, out_weight, up_weight, down_weight, norms
    )
    col_axes = ("mp", "dp", "mp", "dp")
    row_counts = (D, D, D, FF)
    col_counts = (3 * D, D, FF, D)
    masters = (qkv_weight, out_weight, up_weight, down_weight)
    row_states = (qkv_rows, out_rows, up_rows, down_rows)
    col_states = (qkv_cols, out_cols, up_cols, down_cols)
    entries = [(layer, which) for layer in range(layers) for which in range(4)]
    grads = [reduced[layer][which] for layer, which in entries]
    row_olds = [row_states[which][layer] for layer, which in entries]
    col_olds = [col_states[which][layer] for layer, which in entries]
    width = norm_state.shape[2]
    row_parts, col_parts = ([], [])
    for position, (layer, which) in enumerate(entries):
        matrix = grads[position].reshape(grads[position].shape[0], -1)
        square = matrix * matrix + EPS_SQUARE
        row_parts.append(jnp.sum(square, axis=1))
        col_parts.append(jnp.sum(square, axis=0).reshape(col_olds[position].shape))
    model_side = tuple(
        [
            row_parts[position] if col_axes[which] == "mp" else col_parts[position]
            for position, (layer, which) in enumerate(entries)
        ]
    )
    data_side = tuple(
        (
            col_parts[position] if col_axes[which] == "mp" else row_parts[position]
            for position, (layer, which) in enumerate(entries)
        )
    ) + (norm_terms,)
    model_sums = jax.tree.map(
        lambda part: part.astype(jnp.float32), lax.psum(for_sending(model_side), "mp")
    )
    data_sums = lax.psum(data_side, "dp")
    norm_grad = lax.dynamic_slice_in_dim(
        data_sums[len(entries)], lax.axis_index("dp") * width, width, 2
    )
    row_sums = [
        model_sums[position] if col_axes[which] == "mp" else data_sums[position]
        for position, (layer, which) in enumerate(entries)
    ]
    col_sums = [
        data_sums[position] if col_axes[which] == "mp" else model_sums[position]
        for position, (layer, which) in enumerate(entries)
    ]
    row_news = [
        DECAY * row_olds[position] + (1.0 - DECAY) * row_sums[position] / col_counts[which]
        for position, (layer, which) in enumerate(entries)
    ]
    shares = jnp.stack(
        [
            jnp.sum(row_news[position]) / size_of(col_axes[which])
            for position, (layer, which) in enumerate(entries)
        ]
    )
    row_totals = lax.psum(shares, ("dp", "mp"))
    row_means = [
        row_totals[position] / row_counts[which] for position, (layer, which) in enumerate(entries)
    ]
    col_news = [
        DECAY * col_olds[position] + (1.0 - DECAY) * col_sums[position] / row_counts[which]
        for position, (layer, which) in enumerate(entries)
    ]
    directions, step_parts, weight_parts = ([], [], [])
    for position, (layer, which) in enumerate(entries):
        matrix = grads[position].reshape(grads[position].shape[0], -1)
        second = (
            row_news[position][:, None] * col_news[position].reshape(1, -1) / row_means[position]
        )
        direction = matrix * lax.rsqrt(second)
        directions.append(direction)
        step_parts.append(jnp.sum(direction * direction))
        master = masters[which][layer]
        weight_parts.append(jnp.sum(master * master))
    own_norms = lax.dynamic_slice_in_dim(norms, lax.axis_index("dp") * width, width, 2)
    norm_state_new = DECAY * norm_state + (1.0 - DECAY) * (norm_grad * norm_grad + EPS_SQUARE)
    norm_dirs = norm_grad * lax.rsqrt(norm_state_new)
    norm_parts = jnp.sum(norm_dirs * norm_dirs, axis=2) / lax.axis_size("mp")
    step_all = jnp.concatenate(
        [jnp.stack(step_parts).reshape(layers, 4), norm_parts], axis=1
    ).reshape(-1)
    step_total, weight_total = lax.psum((step_all, jnp.stack(weight_parts)), ("dp", "mp"))
    step_total = step_total.reshape(layers, 8)
    matrix_counts = jnp.asarray(
        [float(row_counts[which] * col_counts[which]) for which in range(4)], jnp.float32
    )
    update_rms = jnp.concatenate(
        [jnp.sqrt(step_total[:, :4] / matrix_counts[None, :]), jnp.sqrt(step_total[:, 4:] / D)],
        axis=1,
    )
    news = [[None] * layers for which in range(4)]
    rows_new = [[None] * layers for which in range(4)]
    cols_new = [[None] * layers for which in range(4)]
    for position, (layer, which) in enumerate(entries):
        master = masters[which][layer]
        scale = jnp.sqrt(weight_total[position] / (row_counts[which] * col_counts[which]) + 1e-06)
        clipped = directions[position] / jnp.maximum(1.0, update_rms[layer, which] / CLIP)
        news[which][layer] = master - RATE * scale * clipped.reshape(master.shape)
        rows_new[which][layer] = row_news[position]
        cols_new[which][layer] = col_news[position]
    norm_scale = jnp.sqrt(jnp.mean(norms * norms, axis=2) + 1e-06)
    norm_clipped = norm_dirs / jnp.maximum(1.0, update_rms[:, 4:] / CLIP)[:, :, None]
    norm_new = own_norms - RATE * norm_scale[:, :, None] * norm_clipped
    grad_out = [jnp.stack([reduced[layer][which] for layer in range(layers)]) for which in range(4)]
    new_out = [jnp.stack(news[which]) for which in range(4)]
    row_out = [jnp.stack(rows_new[which]) for which in range(4)]
    col_out = [jnp.stack(cols_new[which]) for which in range(4)]
    return (
        activations,
        grad,
        grad_out[0],
        grad_out[1],
        grad_out[2],
        grad_out[3],
        norm_grad,
        new_out[0],
        new_out[1],
        new_out[2],
        new_out[3],
        norm_new,
        new_out[0].astype(jnp.bfloat16),
        new_out[1].astype(jnp.bfloat16),
        new_out[2].astype(jnp.bfloat16),
        new_out[3].astype(jnp.bfloat16),
        row_out[0],
        col_out[0],
        row_out[1],
        col_out[1],
        row_out[2],
        col_out[2],
        row_out[3],
        col_out[3],
        norm_state_new[:, 0:2],
        norm_state_new[:, 2:4],
        update_rms,
    )


def solution(mesh):
    in_specs = (
        P(("dp", "mp"), None),
        P(("dp", "mp"), None),
        P("dp"),
        P(None, "dp", None, "mp"),
        P(None, "mp", "dp"),
        P(None, "dp", "mp"),
        P(None, "mp", "dp"),
        P(),
        P(None, "dp"),
        P(None, None, "mp"),
        P(None, "mp"),
        P(None, "dp"),
        P(None, "dp"),
        P(None, "mp"),
        P(None, "mp"),
        P(None, "dp"),
        P(None, None, "dp"),
    )
    out_specs = (
        P(("dp", "mp"), None),
        P(("dp", "mp"), None),
        P(None, "dp", None, "mp"),
        P(None, "mp", "dp"),
        P(None, "dp", "mp"),
        P(None, "mp", "dp"),
        P(None, None, "dp"),
        P(None, "dp", None, "mp"),
        P(None, "mp", "dp"),
        P(None, "dp", "mp"),
        P(None, "mp", "dp"),
        P(None, None, "dp"),
        P(None, "dp", None, "mp"),
        P(None, "mp", "dp"),
        P(None, "dp", "mp"),
        P(None, "mp", "dp"),
        P(None, "dp"),
        P(None, None, "mp"),
        P(None, "mp"),
        P(None, "dp"),
        P(None, "dp"),
        P(None, "mp"),
        P(None, "mp"),
        P(None, "dp"),
        P(None, None, "dp"),
        P(None, None, "dp"),
        P(),
    )
    return jax.shard_map(
        per_device, mesh=mesh, in_specs=in_specs, out_specs=out_specs, check_vma=False
    )
```

```python
import functools

import jax
import jax.numpy as jnp
from jax import lax
from jax.experimental import pallas as pl
from jax.experimental.pallas import tpu as pltpu
from jax.sharding import PartitionSpec as P

D = 768
HEAD_DIM = 64
FF = 3072


DECAY = 0.5
EPS_SQUARE = 1e-30
CLIP = 0.25
RATE = 2.0
MASKED = -1e30


def for_sending(value):
    return jax.tree.map(lambda a: a.astype(jnp.bfloat16) if a.dtype == jnp.float32 else a, value)


def layer_norm(rows, gain, shift):
    centre = rows - jnp.mean(rows, axis=-1, keepdims=True)
    spread = jnp.mean(centre * centre, axis=-1, keepdims=True)
    return centre * lax.rsqrt(spread + 1e-06) * gain + shift


def norm_back(rows, gain, shift, grad):
    result, back = jax.vjp(layer_norm, rows, gain, shift)
    return back(grad)


def exact_gelu(values):
    return jax.nn.gelu(values, approximate=False)


def segments(counts, length):
    bounds = jnp.cumsum(counts)
    places = jnp.arange(length, dtype=jnp.int32)
    image = jnp.sum((places[:, None] >= bounds[None, :]).astype(jnp.int32), axis=1)
    live = (places < bounds[-1]).astype(jnp.float32)
    return (image[:, None] == image[None, :], live)


def attention_scores(query, keys, same):
    scale = query.shape[-1] ** (-0.5)
    scores = jnp.einsum("qhd,khd->hqk", query, keys, preferred_element_type=jnp.float32) * scale
    return jnp.where(same[None], scores, MASKED)


def attend(qkv, same):
    scores = attention_scores(qkv[:, 0], qkv[:, 1], same)
    top = jnp.max(scores, axis=-1, keepdims=True)
    raised = jnp.exp(scores - top)
    total = jnp.sum(raised, axis=-1, keepdims=True)
    probs = (raised / total).astype(jnp.bfloat16)
    mixed = jnp.einsum("hqk,khd->qhd", probs, qkv[:, 2], preferred_element_type=jnp.float32)
    return (mixed.reshape(mixed.shape[0], -1), top + jnp.log(total))


def attend_back(qkv, same, log_total, grad_mixed):
    query, keys, values = (qkv[:, 0], qkv[:, 1], qkv[:, 2])
    scale = query.shape[-1] ** (-0.5)
    probs = jnp.exp(attention_scores(query, keys, same) - log_total)
    d_values = jnp.einsum(
        "hqk,qhd->khd", probs.astype(jnp.bfloat16), grad_mixed, preferred_element_type=jnp.float32
    )
    d_probs = jnp.einsum("qhd,khd->hqk", grad_mixed, values, preferred_element_type=jnp.float32)
    d_scores = (probs * (d_probs - jnp.sum(probs * d_probs, axis=-1, keepdims=True))).astype(
        jnp.bfloat16
    )
    d_query = jnp.einsum("hqk,khd->qhd", d_scores, keys, preferred_element_type=jnp.float32) * scale
    d_keys = jnp.einsum("hqk,qhd->khd", d_scores, query, preferred_element_type=jnp.float32) * scale
    return jnp.stack([d_query, d_keys, d_values], axis=1).astype(jnp.bfloat16)


def spread_rows(values):
    return lax.all_gather(values, "mp", axis=0, tiled=True)


def size_of(name):
    return lax.axis_size("dp") if name == "dp" else lax.axis_size("mp")


TILE = 112
VMEM_BYTES = 64 << 20
GROUP = 768
BIG = 1e30
MESH = pl.DeviceIdType.MESH
F32 = jnp.float32
BF16 = jnp.bfloat16
NN = ((1,), (0,))
NT = ((1,), (1,))
PLANE = [(dy, dx, dc) for dy in range(2) for dx in range(2) for dc in range(2)][1:]


def dot(left, right, dims):
    return lax.dot_general(left, right, (dims, ((), ())), preferred_element_type=F32)


class Place:
    def __init__(self, n_dp):
        self.nz = n_dp // 4
        me = lax.axis_index("dp")
        self.core = lax.axis_index("mp")
        self.z, self.y, self.x = me // 4, (me // 2) % 2, me % 2

    def at(self, z, y, x, core):
        return (z * 4 + y * 2 + x, core)

    def over_x(self):
        return self.at(self.z, self.y, 1 - self.x, self.core)

    def over_y(self):
        return self.at(self.z, 1 - self.y, self.x, self.core)

    def over_z(self, step):
        return self.at((self.z + step) % self.nz, self.y, self.x, self.core)

    def over_core(self):
        return self.at(self.z, self.y, self.x, 1 - self.core)

    def near(self, dy, dx, dc):
        return self.at(self.z, (self.y + dy) % 2, (self.x + dx) % 2, (self.core + dc) % 2)

    def barrier(self):
        sem = pltpu.get_barrier_semaphore()
        others = [self.near(dy, dx, dc) for dy, dx, dc in PLANE]
        others += [self.over_z(step) for step in range(1, self.nz)]
        for other in others:
            pl.semaphore_signal(sem, inc=1, device_id=other, device_id_type=MESH)
        pl.semaphore_wait(sem, len(others))


class Sender:
    def __init__(self, send_sems, recv_sems):
        self.send_sems, self.recv_sems = send_sems, recv_sems
        self.count = 0
        self.sent = []

    def start(self, src, dst, device):
        copy = pltpu.make_async_remote_copy(
            src_ref=src,
            dst_ref=dst,
            send_sem=self.send_sems.at[self.count],
            recv_sem=self.recv_sems.at[self.count],
            device_id=device,
            device_id_type=MESH,
        )
        self.count += 1
        copy.start()
        self.sent.append(copy)
        return copy

    def drain(self):
        for copy in self.sent:
            copy.wait_send()
        self.sent = []


class Gather:
    def __init__(self, place, sender, weights, groups):
        self.p, self.sender, self.weights, self.groups = place, sender, weights, groups
        self.first, self.second, self.third = {}, {}, {}
        self.tick_at = 0

    def cut(self, k):
        layer, low = self.groups[k]
        return self.weights[layer], low, low + GROUP // 2, low + GROUP

    def s1(self, k):
        if k >= len(self.groups):
            return
        w, low, mid, high = self.cut(k)
        p = self.p
        own = w.at[p.z, p.y, p.x, :, low:high]
        self.first[k] = [
            self.sender.start(own, own, p.over_z(step)) for step in range(1, p.nz)
        ]

    def s2(self, k):
        if k >= len(self.groups):
            return
        w, low, mid, high = self.cut(k)
        p = self.p
        for copy in self.first[k]:
            copy.wait_recv()
        a, b = w.at[:, p.y, p.x, :, low:mid], w.at[:, p.y, p.x, :, mid:high]
        self.second[k] = [
            self.sender.start(a, a, p.over_y()),
            self.sender.start(b, b, p.over_x()),
        ]

    def s3(self, k):
        if k < 0 or k >= len(self.groups):
            return
        w, low, mid, high = self.cut(k)
        p = self.p
        for copy in self.second[k]:
            copy.wait_recv()
        a, b = w.at[:, :, p.x, :, low:mid], w.at[:, p.y, :, :, mid:high]
        self.third[k] = [
            self.sender.start(a, a, p.over_x()),
            self.sender.start(b, b, p.over_y()),
        ]

    def tick(self):
        k = self.tick_at
        if k > len(self.groups):
            return
        self.s2(k)
        self.s1(k + 3)
        self.s3(k - 1)
        self.tick_at += 1

    def ready(self, k):
        while self.tick_at < k + 2:
            self.tick()
        for copy in self.third.pop(k, ()):
            copy.wait_recv()


class Rounds:
    def __init__(self, place, sender):
        self.p, self.sender = place, sender

    def plane(self, term, slots, cores=False):
        p = self.p
        at = p.y * 2 + p.x
        at = at * 2 + p.core if cores else at
        slots[at] = term[...]
        return [
            self.sender.start(term, slots.at[at], p.near(dy, dx, dc))
            for dy, dx, dc in PLANE
            if cores or not dc
        ]

    def along_z(self, term, slots):
        p = self.p
        slots[p.z] = term[...]
        return [self.sender.start(term, slots.at[p.z], p.over_z(step)) for step in range(1, p.nz)]


def slot_sum(copies, slots):
    for copy in copies:
        copy.wait_recv()
    total = slots[0]
    for at in range(1, slots.shape[0]):
        total = total + slots[at]
    return total


class Scatter:
    def __init__(self, place, sender, grads, groups, r1a, r1b, r2a, r2b, r3, result, cuts, by_row, by_column):
        self.cuts, self.by_row, self.by_column = cuts, by_row, by_column
        self.p, self.sender, self.grads, self.groups = place, sender, grads, groups
        self.r1a, self.r1b, self.r2a, self.r2b, self.r3 = r1a, r1b, r2a, r2b, r3
        self.result = result
        self.first, self.second, self.third = {}, {}, {}
        self.started = 0
        self.tick_at = 0

    def cut(self, k):
        layer, low = self.groups[k]
        return self.grads[layer], low, low + GROUP // 2, low + GROUP

    def s1(self):
        k = self.started
        self.started += 1
        g, low, mid, high = self.cut(k)
        p = self.p
        self.first[k] = [
            self.sender.start(g.at[:, :, 1 - p.x, :, low:mid], self.r1a.at[k % self.r1a.shape[0]], p.over_x()),
            self.sender.start(g.at[:, 1 - p.y, :, :, mid:high], self.r1b.at[k % self.r1b.shape[0]], p.over_y()),
        ]

    def s2(self, k):
        g, low, mid, high = self.cut(k)
        p = self.p
        for copy in self.first[k]:
            copy.wait_recv()
        a, b = g.at[:, :, p.x, :, low:mid], g.at[:, p.y, :, :, mid:high]
        for z in range(p.nz):
            a[z] = (a[z].astype(F32) + self.r1a[k % self.r1a.shape[0], z].astype(F32)).astype(BF16)
            b[z] = (b[z].astype(F32) + self.r1b[k % self.r1b.shape[0], z].astype(F32)).astype(BF16)
        self.second[k] = [
            self.sender.start(g.at[:, 1 - p.y, p.x, :, low:mid], self.r2a.at[k % 4], p.over_y()),
            self.sender.start(g.at[:, p.y, 1 - p.x, :, mid:high], self.r2b.at[k % 4], p.over_x()),
        ]

    def s3(self, k):
        g, low, mid, high = self.cut(k)
        p = self.p
        for copy in self.second[k]:
            copy.wait_recv()
        a, b = g.at[:, p.y, p.x, :, low:mid], g.at[:, p.y, p.x, :, mid:high]
        a[...] = (a[...].astype(F32) + self.r2a[k % 4].astype(F32)).astype(BF16)
        b[...] = (b[...].astype(F32) + self.r2b[k % 4].astype(F32)).astype(BF16)
        self.third[k] = [
            self.sender.start(
                g.at[(p.z + step) % p.nz, p.y, p.x, :, low:high],
                self.r3.at[k % 4, step - 1],
                p.over_z(step),
            )
            for step in range(1, p.nz)
        ]

    def finish(self, k):
        layer, low = self.groups[k]
        g, low, mid, high = self.cut(k)
        p = self.p
        for copy in self.third[k]:
            copy.wait_recv()
        total = g[p.z, p.y, p.x, :, low:high].astype(F32)
        for step in range(1, p.nz):
            total = total + self.r3[k % 4, step - 1].astype(F32)
        self.result[layer, :, low:high] = total
        squares = total * total + EPS_SQUARE
        self.by_column[layer][:, low:high] = jnp.sum(squares, axis=0, keepdims=True)
        lane = lax.broadcasted_iota(jnp.int32, (1, 128), 1)
        for which, (first, end) in enumerate(self.cuts):
            start, stop = max(first, low), min(end, high)
            if start < stop:
                part = jnp.sum(squares[:, start - low : stop - low], axis=1, keepdims=True)
                self.by_row[...] += jnp.where(lane == layer * 4 + which, part, 0.0)

    def tick(self):
        k = self.tick_at
        if k >= self.started + 2:
            return
        if k < self.started:
            self.s2(k)
        if 0 <= k - 1 < self.started:
            self.s3(k - 1)
        if 0 <= k - 2 < self.started:
            self.finish(k - 2)
        self.tick_at += 1


def row_tiles(length, body):
    def step(i, carry):
        body(pl.ds(pl.multiple_of(i * TILE, TILE), TILE))
        return carry

    lax.fori_loop(0, length // TILE, step, 0)


def normalised(rows):
    centre = rows - jnp.mean(rows, axis=-1, keepdims=True)
    spread = jnp.mean(centre * centre, axis=-1, keepdims=True)
    rise = lax.rsqrt(spread + 1e-06)
    return centre * rise, rise


def encode_segments(counts, slots, qe, ke):
    length = qe.shape[0]
    place = lax.broadcasted_iota(jnp.int32, (length, 128), 0)
    lane = lax.broadcasted_iota(jnp.int32, (length, 128), 1) % HEAD_DIM
    image = jnp.zeros((length, 128), jnp.int32)
    total = jnp.int32(0)
    for slot in range(slots):
        total = total + counts[slot]
        image = image + (place >= total).astype(jnp.int32)
    hit = image == lane
    ke[...] = jnp.where(hit, 1.0, 0.0).astype(BF16)
    qe[...] = jnp.where(jnp.logical_or(hit, lane > slots), 0.0, -BIG).astype(BF16)


def attention_forward(qkv, qe, ke, log_total, mixed, between=None):
    length, width = mixed.shape
    lane = lax.broadcasted_iota(jnp.int32, (length, 128), 1)

    def pair(at, carry):
        low = pl.multiple_of(at * 128, 128)
        query = qkv[:, pl.ds(low, 128)] * jnp.asarray(0.125, BF16)
        keys = qkv[:, pl.ds(width + low, 128)]
        values = qkv[:, pl.ds(2 * width + low, 128)].T
        outs = []
        for half in range(2):
            own = (lane < HEAD_DIM) if half == 0 else (lane >= HEAD_DIM)
            q = jnp.where(own, query, qe[...])
            k = jnp.where(own, keys, ke[...])
            scores = dot(k, q, NT)
            top = jnp.max(scores, axis=0, keepdims=True)
            raised = jnp.exp(scores - top)
            total = jnp.sum(raised, axis=0, keepdims=True)
            rows = slice(half * HEAD_DIM, (half + 1) * HEAD_DIM)
            outs.append(dot(values[rows], raised.astype(BF16), NN) / total)
            log_total[pl.ds(at * 2 + half, 1), :] = top + jnp.log(total)
        mixed[:, pl.ds(low, 128)] = jnp.concatenate(outs, axis=0).T.astype(BF16)
        return carry

    lax.fori_loop(0, width // 128, pair, 0)


def attention_backward(qkv, qe, ke, log_total, d_mixed):
    length, width = d_mixed.shape
    lane = lax.broadcasted_iota(jnp.int32, (length, 128), 1)

    def pair(at, carry):
        low = pl.multiple_of(at * 128, 128)
        query = qkv[:, pl.ds(low, 128)] * jnp.asarray(0.125, BF16)
        keys = qkv[:, pl.ds(width + low, 128)]
        values = qkv[:, pl.ds(2 * width + low, 128)]
        d_out = d_mixed[:, pl.ds(low, 128)]
        keys_t = keys.T
        d_query, d_keys, d_values = [], [], []
        for half in range(2):
            own = (lane < HEAD_DIM) if half == 0 else (lane >= HEAD_DIM)
            q = jnp.where(own, query, qe[...])
            k = jnp.where(own, keys, ke[...])
            v = jnp.where(own, values, jnp.zeros_like(values))
            probs = jnp.exp(dot(k, q, NT) - log_total[pl.ds(at * 2 + half, 1), :])
            d_probs = dot(v, d_out, NT)
            mean = jnp.sum(probs * d_probs, axis=0, keepdims=True)
            d_scores = (probs * (d_probs - mean)).astype(BF16)
            d_values.append(dot(probs.astype(BF16), d_out, NN))
            d_keys.append(dot(d_scores, query, NN))
            rows = slice(half * HEAD_DIM, (half + 1) * HEAD_DIM)
            d_query.append(dot(keys_t[rows], d_scores, NN))
        first = lane < HEAD_DIM
        d_q = jnp.concatenate(d_query, axis=0).T * 0.125
        qkv[:, pl.ds(low, 128)] = d_q.astype(BF16)
        qkv[:, pl.ds(width + low, 128)] = jnp.where(first, *d_keys).astype(BF16)
        qkv[:, pl.ds(2 * width + low, 128)] = jnp.where(first, *d_values).astype(BF16)
        return carry

    lax.fori_loop(0, width // 128, pair, 0)


class Exchange:
    def __init__(self, place, sender, out, into):
        self.p, self.sender, self.out, self.into = place, sender, out, into
        self.turn = 0
        self.copies = {}
        length = out.shape[1]
        cut = (length // TILE + 1) // 2 * TILE
        self.chunks = ((0, cut), (cut, length))

    def send(self, compute):
        slot = self.turn % 2
        for copy in self.copies.get(slot, ()):
            copy.wait_send()
            self.sender.sent = [item for item in self.sender.sent if item is not copy]
        self.copies[slot] = []
        for low, high in self.chunks:
            self.out[slot, low:high, :] = compute(low, high).astype(BF16)
            piece = self.out.at[slot, low:high, :]
            self.copies[slot].append(
                self.sender.start(piece, self.into.at[slot, low:high, :], self.p.over_core())
            )

    def take(self, body):
        slot = self.turn % 2
        self.turn += 1
        for (low, high), copy in zip(self.chunks, self.copies[slot]):
            copy.wait_recv()

            def step(i, carry, low=low):
                rows = pl.ds(pl.multiple_of(low + i * TILE, TILE), TILE)
                total = self.out[slot, rows, :].astype(F32) + self.into[slot, rows, :].astype(F32)
                body(rows, total)
                return carry

            lax.fori_loop(0, (high - low) // TILE, step, 0)


def grand_total(value):
    return jnp.sum(jnp.sum(value, axis=1, keepdims=True), axis=0, keepdims=True)


def flat(w, low, high):
    value = w[:, :, :, :, low:high]
    return value.reshape(-1, high - low)


def gelu_and_slope(hidden):
    cdf = 0.5 * (1.0 + lax.erf(hidden * (0.5**0.5)))
    slope = cdf + hidden * (jnp.exp(-0.5 * hidden * hidden) * 0.3989422804014327)
    return hidden * cdf, slope


def forward_kernel(
    n_dp, cuts, slots,
    counts, patches, qkv_w, out_w, up_w, down_w, norms,
    o_weights, o_rows, o_middle, o_normed_a, o_qkv, o_mixed, o_normed_b, o_active, o_slope, o_log,
    o_result, o_squares,
    w0, w1, rows, middle, normed_a, qkv, mixed, normed_b, active, slope, log_total, final,
    x_out, x_in, qe, ke, send_sems, recv_sems, local_sems,
):
    layers, half = 2, patches.shape[0]
    length = 2 * half
    c_qkv, c_out, c_up, c_down = cuts
    p = Place(n_dp)
    sender = Sender(send_sems, recv_sems)
    local = []

    def move(src, dst):
        copy = pltpu.make_async_copy(src, dst, local_sems.at[len(local)])
        copy.start()
        local.append(copy)
        return copy

    weights = (w0, w1)
    local_heads = qkv_w.shape[3]

    def master(layer, which):
        if which == 0:
            return [qkv_w[layer, part] for part in range(3)]
        return [(out_w, up_w, down_w)[which - 1][layer]]

    def place_pieces(layer):
        for which, (low, _) in enumerate(cuts):
            for part, value in enumerate(master(layer, which)):
                cols = slice(low + part * local_heads, low + part * local_heads + value.shape[1])
                weights[layer][p.z, p.y, p.x, :, cols] = value.astype(BF16)

    place_pieces(0)
    p.barrier()
    groups = [(l, low) for l in range(layers) for low in range(0, c_down[1], GROUP)]
    per = len(groups) // layers
    gather = Gather(p, sender, weights, groups)
    gather.s1(0)
    gather.s1(1)
    own_rows = pl.ds(pl.multiple_of(p.core * half, half), half)
    rows[0, own_rows, :] = patches[...].astype(F32)
    swap = sender.start(rows.at[0, own_rows, :], rows.at[0, own_rows, :], p.over_core())
    place_pieces(1)
    gather.s1(2)
    encode_segments(counts, slots, qe, ke)
    swap.wait_recv()
    exchange = Exchange(p, sender, x_out, x_in)

    def norm_into(target, layer, which, at, value):
        hat, _ = normalised(value)
        gain, shift = norms[layer, which : which + 1, :], norms[layer, which + 1 : which + 2, :]
        target[layer, at, :] = (hat * gain + shift).astype(BF16)

    row_tiles(length, lambda at: norm_into(normed_a, 0, 0, at, rows[0, at, :]))
    saves = [(rows, o_rows, 0), (normed_a, o_normed_a, 0)]

    def save(*items):
        for src, dst, layer in items:
            move(src.at[layer], dst.at[layer])

    save(*saves)
    for layer in range(layers):
        w, base = weights[layer], per * layer
        qkv_end = c_qkv[1]
        for k in range(-(-qkv_end // GROUP)):
            gather.ready(base + k)
            low, high = k * GROUP, min(qkv_end, (k + 1) * GROUP)
            qkv[layer, :, low:high] = dot(normed_a[layer], flat(w, low, high), NN).astype(BF16)
        gather.tick()
        attention_forward(qkv.at[layer], qe, ke, log_total.at[layer], mixed.at[layer])
        save((qkv, o_qkv, layer), (log_total, o_log, layer), (mixed, o_mixed, layer))
        gather.ready(base + (c_out[1] - 1) // GROUP)
        w_out = flat(w, *c_out)
        exchange.send(lambda low, high: dot(mixed[layer, low:high, :], w_out, NT))
        gather.tick()

        def mid_step(at, total):
            value = rows[layer, at, :] + total
            middle[layer, at, :] = value
            norm_into(normed_b, layer, 2, at, value)

        exchange.take(mid_step)
        save((middle, o_middle, layer), (normed_b, o_normed_b, layer))
        for k in range(c_up[0] // GROUP, c_up[1] // GROUP):
            gather.ready(base + k)
            low = k * GROUP - c_up[0]
            for at in range(0, GROUP, GROUP // 2):
                cols = slice(low + at, low + at + GROUP // 2)
                first = k * GROUP + at
                hidden = dot(normed_b[layer], flat(w, first, first + GROUP // 2), NN)
                act, rise = gelu_and_slope(hidden)
                active[layer, :, cols] = act.astype(BF16)
                slope[layer, :, cols] = rise.astype(BF16)
        save((active, o_active, layer), (slope, o_slope, layer))
        gather.tick()
        for k in range(c_down[0] // GROUP, c_down[1] // GROUP):
            gather.ready(base + k)
        if True:
            w_down = flat(w, *c_down)
            exchange.send(lambda low, high: dot(active[layer, low:high, :], w_down, NT))
        move(w, o_weights.at[layer])
        gather.tick()
        if layer + 1 < layers:

            def next_step(at, total):
                value = middle[layer, at, :] + total
                rows[layer + 1, at, :] = value
                norm_into(normed_a, layer + 1, 0, at, value)

            exchange.take(next_step)
            save((rows, o_rows, layer + 1), (normed_a, o_normed_a, layer + 1))
        else:

            def last_step(at, total):
                final[at, :] = middle[layer, at, :] + total

            exchange.take(last_step)
    o_result[...] = final[own_rows, :].astype(BF16)
    sender.drain()
    lane = lax.broadcasted_iota(jnp.int32, (1, 128), 1)
    squares = jnp.zeros((1, 128), F32)
    for layer in range(layers):
        for which in range(4):
            total = sum(grand_total(value * value) for value in master(layer, which))
            squares = squares + jnp.where(lane == layer * 4 + which, total, 0.0)
    o_squares[...] = squares
    for copy in local:
        copy.wait()


def backward_kernel(
    n_dp, cuts, totals, slots,
    counts, cotangent, norms, squares, row_states, qkv_c, out_c, up_c, down_c, norm_state,
    i_weights, i_rows, i_middle, i_normed_a, i_qkv, i_mixed, i_normed_b, i_active, i_slope, i_log,
    o_input, o_pieces, o_rows, o_columns, o_scalars, o_steps, o_own,
    g0, g1, r1a, r1b, r2a, r2b, r3,
    w, kept, normed_a, qkv, mixed, normed_b, active, slope, log_total,
    grad, rounded, turned, x_out, x_in, qe, ke, by_row, row_in, square, tall, small, few, last,
    send_sems, recv_sems, local_sems,
):
    layers, half = 2, cotangent.shape[0]
    length = 2 * half
    c_qkv, c_out, c_up, c_down = cuts
    p = Place(n_dp)
    sender = Sender(send_sems, recv_sems)
    count = [0]

    def load(src, dst):
        copy = pltpu.make_async_copy(src, dst, local_sems.at[count[0]])
        count[0] += 1
        copy.start()
        return copy

    def load_mlp(l):
        cols = slice(c_up[0], c_down[1])
        return dict(
            active=load(i_active.at[l], active),
            slope=load(i_slope.at[l], slope),
            weights=load(i_weights.at[l, :, :, :, :, cols], w.at[:, :, :, :, cols]),
            normed_b=load(i_normed_b.at[l], normed_b),
            middle=load(i_middle.at[l], kept),
        )

    def load_attention(l):
        cols = slice(c_qkv[0], c_out[1])
        return dict(
            mixed=load(i_mixed.at[l], mixed),
            weights=load(i_weights.at[l, :, :, :, :, cols], w.at[:, :, :, :, cols]),
            qkv=load(i_qkv.at[l], qkv),
            log=load(i_log.at[l], log_total),
            normed_a=load(i_normed_a.at[l], normed_a),
        )

    mlp = load_mlp(layers - 1)
    att = load_attention(layers - 1)
    p.barrier()
    own_rows = pl.ds(pl.multiple_of(p.core * half, half), half)
    total = jnp.int32(0)
    for slot in range(slots):
        total = total + counts[slot]
    place = lax.broadcasted_iota(jnp.int32, (half, 1), 0) + p.core * half
    grad[own_rows, :] = jnp.where(place < total, cotangent[...].astype(F32), 0.0)
    swap = sender.start(grad.at[own_rows, :], grad.at[own_rows, :], p.over_core())
    encode_segments(counts, slots, qe, ke)
    norm_sums = [small[layer][4] for layer in range(layers)]
    by_row[...] = jnp.zeros_like(by_row)
    for sums in norm_sums:
        sums[...] = jnp.zeros_like(sums)
    exchange = Exchange(p, sender, x_out, x_in)
    grads = (g0, g1)
    per = c_down[1] // GROUP
    order = [k for k in range(c_down[0] // GROUP, per)]
    order += [k for k in range(c_up[0] // GROUP, c_up[1] // GROUP)]
    order += [k for k in reversed(range(0, c_up[0] // GROUP))]
    groups = [(l, k * GROUP) for l in reversed(range(layers)) for k in order]
    scatter = Scatter(p, sender, grads, groups, r1a, r1b, r2a, r2b, r3, o_pieces, cuts, by_row,
                      [small[layer][0] for layer in range(layers)])
    swap.wait_recv()
    sender.drain()

    def store(layer, low, value):
        g = grads[layer]
        shape = g.shape[:4] + (value.shape[1],)
        g[:, :, :, :, low : low + value.shape[1]] = value.astype(BF16).reshape(shape)

    def norm_step(layer, which, at, total):
        hat, rise = normalised(kept[at, :])
        norm_sums[layer][which : which + 1, :] += jnp.sum(total * hat, axis=0, keepdims=True)
        norm_sums[layer][which + 1 : which + 2, :] += jnp.sum(total, axis=0, keepdims=True)
        d_hat = total * norms[layer, which : which + 1, :]
        flat_mean = jnp.mean(d_hat, axis=-1, keepdims=True)
        hat_mean = jnp.mean(d_hat * hat, axis=-1, keepdims=True)
        value = grad[at, :] + rise * (d_hat - flat_mean - hat * hat_mean)
        grad[at, :] = value
        rounded[at, :] = value.astype(BF16)

    def round_step(at):
        rounded[at, :] = grad[at, :].astype(BF16)

    row_tiles(length, round_step)
    for layer in reversed(range(layers)):
        turned[...] = rounded[...].T
        mlp["active"].wait()
        for k in range(c_down[0] // GROUP, c_down[1] // GROUP):
            low = k * GROUP - c_down[0]
            store(layer, k * GROUP, dot(turned[...], active[:, low : low + GROUP], NN))
            scatter.s1()
        mlp["weights"].wait()
        mlp["slope"].wait()
        step = GROUP // 2
        for at in range(0, c_down[1] - c_down[0], step):
            cols = slice(at, at + step)
            first = c_down[0] + at
            d_active = dot(rounded[...], flat(w, first, first + step), NN)
            slope[:, cols] = (d_active * slope[:, cols].astype(F32)).astype(BF16)
        scatter.tick()
        mlp["normed_b"].wait()
        turned[...] = normed_b[...].T
        for k in range(c_up[0] // GROUP, c_up[1] // GROUP):
            low = k * GROUP - c_up[0]
            store(layer, k * GROUP, dot(turned[...], slope[:, low : low + GROUP], NN))
            scatter.s1()
        w_up = flat(w, *c_up)
        exchange.send(lambda low, high: dot(slope[low:high, :], w_up, NT))
        scatter.tick()
        mlp["middle"].wait()
        exchange.take(lambda at, total: norm_step(layer, 2, at, total))
        rows_load = load(i_rows.at[layer], kept)
        if layer:
            mlp = load_mlp_next(load, layer - 1, i_active, i_slope, i_weights, i_normed_b,
                                active, slope, w, normed_b, slice(c_up[0], c_down[1]))
        turned[...] = rounded[...].T
        att["mixed"].wait()
        store(layer, c_out[0], dot(turned[...], mixed[...], NN))
        att["weights"].wait()
        mixed[...] = dot(rounded[...], flat(w, *c_out), NN).astype(BF16)
        scatter.tick()
        att["qkv"].wait()
        att["log"].wait()
        attention_backward(qkv, qe, ke, log_total, mixed)
        att["normed_a"].wait()
        turned[...] = normed_a[...].T
        for k in reversed(range(0, c_out[1] // GROUP)):
            low, high = k * GROUP, min(c_qkv[1], (k + 1) * GROUP)
            store(layer, low, dot(turned[...], qkv[:, low:high], NN))
            scatter.s1()
        w_qkv = flat(w, *c_qkv)
        exchange.send(lambda low, high: dot(qkv[low:high, :], w_qkv, NT))
        scatter.tick()
        rows_load.wait()
        exchange.take(lambda at, total: norm_step(layer, 0, at, total))
        if layer:
            mlp["middle"] = load(i_middle.at[layer - 1], kept)
            att = load_attention(layer - 1)
        scatter.tick()
    o_input[...] = grad[own_rows, :]
    rounds = Rounds(p, sender)
    in_plane, in_z = {}, {}

    def small_plane(layer):
        col, _, col_plane, _, norm, _, norm_plane, _ = small[layer]
        in_plane[layer] = (rounds.plane(col, col_plane), rounds.plane(norm, norm_plane))

    def small_z(layer):
        _, col, col_plane, col_z, _, norm, norm_plane, norm_z = small[layer]
        col[...] = slot_sum(in_plane[layer][0], col_plane)
        first = rounds.along_z(col, col_z)
        norm[...] = slot_sum(in_plane[layer][1], norm_plane)
        in_z[layer] = (first, rounds.along_z(norm, norm_z))

    while scatter.tick_at < len(groups) + 2:
        scatter.tick()
        if scatter.tick_at == len(groups):
            small_plane(1)
        if scatter.tick_at == len(groups) + 1:
            small_z(1)
    small_plane(0)
    lane = lax.broadcasted_iota(jnp.int32, (1, 128), 1)
    entries = [(layer, which) for layer in range(layers) for which in range(4)]
    columns_of = (None, out_c, up_c, down_c)

    def old_columns(layer, which):
        if which == 0:
            return jnp.concatenate([qkv_c[part, layer : layer + 1, :] for part in range(3)], axis=1)
        return columns_of[which][layer : layer + 1, :]

    swap = sender.start(by_row, row_in, p.over_core())
    square[...] = jnp.zeros_like(square)
    olds = jnp.zeros((1, 128), F32)
    for at, (layer, which) in enumerate(entries):
        old = row_states[which][layer : layer + 1, :]
        square[at : at + 1, 0 : old.shape[1]] = old
        share = 0.5
        if which % 2:
            old, share = old_columns(layer, which), 1.0 / n_dp
        olds = olds + jnp.where(lane == 16 + at, jnp.sum(old, axis=1, keepdims=True) * share, 0.0)
    depth = o_pieces.shape[1]
    width = norm_state.shape[2]
    few_term, few_mid, few_plane, few_z = few
    sums = jnp.sum(by_row[...], axis=0, keepdims=True) + olds + pltpu.roll(squares[...], 8, 1)
    few_term[...] = jnp.broadcast_to(sums, few_term.shape)
    few_plane_copies = rounds.plane(few_term, few_plane, True)
    old_rows = square[...].T[0:depth, :]
    small_z(0)
    few_mid[...] = slot_sum(few_plane_copies, few_plane)
    few_z_copies = rounds.along_z(few_mid, few_z)
    swap.wait_recv()
    counts_of = jnp.ones((1, 128), F32)
    for at, (layer, which) in enumerate(entries):
        counts_of = jnp.where(lane == at, 1.0 / totals[which], counts_of)
    new_rows = DECAY * old_rows + (1.0 - DECAY) * (by_row[...] + row_in[...]) * counts_of
    square[...] = jnp.zeros_like(square)
    square[0:depth, :] = new_rows
    o_rows[...] = square[...].T
    by_row_rise = lax.rsqrt(new_rows)
    columns = []
    for layer in range(layers):
        columns.append(slot_sum(in_z[layer][0], small[layer][3]))
    norm_totals = [slot_sum(in_z[layer][1], small[layer][7]) for layer in range(layers)]
    scalars = slot_sum(few_z_copies, few_z)[0:1, :]
    o_scalars[...] = scalars
    steps = jnp.zeros((1, 128), F32)
    for at, (layer, which) in enumerate(entries):
        low, high = cuts[which]
        fresh = columns[layer][:, low:high]
        new_cols = DECAY * old_columns(layer, which) + (1.0 - DECAY) / D * fresh
        o_columns[layer, :, low:high] = new_cols
        mean = row_mean(scalars, at, which, totals)
        by_col = lax.rsqrt(new_cols)
        step = o_pieces[layer, :, low:high] * by_row_rise[:, at : at + 1] * by_col
        steps = steps + jnp.where(lane == at, grand_total(step * step) * mean, 0.0)
    both = norm_totals + [norms[layer] for layer in range(layers)]
    both.append(jnp.zeros((128 - 16, D), F32))
    tall[...] = jnp.concatenate(both, axis=0).T
    me = p.z * 4 + p.y * 2 + p.x
    square[0:depth, :] = tall[pl.ds(pl.multiple_of(me * depth, 8), depth), :]
    o_own[...] = square[...].T
    for layer in range(layers):
        mine = o_own[layer * 4 : layer * 4 + 4, 0:width]
        state = DECAY * norm_state[layer] + (1.0 - DECAY) * (mine * mine + EPS_SQUARE)
        sizes = jnp.sum(mine * mine / state, axis=1, keepdims=True) * 0.5
        for kind in range(4):
            steps = steps + jnp.where(lane == 8 + layer * 4 + kind, sizes[kind : kind + 1], 0.0)
    last_term, last_mid, last_plane, last_z = last
    last_term[...] = jnp.broadcast_to(steps, last_term.shape)
    last_copies = rounds.plane(last_term, last_plane, True)
    last_mid[...] = slot_sum(last_copies, last_plane)
    last_copies = rounds.along_z(last_mid, last_z)
    o_steps[...] = slot_sum(last_copies, last_z)[0:1, :]
    sender.drain()


def row_mean(scalars, at, which, totals):
    count = totals[3] if which == 3 else D
    mean = DECAY * scalars[:, 16 + at : 17 + at] / count
    return mean + (1.0 - DECAY) * scalars[:, at : at + 1] / (D * totals[which])


def load_mlp_next(load, l, i_active, i_slope, i_weights, i_normed_b, active, slope, w, normed_b, cols):
    return dict(
        active=load(i_active.at[l], active),
        slope=load(i_slope.at[l], slope),
        weights=load(i_weights.at[l, :, :, :, :, cols], w.at[:, :, :, :, cols]),
        normed_b=load(i_normed_b.at[l], normed_b),
    )


def apply_kernel(
    cuts, totals,
    result, grad, sums, rows, columns, scalars, steps, own, qkv_w, out_w, up_w, down_w, norms,
    norm_state,
    o_result, o_grad, g_qkv, g_out, g_up, g_down, g_norm, n_qkv, n_out, n_up, n_down, n_norm,
    k_qkv, k_out, k_up, k_down,
    qkv_rn, qkv_cn, out_rn, out_cn, up_rn, up_cn, down_rn, down_cn, moments_a, moments_f, rms,
    square,
):
    layers, depth = sums.shape[0], sums.shape[1]
    width, local = norm_state.shape[2], qkv_w.shape[3]
    o_result[...] = result[...]
    o_grad[...] = grad[...]
    lane = lax.broadcasted_iota(jnp.int32, (1, 128), 1)
    entries = [(layer, which) for layer in range(layers) for which in range(4)]
    means = jnp.ones((1, 128), F32)
    for at, (layer, which) in enumerate(entries):
        means = jnp.where(lane == at, 1.0 / (D * totals[which]), means)
        means = jnp.where(lane == 8 + at, 1.0 / D, means)
    size = jnp.sqrt(steps[...] * means)
    shrink = 1.0 / jnp.maximum(1.0, size / CLIP)
    row_news = (qkv_rn, out_cn, up_rn, down_cn)
    square[...] = rows[...].T
    by_row = lax.rsqrt(square[0:depth, :])
    for layer in range(layers):
        rms[layer : layer + 1, 0:4] = size[:, layer * 4 : layer * 4 + 4]
        rms[layer : layer + 1, 4:8] = size[:, 8 + layer * 4 : 12 + layer * 4]
        vectors = norms[layer]
        scale = jnp.sqrt(jnp.mean(vectors * vectors, axis=1, keepdims=True) + 1e-06)
        shrinks = jnp.concatenate(
            [shrink[:, 8 + layer * 4 + kind : 9 + layer * 4 + kind] for kind in range(4)], axis=0
        )
        mine = own[layer * 4 : layer * 4 + 4, 0:width]
        state = DECAY * norm_state[layer] + (1.0 - DECAY) * (mine * mine + EPS_SQUARE)
        g_norm[layer] = mine
        moments_a[layer] = state[0:2]
        moments_f[layer] = state[2:4]
        before = own[8 + layer * 4 : 12 + layer * 4, 0:width]
        n_norm[layer] = before - RATE * scale * (mine * lax.rsqrt(state) * shrinks)
    for at, (layer, which) in enumerate(entries):
        row_news[which][layer : layer + 1, :] = rows[at : at + 1, 0:depth]
        scale = jnp.sqrt(scalars[:, 8 + at : 9 + at] / (D * totals[which]) + 1e-06)
        factor = RATE * scale * shrink[:, at : at + 1]
        factor = factor * jnp.sqrt(row_mean(scalars[...], at, which, totals))
        factor = factor * by_row[:, at : at + 1]
        for part in range(3 if which == 0 else 1):
            low, high = cuts[which]
            if which == 0:
                low, high = part * local, part * local + local
                refs = [ref.at[layer, part] for ref in (qkv_w, g_qkv, n_qkv, k_qkv)]
                qkv_cn[part, layer : layer + 1, :] = columns[layer, :, low:high]
            else:
                table = (
                    (out_w, g_out, n_out, k_out),
                    (up_w, g_up, n_up, k_up),
                    (down_w, g_down, n_down, k_down),
                )
                refs = [ref.at[layer] for ref in table[which - 1]]
                new_ref = (out_rn, up_cn, down_rn)[which - 1]
                new_ref[layer : layer + 1, :] = columns[layer, :, low:high]
            grad_piece = sums[layer, :, low:high]
            new = refs[0][...] - grad_piece * factor * lax.rsqrt(columns[layer, :, low:high])
            refs[1][...] = grad_piece
            refs[2][...] = new
            refs[3][...] = new.astype(BF16)


def passes_by_xla(
    patches,
    cotangent,
    patch_counts,
    qkv_weight,
    out_weight,
    up_weight,
    down_weight,
    norms,
):
    layers = qkv_weight.shape[0]
    half = patches.shape[0]
    length = half * lax.axis_size("mp")
    same, live_all = segments(patch_counts, length)
    live = lax.dynamic_slice_in_dim(live_all, lax.axis_index("mp") * half, half)
    rows = patches.astype(jnp.float32)
    kept = []
    for layer in range(layers):
        pieces = (
            qkv_weight[layer].astype(jnp.bfloat16),
            out_weight[layer].astype(jnp.bfloat16),
            up_weight[layer].astype(jnp.bfloat16),
            down_weight[layer].astype(jnp.bfloat16),
        )
        whole = (
            lax.all_gather(pieces[0], "dp", axis=0, tiled=True),
            lax.all_gather(pieces[1], "dp", axis=1, tiled=True),
            lax.all_gather(pieces[2], "dp", axis=0, tiled=True),
            lax.all_gather(pieces[3], "dp", axis=1, tiled=True),
        )
        w_qkv, w_out, w_up, w_down = whole
        local = w_qkv.shape[2]
        normed_a = spread_rows(
            layer_norm(rows, norms[layer, 0], norms[layer, 1]).astype(jnp.bfloat16)
        )
        qkv = jnp.dot(normed_a, w_qkv.reshape(D, 3 * local), preferred_element_type=jnp.float32)
        qkv = qkv.astype(jnp.bfloat16).reshape(length, 3, local // HEAD_DIM, HEAD_DIM)
        mixed, log_total = attend(qkv, same)
        mixed = mixed.astype(jnp.bfloat16)
        middle = rows + lax.psum_scatter(
            jnp.dot(mixed, w_out, preferred_element_type=jnp.float32).astype(jnp.bfloat16),
            "mp",
            scatter_dimension=0,
            tiled=True,
        ).astype(jnp.float32)
        normed_b = spread_rows(
            layer_norm(middle, norms[layer, 2], norms[layer, 3]).astype(jnp.bfloat16)
        )
        hidden = jnp.dot(normed_b, w_up, preferred_element_type=jnp.float32)
        active = exact_gelu(hidden).astype(jnp.bfloat16)
        after = middle + lax.psum_scatter(
            jnp.dot(active, w_down, preferred_element_type=jnp.float32).astype(jnp.bfloat16),
            "mp",
            scatter_dimension=0,
            tiled=True,
        ).astype(jnp.float32)
        stored = None
        kept.append(
            (
                rows,
                normed_a,
                qkv,
                log_total,
                mixed,
                middle,
                normed_b,
                hidden,
                active,
                stored,
                pieces,
            )
        )
        rows = after
    activations = rows.astype(jnp.bfloat16)
    grad = cotangent.astype(jnp.float32) * live[:, None]
    reduced = [None] * layers
    for layer in reversed(range(layers)):
        (
            rows_in,
            normed_a,
            qkv,
            log_total,
            mixed,
            middle,
            normed_b,
            hidden,
            active,
            stored,
            pieces,
        ) = kept[layer]
        whole = (
            lax.all_gather(pieces[0], "dp", axis=0, tiled=True),
            lax.all_gather(pieces[1], "dp", axis=1, tiled=True),
            lax.all_gather(pieces[2], "dp", axis=0, tiled=True),
            lax.all_gather(pieces[3], "dp", axis=1, tiled=True),
        )
        w_qkv, w_out, w_up, w_down = whole
        local = w_qkv.shape[2]
        grad_down = spread_rows(grad.astype(jnp.bfloat16))
        g_down = jnp.einsum("tf,td->fd", active, grad_down, preferred_element_type=jnp.float32)
        d_active = jnp.einsum("td,fd->tf", grad_down, w_down, preferred_element_type=jnp.float32)
        gelu_value, gelu_back = jax.vjp(exact_gelu, hidden)
        d_hidden = gelu_back(d_active)[0].astype(jnp.bfloat16)
        g_up = jnp.einsum("td,tf->df", normed_b, d_hidden, preferred_element_type=jnp.float32)
        d_normed_b = lax.psum_scatter(
            jnp.einsum("tf,df->td", d_hidden, w_up, preferred_element_type=jnp.float32).astype(
                jnp.bfloat16
            ),
            "mp",
            scatter_dimension=0,
            tiled=True,
        ).astype(jnp.float32)
        d_middle, g_gain_b, g_shift_b = norm_back(
            middle, norms[layer, 2], norms[layer, 3], d_normed_b
        )
        grad_mid = grad + d_middle
        grad_out = spread_rows(grad_mid.astype(jnp.bfloat16))
        g_out = jnp.einsum("tc,td->cd", mixed, grad_out, preferred_element_type=jnp.float32)
        d_mixed = jnp.einsum(
            "td,cd->tc", grad_out, w_out, preferred_element_type=jnp.float32
        ).astype(jnp.bfloat16)
        d_qkv = attend_back(
            qkv, same, log_total, d_mixed.reshape(length, local // HEAD_DIM, HEAD_DIM)
        )
        d_qkv = d_qkv.reshape(length, 3 * local)
        g_qkv = jnp.einsum(
            "td,tc->dc", normed_a, d_qkv, preferred_element_type=jnp.float32
        ).reshape(D, 3, local)
        d_normed_a = lax.psum_scatter(
            jnp.einsum(
                "tc,dc->td", d_qkv, w_qkv.reshape(D, 3 * local), preferred_element_type=jnp.float32
            ).astype(jnp.bfloat16),
            "mp",
            scatter_dimension=0,
            tiled=True,
        ).astype(jnp.float32)
        d_input, g_gain_a, g_shift_a = norm_back(
            rows_in, norms[layer, 0], norms[layer, 1], d_normed_a
        )
        grad = grad_mid + d_input
        norm_terms = jnp.stack([g_gain_a, g_shift_a, g_gain_b, g_shift_b])
        reduced[layer] = (
            lax.psum_scatter(g_qkv, "dp", scatter_dimension=0, tiled=True),
            lax.psum_scatter(g_out, "dp", scatter_dimension=1, tiled=True),
            lax.psum_scatter(g_up, "dp", scatter_dimension=0, tiled=True),
            lax.psum_scatter(g_down, "dp", scatter_dimension=1, tiled=True),
            lax.psum(norm_terms, "mp"),
        )
    return activations, grad, [item[:4] for item in reduced], jnp.stack([item[4] for item in reduced])


def step_by_kernels(
    patches,
    cotangent,
    patch_counts,
    qkv_weight,
    out_weight,
    up_weight,
    down_weight,
    norms,
    qkv_rows,
    qkv_cols,
    out_rows,
    out_cols,
    up_rows,
    up_cols,
    down_rows,
    down_cols,
    norm_state,
):
    layers, depth, _, local = qkv_weight.shape
    n_dp = lax.axis_size("dp")
    nz, half, wide = n_dp // 4, patches.shape[0], up_weight.shape[2]
    length, slots = 2 * half, patch_counts.shape[0]
    ends = [0, 3 * local, 4 * local, 4 * local + wide, 4 * local + 2 * wide]
    cuts = tuple(zip(ends[:-1], ends[1:]))
    totals = tuple(2.0 * (high - low) for low, high in cuts)
    columns, n_groups = ends[-1], layers * ends[-1] // GROUP
    masters = (
        qkv_weight.transpose(0, 2, 1, 3),
        out_weight.transpose(0, 2, 1),
        up_weight,
        down_weight.transpose(0, 2, 1),
    )
    states_by_row = (qkv_rows, out_cols, up_rows, down_cols)
    states_by_column = (qkv_cols.transpose(1, 0, 2), out_rows, up_cols, down_rows)
    vmem, smem, hbm = [
        pl.BlockSpec(memory_space=space) for space in (pltpu.VMEM, pltpu.SMEM, pl.ANY)
    ]
    shape = jax.ShapeDtypeStruct
    whole = (nz, 2, 2, depth, columns)
    rows_f32, rows_bf16 = ((length, D), F32), ((length, D), BF16)
    kept = [
        rows_f32,
        rows_f32,
        rows_bf16,
        ((length, 3 * local), BF16),
        ((length, local), BF16),
        rows_bf16,
        ((length, wide), BF16),
        ((length, wide), BF16),
        ((8, length), F32),
    ]
    saved = [shape((layers,) + dims, kind) for dims, kind in kept]
    line = shape((1, 128), F32)
    sems = [
        pltpu.SemaphoreType.DMA((160,)),
        pltpu.SemaphoreType.DMA((160,)),
        pltpu.SemaphoreType.DMA((32,)),
    ]
    codes = [pltpu.VMEM((length, 128), BF16)] * 2
    swaps = [pltpu.VMEM((2, length, D), BF16)] * 2

    def around(dims, plane):
        return [pltpu.VMEM(dims, F32)] * 2 + [
            pltpu.VMEM((places,) + dims, F32) for places in (plane, nz)
        ]

    outs = pl.pallas_call(
        functools.partial(forward_kernel, n_dp, cuts, slots),
        out_shape=[shape((layers,) + whole, BF16)] + saved + [shape((half, D), BF16), line],
        in_specs=[smem] + [vmem] * 6,
        out_specs=[hbm] * (1 + len(saved)) + [vmem] * 2,
        scratch_shapes=[pltpu.VMEM(whole, BF16)] * layers
        + [pltpu.VMEM((layers,) + dims, kind) for dims, kind in kept]
        + [pltpu.VMEM((length, D), F32)]
        + swaps
        + codes
        + sems,
        compiler_params=pltpu.CompilerParams(
            collective_id=0, has_side_effects=True, vmem_limit_bytes=VMEM_BYTES
        ),
        name="forward",
    )(patch_counts, patches, *masters, norms)
    saved, activations, squares = outs[:-2], outs[-2], outs[-1]
    own = (nz, 2, depth, GROUP // 2)
    small = around((1, columns), 4) + around((4, D), 4)
    grad, sums, rows, fresh, scalars, steps, norm_own = pl.pallas_call(
        functools.partial(backward_kernel, n_dp, cuts, totals, slots),
        out_shape=[
            shape((half, D), F32),
            shape((layers, depth, columns), F32),
            shape((128, 128), F32),
            shape((layers, 1, columns), F32),
            line,
            line,
            shape((128, 128), F32),
        ],
        in_specs=[smem] + [vmem] * 3 + [(vmem,) * 4] + [vmem] * 5 + [hbm] * len(saved),
        out_specs=[vmem] * 7,
        scratch_shapes=[pltpu.VMEM(whole, BF16)] * layers
        + [pltpu.VMEM((n_groups // 2,) + own, BF16)] * 2
        + [pltpu.VMEM((4, nz, depth, GROUP // 2), BF16)] * 2
        + [pltpu.VMEM((4, nz - 1, depth, GROUP), BF16)]
        + [pltpu.VMEM(whole, BF16)]
        + [pltpu.VMEM(dims, kind) for dims, kind in kept[1:]]
        + [
            pltpu.VMEM((length, D), F32),
            pltpu.VMEM((length, D), BF16),
            pltpu.VMEM((D, length), BF16),
        ]
        + swaps
        + codes
        + [pltpu.VMEM((depth, 128), F32)] * 2
        + [pltpu.VMEM((128, 128), F32), pltpu.VMEM((D, 128), F32)]
        + [[small] * layers, around((8, 128), 8), around((8, 128), 8)]
        + sems,
        compiler_params=pltpu.CompilerParams(
            collective_id=1, has_side_effects=True, vmem_limit_bytes=VMEM_BYTES
        ),
        name="backward",
    )(
        patch_counts,
        cotangent,
        norms,
        squares,
        states_by_row,
        *states_by_column,
        norm_state,
        *saved,
    )
    like = lambda arrays, kind: [shape(array.shape, kind) for array in arrays]
    vectors = [shape(norm_state.shape, F32)]
    states = (
        qkv_rows, states_by_column[0], out_rows, out_cols,
        up_rows, up_cols, down_rows, down_cols,
    )
    results = [shape((half, D), BF16), shape((half, D), F32)]
    results += like(masters, F32) + vectors + like(masters, F32) + vectors + like(masters, BF16)
    results += like(states, F32)
    results += [shape((layers, 2, norm_state.shape[2]), F32)] * 2 + [shape((layers, 8), F32)]
    out = pl.pallas_call(
        functools.partial(apply_kernel, cuts, totals),
        out_shape=results,
        in_specs=[vmem] * 14,
        out_specs=[vmem] * len(results),
        scratch_shapes=[pltpu.VMEM((128, 128), F32)],
        compiler_params=pltpu.CompilerParams(vmem_limit_bytes=VMEM_BYTES),
        name="apply",
    )(
        activations, grad, sums, rows, fresh, scalars, steps, norm_own, *masters, norms, norm_state
    )
    out = list(out)
    for at in (2, 7, 12):
        out[at] = out[at].transpose(0, 2, 1, 3)
        out[at + 1] = out[at + 1].transpose(0, 2, 1)
        out[at + 3] = out[at + 3].transpose(0, 2, 1)
    out[17] = out[17].transpose(1, 0, 2)
    return tuple(out)


def kernels_fit(patches, qkv_weight):
    length = 2 * patches.shape[0]
    depth, local = qkv_weight.shape[1], qkv_weight.shape[3]
    return (
        lax.axis_size("mp") == 2
        and lax.axis_size("dp") % 4 == 0
        and depth % 16 == 0
        and length % TILE == 0
        and (4 * local) % GROUP == 0
    )


def per_device(*arrays):
    if kernels_fit(arrays[0], arrays[3]):
        return step_by_kernels(*arrays)
    return step_by_xla(*arrays)


def step_by_xla(
    patches,
    cotangent,
    patch_counts,
    qkv_weight,
    out_weight,
    up_weight,
    down_weight,
    norms,
    qkv_rows,
    qkv_cols,
    out_rows,
    out_cols,
    up_rows,
    up_cols,
    down_rows,
    down_cols,
    norm_state,
):
    layers = qkv_weight.shape[0]
    activations, grad, reduced, norm_terms = passes_by_xla(
        patches, cotangent, patch_counts, qkv_weight, out_weight, up_weight, down_weight, norms
    )
    col_axes = ("mp", "dp", "mp", "dp")
    row_counts = (D, D, D, FF)
    col_counts = (3 * D, D, FF, D)
    masters = (qkv_weight, out_weight, up_weight, down_weight)
    row_states = (qkv_rows, out_rows, up_rows, down_rows)
    col_states = (qkv_cols, out_cols, up_cols, down_cols)
    entries = [(layer, which) for layer in range(layers) for which in range(4)]
    grads = [reduced[layer][which] for layer, which in entries]
    row_olds = [row_states[which][layer] for layer, which in entries]
    col_olds = [col_states[which][layer] for layer, which in entries]
    width = norm_state.shape[2]
    row_parts, col_parts = ([], [])
    for position, (layer, which) in enumerate(entries):
        matrix = grads[position].reshape(grads[position].shape[0], -1)
        square = matrix * matrix + EPS_SQUARE
        row_parts.append(jnp.sum(square, axis=1))
        col_parts.append(jnp.sum(square, axis=0).reshape(col_olds[position].shape))
    model_side = tuple(
        [
            row_parts[position] if col_axes[which] == "mp" else col_parts[position]
            for position, (layer, which) in enumerate(entries)
        ]
    )
    data_side = tuple(
        (
            col_parts[position] if col_axes[which] == "mp" else row_parts[position]
            for position, (layer, which) in enumerate(entries)
        )
    ) + (norm_terms,)
    model_sums = jax.tree.map(
        lambda part: part.astype(jnp.float32), lax.psum(for_sending(model_side), "mp")
    )
    data_sums = lax.psum(data_side, "dp")
    norm_grad = lax.dynamic_slice_in_dim(
        data_sums[len(entries)], lax.axis_index("dp") * width, width, 2
    )
    row_sums = [
        model_sums[position] if col_axes[which] == "mp" else data_sums[position]
        for position, (layer, which) in enumerate(entries)
    ]
    col_sums = [
        data_sums[position] if col_axes[which] == "mp" else model_sums[position]
        for position, (layer, which) in enumerate(entries)
    ]
    row_news = [
        DECAY * row_olds[position] + (1.0 - DECAY) * row_sums[position] / col_counts[which]
        for position, (layer, which) in enumerate(entries)
    ]
    shares = jnp.stack(
        [
            jnp.sum(row_news[position]) / size_of(col_axes[which])
            for position, (layer, which) in enumerate(entries)
        ]
    )
    row_totals = lax.psum(shares, ("dp", "mp"))
    row_means = [
        row_totals[position] / row_counts[which] for position, (layer, which) in enumerate(entries)
    ]
    col_news = [
        DECAY * col_olds[position] + (1.0 - DECAY) * col_sums[position] / row_counts[which]
        for position, (layer, which) in enumerate(entries)
    ]
    directions, step_parts, weight_parts = ([], [], [])
    for position, (layer, which) in enumerate(entries):
        matrix = grads[position].reshape(grads[position].shape[0], -1)
        second = (
            row_news[position][:, None] * col_news[position].reshape(1, -1) / row_means[position]
        )
        direction = matrix * lax.rsqrt(second)
        directions.append(direction)
        step_parts.append(jnp.sum(direction * direction))
        master = masters[which][layer]
        weight_parts.append(jnp.sum(master * master))
    own_norms = lax.dynamic_slice_in_dim(norms, lax.axis_index("dp") * width, width, 2)
    norm_state_new = DECAY * norm_state + (1.0 - DECAY) * (norm_grad * norm_grad + EPS_SQUARE)
    norm_dirs = norm_grad * lax.rsqrt(norm_state_new)
    norm_parts = jnp.sum(norm_dirs * norm_dirs, axis=2) / lax.axis_size("mp")
    step_all = jnp.concatenate(
        [jnp.stack(step_parts).reshape(layers, 4), norm_parts], axis=1
    ).reshape(-1)
    step_total, weight_total = lax.psum((step_all, jnp.stack(weight_parts)), ("dp", "mp"))
    step_total = step_total.reshape(layers, 8)
    matrix_counts = jnp.asarray(
        [float(row_counts[which] * col_counts[which]) for which in range(4)], jnp.float32
    )
    update_rms = jnp.concatenate(
        [jnp.sqrt(step_total[:, :4] / matrix_counts[None, :]), jnp.sqrt(step_total[:, 4:] / D)],
        axis=1,
    )
    news = [[None] * layers for which in range(4)]
    rows_new = [[None] * layers for which in range(4)]
    cols_new = [[None] * layers for which in range(4)]
    for position, (layer, which) in enumerate(entries):
        master = masters[which][layer]
        scale = jnp.sqrt(weight_total[position] / (row_counts[which] * col_counts[which]) + 1e-06)
        clipped = directions[position] / jnp.maximum(1.0, update_rms[layer, which] / CLIP)
        news[which][layer] = master - RATE * scale * clipped.reshape(master.shape)
        rows_new[which][layer] = row_news[position]
        cols_new[which][layer] = col_news[position]
    norm_scale = jnp.sqrt(jnp.mean(norms * norms, axis=2) + 1e-06)
    norm_clipped = norm_dirs / jnp.maximum(1.0, update_rms[:, 4:] / CLIP)[:, :, None]
    norm_new = own_norms - RATE * norm_scale[:, :, None] * norm_clipped
    grad_out = [jnp.stack([reduced[layer][which] for layer in range(layers)]) for which in range(4)]
    new_out = [jnp.stack(news[which]) for which in range(4)]
    row_out = [jnp.stack(rows_new[which]) for which in range(4)]
    col_out = [jnp.stack(cols_new[which]) for which in range(4)]
    return (
        activations,
        grad,
        grad_out[0],
        grad_out[1],
        grad_out[2],
        grad_out[3],
        norm_grad,
        new_out[0],
        new_out[1],
        new_out[2],
        new_out[3],
        norm_new,
        new_out[0].astype(jnp.bfloat16),
        new_out[1].astype(jnp.bfloat16),
        new_out[2].astype(jnp.bfloat16),
        new_out[3].astype(jnp.bfloat16),
        row_out[0],
        col_out[0],
        row_out[1],
        col_out[1],
        row_out[2],
        col_out[2],
        row_out[3],
        col_out[3],
        norm_state_new[:, 0:2],
        norm_state_new[:, 2:4],
        update_rms,
    )


def solution(mesh):
    in_specs = (
        P(("dp", "mp"), None),
        P(("dp", "mp"), None),
        P("dp"),
        P(None, "dp", None, "mp"),
        P(None, "mp", "dp"),
        P(None, "dp", "mp"),
        P(None, "mp", "dp"),
        P(),
        P(None, "dp"),
        P(None, None, "mp"),
        P(None, "mp"),
        P(None, "dp"),
        P(None, "dp"),
        P(None, "mp"),
        P(None, "mp"),
        P(None, "dp"),
        P(None, None, "dp"),
    )
    out_specs = (
        P(("dp", "mp"), None),
        P(("dp", "mp"), None),
        P(None, "dp", None, "mp"),
        P(None, "mp", "dp"),
        P(None, "dp", "mp"),
        P(None, "mp", "dp"),
        P(None, None, "dp"),
        P(None, "dp", None, "mp"),
        P(None, "mp", "dp"),
        P(None, "dp", "mp"),
        P(None, "mp", "dp"),
        P(None, None, "dp"),
        P(None, "dp", None, "mp"),
        P(None, "mp", "dp"),
        P(None, "dp", "mp"),
        P(None, "mp", "dp"),
        P(None, "dp"),
        P(None, None, "mp"),
        P(None, "mp"),
        P(None, "dp"),
        P(None, "dp"),
        P(None, "mp"),
        P(None, "mp"),
        P(None, "dp"),
        P(None, None, "dp"),
        P(None, None, "dp"),
        P(),
    )
    return jax.shard_map(
        per_device, mesh=mesh, in_specs=in_specs, out_specs=out_specs, check_vma=False
    )
```

```python
import functools

import jax
import jax.numpy as jnp
from jax import lax
from jax.experimental import pallas as pl
from jax.experimental.pallas import tpu as pltpu
from jax.sharding import PartitionSpec as P

D = 768
HEAD_DIM = 64
FF = 3072


DECAY = 0.5
EPS_SQUARE = 1e-30
CLIP = 0.25
RATE = 2.0
MASKED = -1e30


def for_sending(value):
    return jax.tree.map(lambda a: a.astype(jnp.bfloat16) if a.dtype == jnp.float32 else a, value)


def layer_norm(rows, gain, shift):
    centre = rows - jnp.mean(rows, axis=-1, keepdims=True)
    spread = jnp.mean(centre * centre, axis=-1, keepdims=True)
    return centre * lax.rsqrt(spread + 1e-06) * gain + shift


def norm_back(rows, gain, shift, grad):
    result, back = jax.vjp(layer_norm, rows, gain, shift)
    return back(grad)


def exact_gelu(values):
    return jax.nn.gelu(values, approximate=False)


def segments(counts, length):
    bounds = jnp.cumsum(counts)
    places = jnp.arange(length, dtype=jnp.int32)
    image = jnp.sum((places[:, None] >= bounds[None, :]).astype(jnp.int32), axis=1)
    live = (places < bounds[-1]).astype(jnp.float32)
    return (image[:, None] == image[None, :], live)


def attention_scores(query, keys, same):
    scale = query.shape[-1] ** (-0.5)
    scores = jnp.einsum("qhd,khd->hqk", query, keys, preferred_element_type=jnp.float32) * scale
    return jnp.where(same[None], scores, MASKED)


def attend(qkv, same):
    scores = attention_scores(qkv[:, 0], qkv[:, 1], same)
    top = jnp.max(scores, axis=-1, keepdims=True)
    raised = jnp.exp(scores - top)
    total = jnp.sum(raised, axis=-1, keepdims=True)
    probs = (raised / total).astype(jnp.bfloat16)
    mixed = jnp.einsum("hqk,khd->qhd", probs, qkv[:, 2], preferred_element_type=jnp.float32)
    return (mixed.reshape(mixed.shape[0], -1), top + jnp.log(total))


def attend_back(qkv, same, log_total, grad_mixed):
    query, keys, values = (qkv[:, 0], qkv[:, 1], qkv[:, 2])
    scale = query.shape[-1] ** (-0.5)
    probs = jnp.exp(attention_scores(query, keys, same) - log_total)
    d_values = jnp.einsum(
        "hqk,qhd->khd", probs.astype(jnp.bfloat16), grad_mixed, preferred_element_type=jnp.float32
    )
    d_probs = jnp.einsum("qhd,khd->hqk", grad_mixed, values, preferred_element_type=jnp.float32)
    d_scores = (probs * (d_probs - jnp.sum(probs * d_probs, axis=-1, keepdims=True))).astype(
        jnp.bfloat16
    )
    d_query = jnp.einsum("hqk,khd->qhd", d_scores, keys, preferred_element_type=jnp.float32) * scale
    d_keys = jnp.einsum("hqk,qhd->khd", d_scores, query, preferred_element_type=jnp.float32) * scale
    return jnp.stack([d_query, d_keys, d_values], axis=1).astype(jnp.bfloat16)


def spread_rows(values):
    return lax.all_gather(values, "mp", axis=0, tiled=True)


def size_of(name):
    return lax.axis_size("dp") if name == "dp" else lax.axis_size("mp")


TILE = 112
VMEM_BYTES = 64 << 20
GROUP = 384
PATHS = (((128, "zyx"), (256, "xzy")), ((128, "zxy"), (256, "yzx")))
BIG = 1e30
MESH = pl.DeviceIdType.MESH
F32 = jnp.float32
BF16 = jnp.bfloat16
NN = ((1,), (0,))
NT = ((1,), (1,))
PLANE = [(dy, dx, dc) for dy in range(2) for dx in range(2) for dc in range(2)][1:]


def dot(left, right, dims):
    return lax.dot_general(left, right, (dims, ((), ())), preferred_element_type=F32)


class Place:
    def __init__(self, n_dp):
        self.nz = n_dp // 4
        me = lax.axis_index("dp")
        self.core = lax.axis_index("mp")
        self.z, self.y, self.x = me // 4, (me // 2) % 2, me % 2

    def at(self, z, y, x, core):
        return (z * 4 + y * 2 + x, core)

    def over_x(self):
        return self.at(self.z, self.y, 1 - self.x, self.core)

    def over_y(self):
        return self.at(self.z, 1 - self.y, self.x, self.core)

    def over_z(self, step):
        return self.at((self.z + step) % self.nz, self.y, self.x, self.core)

    def over_core(self):
        return self.at(self.z, self.y, self.x, 1 - self.core)

    def near(self, dy, dx, dc):
        return self.at(self.z, (self.y + dy) % 2, (self.x + dx) % 2, (self.core + dc) % 2)

    def barrier(self):
        sem = pltpu.get_barrier_semaphore()
        others = [self.near(dy, dx, dc) for dy, dx, dc in PLANE]
        others += [self.over_z(step) for step in range(1, self.nz)]
        for other in others:
            pl.semaphore_signal(sem, inc=1, device_id=other, device_id_type=MESH)
        pl.semaphore_wait(sem, len(others))


class Sender:
    def __init__(self, send_sems, recv_sems):
        self.send_sems, self.recv_sems = send_sems, recv_sems
        self.count = 0
        self.sent = []

    def make(self, src, dst, device, number=None):
        at = self.count
        self.count += 1
        return pltpu.make_async_remote_copy(
            src_ref=src,
            dst_ref=dst,
            send_sem=self.send_sems.at[at],
            recv_sem=self.recv_sems.at[at if number is None else number],
            device_id=device,
            device_id_type=MESH,
        )

    def start(self, src, dst, device):
        copy = self.make(src, dst, device)
        copy.start()
        self.sent.append(copy)
        return copy

    def drain(self):
        for copy in self.sent:
            copy.wait_send()
        self.sent = []


def parts_of(layer, low, turn):
    parts = []
    for width, order in PATHS[turn % 2]:
        parts.append((layer, low, low + width, order))
        low += width
    return parts


class Links:
    def __init__(self, place, sender):
        self.p, self.sender = place, sender
        self.inner = jnp.logical_or(place.z == 1, place.z == 2)
        self.copies = {}
        self.only_inner, self.only_outer = [], []

    def over_z_bit(self, bit):
        return self.p.at(self.p.z ^ bit, self.p.y, self.p.x, self.p.core)

    def steps(self, order):
        return order.replace("z", "zf")

    def over(self, axis):
        return self.p.over_x() if axis == "x" else self.p.over_y()

    def drain(self):
        @pl.when(self.inner)
        def _():
            for copy in self.only_inner:
                copy.wait_send()

        @pl.when(jnp.logical_not(self.inner))
        def _():
            for copy in self.only_outer:
                copy.wait_send()


class Gather(Links):
    def __init__(self, place, sender, weights, groups):
        super().__init__(place, sender)
        self.weights, self.groups = weights, groups
        self.tick_at = 0

    def view(self, part, done, z=None):
        layer, low, high, order = part
        p = self.p
        at_z = slice(None) if "z" in done else (p.z if z is None else z)
        at_y = slice(None) if "y" in done else p.y
        at_x = slice(None) if "x" in done else p.x
        return self.weights[layer].at[at_z, at_y, at_x, :, low:high]

    def stage(self, part, at):
        steps = self.steps(part[3])
        axis, done = steps[at], steps[:at].replace("f", "")
        before = self.copies.get((part, at - 1), ())
        if axis == "f":
            near, far, third, number = before
            far.wait_recv()
            piece = self.view(part, done.replace("z", ""), self.p.z ^ 2)
            onward = self.sender.make(piece, piece, self.over_z_bit(1), number)

            @pl.when(self.inner)
            def _():
                onward.start()

            self.only_inner.append(onward)
            self.copies[part, at] = [near, third]
            return
        for copy in before:
            copy.wait_recv()
        piece = self.view(part, done)
        if axis == "z":
            near = self.sender.start(piece, piece, self.over_z_bit(1))
            far = self.sender.start(piece, piece, self.over_z_bit(2))
            number = self.sender.count
            third = self.sender.make(piece, piece, self.over_z_bit(3))

            @pl.when(self.inner)
            def _():
                third.start()

            self.only_inner.append(third)
            self.copies[part, at] = (near, far, third, number)
        else:
            self.copies[part, at] = [self.sender.start(piece, piece, self.over(axis))]

    def tick(self):
        t = self.tick_at
        self.tick_at += 1
        for at in range(4):
            if 0 <= t - at < len(self.groups):
                for part in self.groups[t - at]:
                    self.stage(part, at)

    def poll(self):
        if self.tick_at < len(self.groups) + 3:
            self.tick()

    def ready(self, k):
        while self.tick_at < min(k + 4 + 1, len(self.groups) + 3):
            self.tick()
        for part in self.groups[k]:
            for copy in self.copies.pop((part, 3), ()):
                copy.wait_recv()


class Rounds:
    def __init__(self, place, sender):
        self.p, self.sender = place, sender

    def plane(self, term, slots, cores=False):
        p = self.p
        at = p.y * 2 + p.x
        at = at * 2 + p.core if cores else at
        slots[at] = term[...]
        return [
            self.sender.start(term, slots.at[at], p.near(dy, dx, dc))
            for dy, dx, dc in PLANE
            if cores or not dc
        ]

    def along_z(self, term, slots):
        p = self.p
        slots[p.z] = term[...]
        return [self.sender.start(term, slots.at[p.z], p.over_z(step)) for step in range(1, p.nz)]


def slot_sum(copies, slots):
    for copy in copies:
        copy.wait_recv()
    total = slots[0]
    for at in range(1, slots.shape[0]):
        total = total + slots[at]
    return total


class Scatter(Links):
    def __init__(
        self, place, sender, grads, groups, buffers, result, cuts, by_row, by_column
    ):
        super().__init__(place, sender)
        self.grads, self.groups, self.buffers, self.result = grads, groups, buffers, result
        self.cuts, self.by_row, self.by_column = cuts, by_row, by_column
        self.started = 0
        self.tick_at = 0

    def view(self, part, done, z=None, y=None, x=None):
        layer, low, high, order = part
        p = self.p
        at_z = slice(None) if z is None and "z" not in done else (p.z if z is None else z)
        at_y = slice(None) if y is None and "y" not in done else (p.y if y is None else y)
        at_x = slice(None) if x is None and "x" not in done else (p.x if x is None else x)
        return self.grads[layer].at[at_z, at_y, at_x, :, low:high]

    def add(self, into, term):
        into[...] = (into[...].astype(F32) + term[...].astype(F32)).astype(BF16)

    def put(self, part, into, value, last):
        if last:
            layer, low, high, _ = part
            self.result[layer, :, low:high] = value
        else:
            into[...] = value.astype(BF16)

    def buffer(self, k, at, name):
        ref = self.buffers[self.groups[k][at][3]][name]
        return ref.at[(k // 2) % ref.shape[0]]

    def absorb(self, k, at, step):
        part = self.groups[k][at]
        steps = self.steps(part[3])
        if step == 0:
            return ""
        axis, done = steps[step - 1], steps[: step - 1].replace("f", "")
        copies = self.copies.pop((k, at, step - 1))
        last = step == len(steps)
        if axis in "xy":
            copies[0].wait_recv()
            total = self.view(part, done + axis)
            value = total[...].astype(F32) + self.buffer(k, at, axis)[...].astype(F32)
            self.put(part, total, value, last)
        elif axis == "f":
            near, far, third = copies
            done = done.replace("z", "")
            total = self.view(part, done + "z")
            slots = self.buffer(k, at, "z")
            near.wait_recv()
            far.wait_recv()
            value = total[...].astype(F32) + slots[0].astype(F32) + slots[1].astype(F32)
            self.put(part, total, value, last)

            @pl.when(self.inner)
            def _():
                third.wait_recv()
                self.put(part, total, value + slots[2].astype(F32), last)

            done = done + "z"
            return done
        return done + axis

    def stage(self, k, at, step):
        part = self.groups[k][at]
        steps = self.steps(part[3])
        p = self.p
        if step < len(steps) and steps[step] == "f":
            near, far, third, relay, far_number = self.copies.pop((k, at, step - 1))
            done = steps[: step - 1]
            slots = self.buffer(k, at, "z")
            piece = self.view(part, done, z=p.z ^ 2)
            onward = self.sender.make(piece, slots.at[1], self.over_z_bit(2), far_number)

            @pl.when(self.inner)
            def _():
                relay.wait_recv()
                self.add(piece, slots.at[3])
                onward.start()

            self.only_inner.append(onward)
            self.copies[k, at, step] = (near, far, third)
            return
        done = self.absorb(k, at, step)
        if step == len(steps):
            self.measure(part)
            return
        axis = steps[step]
        if axis == "z":
            slots = self.buffer(k, at, "z")
            near = self.sender.start(
                self.view(part, done, z=p.z ^ 1), slots.at[0], self.over_z_bit(1)
            )
            far_number = self.sender.count
            far = self.sender.make(
                self.view(part, done, z=p.z ^ 2), slots.at[1], self.over_z_bit(2)
            )
            across = self.view(part, done, z=p.z ^ 3)
            third = self.sender.make(across, slots.at[2], self.over_z_bit(3))
            relay = self.sender.make(across, slots.at[3], self.over_z_bit(1))

            @pl.when(self.inner)
            def _():
                third.start()

            @pl.when(jnp.logical_not(self.inner))
            def _():
                relay.start()
                far.start()

            self.only_inner.append(third)
            self.only_outer += [relay, far]
            self.copies[k, at, step] = (near, far, third, relay, far_number)
        else:
            flip = {axis: 1 - (p.x if axis == "x" else p.y)}
            self.copies[k, at, step] = [
                self.sender.start(
                    self.view(part, done, **flip), self.buffer(k, at, axis), self.over(axis)
                )
            ]

    def measure(self, part):
        layer, low, high, _ = part
        total = self.result[layer, :, low:high]
        squares = total * total + EPS_SQUARE
        self.by_column[layer][:, low:high] = jnp.sum(squares, axis=0, keepdims=True)
        lane = lax.broadcasted_iota(jnp.int32, (1, 128), 1)
        for which, (first, end) in enumerate(self.cuts):
            if first <= low < end:
                term = jnp.sum(squares, axis=1, keepdims=True)
                self.by_row[...] += jnp.where(lane == layer * 4 + which, term, 0.0)

    def poll(self):
        if self.tick_at < self.started - 1:
            self.tick()

    def start(self):
        for at in range(len(self.groups[self.started])):
            self.stage(self.started, at, 0)
        self.started += 1

    def tick(self):
        t = self.tick_at
        if t >= self.started + 3:
            return
        self.tick_at += 1
        for step in range(1, 5):
            k = t + 1 - step
            if 0 <= k < self.started:
                for at in range(len(self.groups[k])):
                    self.stage(k, at, step)

    def finish(self):
        while self.tick_at < len(self.groups) + 3:
            self.tick()


def row_tiles(length, body):
    def step(i, carry):
        body(pl.ds(pl.multiple_of(i * TILE, TILE), TILE))
        return carry

    lax.fori_loop(0, length // TILE, step, 0)


def normalised(rows):
    centre = rows - jnp.mean(rows, axis=-1, keepdims=True)
    spread = jnp.mean(centre * centre, axis=-1, keepdims=True)
    rise = lax.rsqrt(spread + 1e-06)
    return centre * rise, rise


def encode_segments(counts, slots, qe, ke):
    length = qe.shape[0]
    place = lax.broadcasted_iota(jnp.int32, (length, 128), 0)
    lane = lax.broadcasted_iota(jnp.int32, (length, 128), 1) % HEAD_DIM
    image = jnp.zeros((length, 128), jnp.int32)
    total = jnp.int32(0)
    for slot in range(slots):
        total = total + counts[slot]
        image = image + (place >= total).astype(jnp.int32)
    hit = image == lane
    ke[...] = jnp.where(hit, 1.0, 0.0).astype(BF16)
    qe[...] = jnp.where(jnp.logical_or(hit, lane > slots), 0.0, -BIG).astype(BF16)


def attention_forward(qkv, qe, ke, log_total, mixed, between):
    length, width = mixed.shape
    lane = lax.broadcasted_iota(jnp.int32, (length, 128), 1)

    def pair(at, carry):
        low = pl.multiple_of(at * 128, 128)
        query = qkv[:, pl.ds(low, 128)] * jnp.asarray(0.125, BF16)
        keys = qkv[:, pl.ds(width + low, 128)]
        values = qkv[:, pl.ds(2 * width + low, 128)].T
        outs = []
        for half in range(2):
            own = (lane < HEAD_DIM) if half == 0 else (lane >= HEAD_DIM)
            q = jnp.where(own, query, qe[...])
            k = jnp.where(own, keys, ke[...])
            scores = dot(k, q, NT)
            top = jnp.max(scores, axis=0, keepdims=True)
            raised = jnp.exp(scores - top)
            total = jnp.sum(raised, axis=0, keepdims=True)
            rows = slice(half * HEAD_DIM, (half + 1) * HEAD_DIM)
            outs.append(dot(values[rows], raised.astype(BF16), NN) / total)
            log_total[pl.ds(at * 2 + half, 1), :] = top + jnp.log(total)
        mixed[:, pl.ds(low, 128)] = jnp.concatenate(outs, axis=0).T.astype(BF16)
        return carry

    for at in range(width // 128):
        lax.fori_loop(at, at + 1, pair, 0)
        between()


def attention_backward(qkv, qe, ke, log_total, d_mixed, between):
    length, width = d_mixed.shape
    lane = lax.broadcasted_iota(jnp.int32, (length, 128), 1)

    def pair(at, carry):
        low = pl.multiple_of(at * 128, 128)
        query = qkv[:, pl.ds(low, 128)] * jnp.asarray(0.125, BF16)
        keys = qkv[:, pl.ds(width + low, 128)]
        values = qkv[:, pl.ds(2 * width + low, 128)]
        d_out = d_mixed[:, pl.ds(low, 128)]
        keys_t = keys.T
        d_query, d_keys, d_values = [], [], []
        for half in range(2):
            own = (lane < HEAD_DIM) if half == 0 else (lane >= HEAD_DIM)
            q = jnp.where(own, query, qe[...])
            k = jnp.where(own, keys, ke[...])
            v = jnp.where(own, values, jnp.zeros_like(values))
            probs = jnp.exp(dot(k, q, NT) - log_total[pl.ds(at * 2 + half, 1), :])
            d_probs = dot(v, d_out, NT)
            mean = jnp.sum(probs * d_probs, axis=0, keepdims=True)
            d_scores = (probs * (d_probs - mean)).astype(BF16)
            d_values.append(dot(probs.astype(BF16), d_out, NN))
            d_keys.append(dot(d_scores, query, NN))
            rows = slice(half * HEAD_DIM, (half + 1) * HEAD_DIM)
            d_query.append(dot(keys_t[rows], d_scores, NN))
        first = lane < HEAD_DIM
        d_q = jnp.concatenate(d_query, axis=0).T * 0.125
        qkv[:, pl.ds(low, 128)] = d_q.astype(BF16)
        qkv[:, pl.ds(width + low, 128)] = jnp.where(first, *d_keys).astype(BF16)
        qkv[:, pl.ds(2 * width + low, 128)] = jnp.where(first, *d_values).astype(BF16)
        return carry

    for at in range(width // 128):
        lax.fori_loop(at, at + 1, pair, 0)
        between()


class Exchange:
    def __init__(self, place, sender, out, into):
        self.p, self.sender, self.out, self.into = place, sender, out, into
        self.turn = 0
        self.copies = {}
        length = out.shape[1]
        cut = (length // TILE + 1) // 2 * TILE
        self.chunks = ((0, cut), (cut, length))

    def send(self, compute):
        slot = self.turn % 2
        for copy in self.copies.get(slot, ()):
            copy.wait_send()
            self.sender.sent = [item for item in self.sender.sent if item is not copy]
        self.copies[slot] = []
        for low, high in self.chunks:
            self.out[slot, low:high, :] = compute(low, high).astype(BF16)
            piece = self.out.at[slot, low:high, :]
            self.copies[slot].append(
                self.sender.start(piece, self.into.at[slot, low:high, :], self.p.over_core())
            )

    def swap_halves(self, compute, body):
        slot = self.turn % 2
        for copy in self.copies.get(slot, ()):
            copy.wait_send()
            self.sender.sent = [item for item in self.sender.sent if item is not copy]
        length = self.out.shape[1]
        count = (length // TILE + 1) // 2 * TILE
        first = (length // 2 // TILE) * TILE
        core = self.p.core
        theirs = pl.ds(pl.multiple_of((1 - core) * first, TILE), count)
        self.out[slot, theirs, :] = compute(theirs).astype(BF16)
        copy = self.sender.start(
            self.out.at[slot, theirs, :], self.into.at[slot, theirs, :], self.p.over_core()
        )
        mine = pl.ds(pl.multiple_of(core * first, TILE), count)
        own = compute(mine).astype(BF16).astype(F32)
        copy.wait_recv()
        body(mine, own + self.into[slot, mine, :].astype(F32))

    def take(self, body):
        slot = self.turn % 2
        self.turn += 1
        for (low, high), copy in zip(self.chunks, self.copies[slot]):
            copy.wait_recv()

            def step(i, carry, low=low):
                rows = pl.ds(pl.multiple_of(low + i * TILE, TILE), TILE)
                total = self.out[slot, rows, :].astype(F32) + self.into[slot, rows, :].astype(F32)
                body(rows, total)
                return carry

            lax.fori_loop(0, (high - low) // TILE, step, 0)


def grand_total(value):
    return jnp.sum(jnp.sum(value, axis=1, keepdims=True), axis=0, keepdims=True)


def flat(w, low, high):
    value = w[:, :, :, :, low:high]
    return value.reshape(-1, high - low)


def gelu_and_slope(hidden):
    cdf = 0.5 * (1.0 + lax.erf(hidden * (0.5**0.5)))
    slope = cdf + hidden * (jnp.exp(-0.5 * hidden * hidden) * 0.3989422804014327)
    return hidden * cdf, slope


def forward_kernel(
    n_dp, cuts, slots,
    counts, patches, qkv_w, out_w, up_w, down_w, norms,
    o_weights, o_rows, o_middle, o_normed_a, o_qkv, o_mixed, o_normed_b, o_active, o_slope, o_log,
    o_result, o_squares,
    w0, w1, rows, middle, normed_a, qkv, mixed, normed_b, active, slope, log_total, final,
    x_out, x_in, qe, ke, send_sems, recv_sems, local_sems,
):
    layers, half = 2, patches.shape[0]
    length = 2 * half
    c_qkv, c_out, c_up, c_down = cuts
    p = Place(n_dp)
    sender = Sender(send_sems, recv_sems)
    local = []

    def move(src, dst):
        copy = pltpu.make_async_copy(src, dst, local_sems.at[len(local)])
        copy.start()
        local.append(copy)
        return copy

    weights = (w0, w1)
    local_heads = qkv_w.shape[3]

    def master(layer, which):
        if which == 0:
            return [qkv_w[layer, part] for part in range(3)]
        return [(out_w, up_w, down_w)[which - 1][layer]]

    def place_pieces(layer):
        for which, (low, _) in enumerate(cuts):
            for part, value in enumerate(master(layer, which)):
                cols = slice(low + part * local_heads, low + part * local_heads + value.shape[1])
                weights[layer][p.z, p.y, p.x, :, cols] = value.astype(BF16)

    place_pieces(0)
    p.barrier()
    starts = [(l, low) for l in range(layers) for low in range(0, c_down[1], GROUP)]
    groups = [parts_of(l, low, turn) for turn, (l, low) in enumerate(starts)]
    per = len(groups) // layers
    gather = Gather(p, sender, weights, groups)
    gather.tick()
    own_rows = pl.ds(pl.multiple_of(p.core * half, half), half)
    rows[0, own_rows, :] = patches[...].astype(F32)
    swap = sender.start(rows.at[0, own_rows, :], rows.at[0, own_rows, :], p.over_core())
    place_pieces(1)
    gather.tick()
    encode_segments(counts, slots, qe, ke)
    gather.tick()
    swap.wait_recv()
    exchange = Exchange(p, sender, x_out, x_in)

    def norm_into(target, layer, which, at, value):
        hat, _ = normalised(value)
        gain, shift = norms[layer, which : which + 1, :], norms[layer, which + 1 : which + 2, :]
        target[layer, at, :] = (hat * gain + shift).astype(BF16)

    row_tiles(length, lambda at: norm_into(normed_a, 0, 0, at, rows[0, at, :]))
    saves = [(rows, o_rows, 0), (normed_a, o_normed_a, 0)]

    def save(*items):
        for src, dst, layer in items:
            move(src.at[layer], dst.at[layer])

    save(*saves)
    for layer in range(layers):
        w, base = weights[layer], per * layer
        for k in range(c_qkv[1] // GROUP):
            gather.ready(base + k)
            cols = slice(k * GROUP, (k + 1) * GROUP)
            value = dot(normed_a[layer], flat(w, cols.start, cols.stop), NN)
            qkv[layer, :, cols] = value.astype(BF16)
        attention_forward(
            qkv.at[layer], qe, ke, log_total.at[layer], mixed.at[layer], gather.poll
        )
        save((qkv, o_qkv, layer), (log_total, o_log, layer), (mixed, o_mixed, layer))
        gather.ready(base + c_out[0] // GROUP)
        w_out = flat(w, *c_out)
        exchange.send(lambda low, high: dot(mixed[layer, low:high, :], w_out, NT))
        gather.poll()

        def mid_step(at, total):
            value = rows[layer, at, :] + total
            middle[layer, at, :] = value
            norm_into(normed_b, layer, 2, at, value)

        exchange.take(mid_step)
        save((middle, o_middle, layer), (normed_b, o_normed_b, layer))
        for k in range(c_up[0] // GROUP, c_up[1] // GROUP):
            gather.ready(base + k)
            low = k * GROUP
            cols = slice(low - c_up[0], low - c_up[0] + GROUP)
            hidden = dot(normed_b[layer], flat(w, low, low + GROUP), NN)
            act, rise = gelu_and_slope(hidden)
            active[layer, :, cols] = act.astype(BF16)
            slope[layer, :, cols] = rise.astype(BF16)
        save((active, o_active, layer), (slope, o_slope, layer))
        for k in range(c_down[0] // GROUP, c_down[1] // GROUP - 1):
            gather.ready(base + k)
            low = k * GROUP
            cols = slice(low - c_down[0], low - c_down[0] + GROUP)
            term = dot(active[layer, :, cols], flat(w, low, low + GROUP), NT)
            if k * GROUP == c_down[0]:
                final[...] = term
            else:
                final[...] += term
        gather.ready(base + c_down[1] // GROUP - 1)
        w_down = flat(w, c_down[1] - GROUP, c_down[1])
        cols = slice(c_down[1] - c_down[0] - GROUP, c_down[1] - c_down[0])
        if layer + 1 < layers:
            exchange.send(
                lambda low, high: final[low:high, :]
                + dot(active[layer, low:high, cols], w_down, NT)
            )
            move(w, o_weights.at[layer])
            gather.poll()

            def next_step(at, total):
                value = middle[layer, at, :] + total
                rows[layer + 1, at, :] = value
                norm_into(normed_a, layer + 1, 0, at, value)

            exchange.take(next_step)
            save((rows, o_rows, layer + 1), (normed_a, o_normed_a, layer + 1))
        else:
            move(w, o_weights.at[layer])

            def last_step(at, total):
                final[at, :] = middle[layer, at, :] + total

            exchange.swap_halves(
                lambda at: final[at, :] + dot(active[layer, at, cols], w_down, NT), last_step
            )
    o_result[...] = final[own_rows, :].astype(BF16)
    sender.drain()
    gather.drain()
    lane = lax.broadcasted_iota(jnp.int32, (1, 128), 1)
    squares = jnp.zeros((1, 128), F32)
    for layer in range(layers):
        for which in range(4):
            total = sum(grand_total(value * value) for value in master(layer, which))
            squares = squares + jnp.where(lane == layer * 4 + which, total, 0.0)
    o_squares[...] = squares
    for copy in local:
        copy.wait()


def backward_kernel(
    n_dp, cuts, totals, slots,
    counts, cotangent, norms, squares, row_states, qkv_c, out_c, up_c, down_c, norm_state,
    i_weights, i_rows, i_middle, i_normed_a, i_qkv, i_mixed, i_normed_b, i_active, i_slope, i_log,
    o_input, o_pieces, o_rows, o_columns, o_scalars, o_steps, o_own,
    g0, g1, buffers,
    w, kept, normed_a, qkv, mixed, normed_b, active, slope, log_total,
    grad, rounded, turned, x_out, x_in, qe, ke, by_row, row_in, square, tall, small, few, last,
    send_sems, recv_sems, local_sems,
):
    layers, half = 2, cotangent.shape[0]
    length = 2 * half
    c_qkv, c_out, c_up, c_down = cuts
    p = Place(n_dp)
    sender = Sender(send_sems, recv_sems)
    count = [0]

    def load(src, dst):
        copy = pltpu.make_async_copy(src, dst, local_sems.at[count[0]])
        count[0] += 1
        copy.start()
        return copy

    def load_mlp(l):
        cols = slice(c_up[0], c_down[1])
        return dict(
            active=load(i_active.at[l], active),
            slope=load(i_slope.at[l], slope),
            weights=load(i_weights.at[l, :, :, :, :, cols], w.at[:, :, :, :, cols]),
            normed_b=load(i_normed_b.at[l], normed_b),
        )

    def load_attention(l):
        cols = slice(c_qkv[0], c_out[1])
        return dict(
            mixed=load(i_mixed.at[l], mixed),
            weights=load(i_weights.at[l, :, :, :, :, cols], w.at[:, :, :, :, cols]),
            qkv=load(i_qkv.at[l], qkv),
            log=load(i_log.at[l], log_total),
            normed_a=load(i_normed_a.at[l], normed_a),
        )

    mlp = load_mlp(layers - 1)
    mlp["middle"] = load(i_middle.at[layers - 1], kept)
    att = load_attention(layers - 1)
    p.barrier()
    own_rows = pl.ds(pl.multiple_of(p.core * half, half), half)
    total = jnp.int32(0)
    for slot in range(slots):
        total = total + counts[slot]
    place = lax.broadcasted_iota(jnp.int32, (half, 1), 0) + p.core * half
    grad[own_rows, :] = jnp.where(place < total, cotangent[...].astype(F32), 0.0)
    swap = sender.start(grad.at[own_rows, :], grad.at[own_rows, :], p.over_core())
    encode_segments(counts, slots, qe, ke)
    norm_sums = [small[layer][4] for layer in range(layers)]
    by_row[...] = jnp.zeros_like(by_row)
    for sums in norm_sums:
        sums[...] = jnp.zeros_like(sums)
    exchange = Exchange(p, sender, x_out, x_in)
    grads = (g0, g1)
    starts = list(range(c_down[0], c_down[1], GROUP)) + list(range(c_up[0], c_up[1], GROUP))
    starts += list(range(c_out[0], c_out[1], GROUP)) + list(range(c_qkv[0], c_qkv[1], GROUP))
    starts = [(l, low) for l in reversed(range(layers)) for low in starts]
    groups = [
        [(layer, a, b, order[::-1]) for layer, a, b, order in parts_of(l, low, turn)]
        for turn, (l, low) in enumerate(starts)
    ]
    columns_of_layer = [small[layer][0] for layer in range(layers)]
    scatter = Scatter(
        p, sender, grads, groups, buffers, o_pieces, cuts, by_row, columns_of_layer
    )
    swap.wait_recv()
    sender.drain()

    def store(layer, low, value):
        g = grads[layer]
        shape = g.shape[:4] + (value.shape[1],)
        g[:, :, :, :, low : low + value.shape[1]] = value.astype(BF16).reshape(shape)

    def norm_step(layer, which, at, total):
        hat, rise = normalised(kept[at, :])
        norm_sums[layer][which : which + 1, :] += jnp.sum(total * hat, axis=0, keepdims=True)
        norm_sums[layer][which + 1 : which + 2, :] += jnp.sum(total, axis=0, keepdims=True)
        d_hat = total * norms[layer, which : which + 1, :]
        flat_mean = jnp.mean(d_hat, axis=-1, keepdims=True)
        hat_mean = jnp.mean(d_hat * hat, axis=-1, keepdims=True)
        value = grad[at, :] + rise * (d_hat - flat_mean - hat * hat_mean)
        grad[at, :] = value
        rounded[at, :] = value.astype(BF16)

    def round_step(at):
        rounded[at, :] = grad[at, :].astype(BF16)

    row_tiles(length, round_step)
    for layer in reversed(range(layers)):
        turned[...] = rounded[...].T
        mlp["active"].wait()
        for low in range(c_down[0], c_down[1], GROUP):
            cols = slice(low - c_down[0], low - c_down[0] + GROUP)
            store(layer, low, dot(turned[...], active[:, cols], NN))
            scatter.start()
        scatter.poll()
        mlp["weights"].wait()
        mlp["slope"].wait()
        for low in range(c_down[0], c_down[1], GROUP):
            cols = slice(low - c_down[0], low - c_down[0] + GROUP)
            d_active = dot(rounded[...], flat(w, low, low + GROUP), NN)
            slope[:, cols] = (d_active * slope[:, cols].astype(F32)).astype(BF16)
        scatter.poll()
        mlp["normed_b"].wait()
        turned[...] = normed_b[...].T
        for low in range(c_up[0], c_up[1], GROUP):
            cols = slice(low - c_up[0], low - c_up[0] + GROUP)
            store(layer, low, dot(turned[...], slope[:, cols], NN))
            scatter.start()
        scatter.poll()
        w_up = flat(w, *c_up)
        exchange.send(lambda low, high: dot(slope[low:high, :], w_up, NT))
        scatter.poll()
        mlp["middle"].wait()
        exchange.take(lambda at, total: norm_step(layer, 2, at, total))
        rows_load = load(i_rows.at[layer], kept)
        if layer:
            mlp = load_mlp(layer - 1)
        scatter.poll()
        turned[...] = rounded[...].T
        att["mixed"].wait()
        store(layer, c_out[0], dot(turned[...], mixed[...], NN))
        scatter.start()
        att["weights"].wait()
        mixed[...] = dot(rounded[...], flat(w, *c_out), NN).astype(BF16)
        scatter.poll()
        att["qkv"].wait()
        att["log"].wait()
        attention_backward(qkv, qe, ke, log_total, mixed, scatter.poll)
        att["normed_a"].wait()
        turned[...] = normed_a[...].T
        for low in range(c_qkv[0], c_qkv[1], GROUP):
            store(layer, low, dot(turned[...], qkv[:, low : low + GROUP], NN))
            scatter.start()
        scatter.poll()
        w_qkv = flat(w, *c_qkv)
        exchange.send(lambda low, high: dot(qkv[low:high, :], w_qkv, NT))
        scatter.poll()
        rows_load.wait()
        exchange.take(lambda at, total: norm_step(layer, 0, at, total))
        if layer:
            mlp["middle"] = load(i_middle.at[layer - 1], kept)
            att = load_attention(layer - 1)
        scatter.poll()
    o_input[...] = grad[own_rows, :]
    rounds = Rounds(p, sender)
    in_plane, in_z = {}, {}

    def small_plane(layer):
        col, _, col_plane, _, norm, _, norm_plane, _ = small[layer]
        in_plane[layer] = (rounds.plane(col, col_plane), rounds.plane(norm, norm_plane))

    def small_z(layer):
        _, col, col_plane, col_z, _, norm, norm_plane, norm_z = small[layer]
        col[...] = slot_sum(in_plane[layer][0], col_plane)
        first = rounds.along_z(col, col_z)
        norm[...] = slot_sum(in_plane[layer][1], norm_plane)
        in_z[layer] = (first, rounds.along_z(norm, norm_z))

    while scatter.tick_at < len(groups) + 3:
        scatter.tick()
        if scatter.tick_at == len(groups) + 1:
            small_plane(1)
        if scatter.tick_at == len(groups) + 2:
            small_z(1)
    scatter.drain()
    small_plane(0)
    lane = lax.broadcasted_iota(jnp.int32, (1, 128), 1)
    entries = [(layer, which) for layer in range(layers) for which in range(4)]
    columns_of = (None, out_c, up_c, down_c)

    def old_columns(layer, which):
        if which == 0:
            return jnp.concatenate([qkv_c[part, layer : layer + 1, :] for part in range(3)], axis=1)
        return columns_of[which][layer : layer + 1, :]

    swap = sender.start(by_row, row_in, p.over_core())
    square[...] = jnp.zeros_like(square)
    olds = jnp.zeros((1, 128), F32)
    for at, (layer, which) in enumerate(entries):
        old = row_states[which][layer : layer + 1, :]
        square[at : at + 1, 0 : old.shape[1]] = old
        share = 0.5
        if which % 2:
            old, share = old_columns(layer, which), 1.0 / n_dp
        olds = olds + jnp.where(lane == 16 + at, jnp.sum(old, axis=1, keepdims=True) * share, 0.0)
    depth = o_pieces.shape[1]
    width = norm_state.shape[2]
    few_term, few_mid, few_plane, few_z = few
    sums = jnp.sum(by_row[...], axis=0, keepdims=True) + olds + pltpu.roll(squares[...], 8, 1)
    few_term[...] = jnp.broadcast_to(sums, few_term.shape)
    few_plane_copies = rounds.plane(few_term, few_plane, True)
    old_rows = square[...].T[0:depth, :]
    small_z(0)
    few_mid[...] = slot_sum(few_plane_copies, few_plane)
    few_z_copies = rounds.along_z(few_mid, few_z)
    swap.wait_recv()
    counts_of = jnp.ones((1, 128), F32)
    for at, (layer, which) in enumerate(entries):
        counts_of = jnp.where(lane == at, 1.0 / totals[which], counts_of)
    new_rows = DECAY * old_rows + (1.0 - DECAY) * (by_row[...] + row_in[...]) * counts_of
    square[...] = jnp.zeros_like(square)
    square[0:depth, :] = new_rows
    o_rows[...] = square[...].T
    by_row_rise = lax.rsqrt(new_rows)
    columns = []
    for layer in range(layers):
        columns.append(slot_sum(in_z[layer][0], small[layer][3]))
    norm_totals = [slot_sum(in_z[layer][1], small[layer][7]) for layer in range(layers)]
    scalars = slot_sum(few_z_copies, few_z)[0:1, :]
    o_scalars[...] = scalars
    steps = jnp.zeros((1, 128), F32)
    for at, (layer, which) in enumerate(entries):
        low, high = cuts[which]
        fresh = columns[layer][:, low:high]
        new_cols = DECAY * old_columns(layer, which) + (1.0 - DECAY) / D * fresh
        o_columns[layer, :, low:high] = new_cols
        mean = row_mean(scalars, at, which, totals)
        by_col = lax.rsqrt(new_cols)
        step = o_pieces[layer, :, low:high] * by_row_rise[:, at : at + 1] * by_col
        steps = steps + jnp.where(lane == at, grand_total(step * step) * mean, 0.0)
    both = norm_totals + [norms[layer] for layer in range(layers)]
    both.append(jnp.zeros((128 - 16, D), F32))
    tall[...] = jnp.concatenate(both, axis=0).T
    me = p.z * 4 + p.y * 2 + p.x
    square[0:depth, :] = tall[pl.ds(pl.multiple_of(me * depth, 8), depth), :]
    o_own[...] = square[...].T
    for layer in range(layers):
        mine = o_own[layer * 4 : layer * 4 + 4, 0:width]
        state = DECAY * norm_state[layer] + (1.0 - DECAY) * (mine * mine + EPS_SQUARE)
        sizes = jnp.sum(mine * mine / state, axis=1, keepdims=True) * 0.5
        for kind in range(4):
            steps = steps + jnp.where(lane == 8 + layer * 4 + kind, sizes[kind : kind + 1], 0.0)
    last_term, last_mid, last_plane, last_z = last
    last_term[...] = jnp.broadcast_to(steps, last_term.shape)
    last_copies = rounds.plane(last_term, last_plane, True)
    last_mid[...] = slot_sum(last_copies, last_plane)
    last_copies = rounds.along_z(last_mid, last_z)
    o_steps[...] = slot_sum(last_copies, last_z)[0:1, :]
    sender.drain()


def row_mean(scalars, at, which, totals):
    count = totals[3] if which == 3 else D
    mean = DECAY * scalars[:, 16 + at : 17 + at] / count
    return mean + (1.0 - DECAY) * scalars[:, at : at + 1] / (D * totals[which])


def apply_kernel(
    cuts, totals,
    result, grad, sums, rows, columns, scalars, steps, own, qkv_w, out_w, up_w, down_w, norms,
    norm_state,
    o_result, o_grad, g_qkv, g_out, g_up, g_down, g_norm, n_qkv, n_out, n_up, n_down, n_norm,
    k_qkv, k_out, k_up, k_down,
    qkv_rn, qkv_cn, out_rn, out_cn, up_rn, up_cn, down_rn, down_cn, moments_a, moments_f, rms,
    square,
):
    layers, depth = sums.shape[0], sums.shape[1]
    width, local = norm_state.shape[2], qkv_w.shape[3]
    o_result[...] = result[...]
    o_grad[...] = grad[...]
    lane = lax.broadcasted_iota(jnp.int32, (1, 128), 1)
    entries = [(layer, which) for layer in range(layers) for which in range(4)]
    means = jnp.ones((1, 128), F32)
    for at, (layer, which) in enumerate(entries):
        means = jnp.where(lane == at, 1.0 / (D * totals[which]), means)
        means = jnp.where(lane == 8 + at, 1.0 / D, means)
    size = jnp.sqrt(steps[...] * means)
    shrink = 1.0 / jnp.maximum(1.0, size / CLIP)
    row_news = (qkv_rn, out_cn, up_rn, down_cn)
    square[...] = rows[...].T
    by_row = lax.rsqrt(square[0:depth, :])
    for layer in range(layers):
        rms[layer : layer + 1, 0:4] = size[:, layer * 4 : layer * 4 + 4]
        rms[layer : layer + 1, 4:8] = size[:, 8 + layer * 4 : 12 + layer * 4]
        vectors = norms[layer]
        scale = jnp.sqrt(jnp.mean(vectors * vectors, axis=1, keepdims=True) + 1e-06)
        shrinks = jnp.concatenate(
            [shrink[:, 8 + layer * 4 + kind : 9 + layer * 4 + kind] for kind in range(4)], axis=0
        )
        mine = own[layer * 4 : layer * 4 + 4, 0:width]
        state = DECAY * norm_state[layer] + (1.0 - DECAY) * (mine * mine + EPS_SQUARE)
        g_norm[layer] = mine
        moments_a[layer] = state[0:2]
        moments_f[layer] = state[2:4]
        before = own[8 + layer * 4 : 12 + layer * 4, 0:width]
        n_norm[layer] = before - RATE * scale * (mine * lax.rsqrt(state) * shrinks)
    for at, (layer, which) in enumerate(entries):
        row_news[which][layer : layer + 1, :] = rows[at : at + 1, 0:depth]
        scale = jnp.sqrt(scalars[:, 8 + at : 9 + at] / (D * totals[which]) + 1e-06)
        factor = RATE * scale * shrink[:, at : at + 1]
        factor = factor * jnp.sqrt(row_mean(scalars[...], at, which, totals))
        factor = factor * by_row[:, at : at + 1]
        for part in range(3 if which == 0 else 1):
            low, high = cuts[which]
            if which == 0:
                low, high = part * local, part * local + local
                refs = [ref.at[layer, part] for ref in (qkv_w, g_qkv, n_qkv, k_qkv)]
                qkv_cn[part, layer : layer + 1, :] = columns[layer, :, low:high]
            else:
                table = (
                    (out_w, g_out, n_out, k_out),
                    (up_w, g_up, n_up, k_up),
                    (down_w, g_down, n_down, k_down),
                )
                refs = [ref.at[layer] for ref in table[which - 1]]
                new_ref = (out_rn, up_cn, down_rn)[which - 1]
                new_ref[layer : layer + 1, :] = columns[layer, :, low:high]
            grad_piece = sums[layer, :, low:high]
            new = refs[0][...] - grad_piece * factor * lax.rsqrt(columns[layer, :, low:high])
            refs[1][...] = grad_piece
            refs[2][...] = new
            refs[3][...] = new.astype(BF16)


def passes_by_xla(
    patches,
    cotangent,
    patch_counts,
    qkv_weight,
    out_weight,
    up_weight,
    down_weight,
    norms,
):
    layers = qkv_weight.shape[0]
    half = patches.shape[0]
    length = half * lax.axis_size("mp")
    same, live_all = segments(patch_counts, length)
    live = lax.dynamic_slice_in_dim(live_all, lax.axis_index("mp") * half, half)
    rows = patches.astype(jnp.float32)
    kept = []
    for layer in range(layers):
        pieces = (
            qkv_weight[layer].astype(jnp.bfloat16),
            out_weight[layer].astype(jnp.bfloat16),
            up_weight[layer].astype(jnp.bfloat16),
            down_weight[layer].astype(jnp.bfloat16),
        )
        whole = (
            lax.all_gather(pieces[0], "dp", axis=0, tiled=True),
            lax.all_gather(pieces[1], "dp", axis=1, tiled=True),
            lax.all_gather(pieces[2], "dp", axis=0, tiled=True),
            lax.all_gather(pieces[3], "dp", axis=1, tiled=True),
        )
        w_qkv, w_out, w_up, w_down = whole
        local = w_qkv.shape[2]
        normed_a = spread_rows(
            layer_norm(rows, norms[layer, 0], norms[layer, 1]).astype(jnp.bfloat16)
        )
        qkv = jnp.dot(normed_a, w_qkv.reshape(D, 3 * local), preferred_element_type=jnp.float32)
        qkv = qkv.astype(jnp.bfloat16).reshape(length, 3, local // HEAD_DIM, HEAD_DIM)
        mixed, log_total = attend(qkv, same)
        mixed = mixed.astype(jnp.bfloat16)
        middle = rows + lax.psum_scatter(
            jnp.dot(mixed, w_out, preferred_element_type=jnp.float32).astype(jnp.bfloat16),
            "mp",
            scatter_dimension=0,
            tiled=True,
        ).astype(jnp.float32)
        normed_b = spread_rows(
            layer_norm(middle, norms[layer, 2], norms[layer, 3]).astype(jnp.bfloat16)
        )
        hidden = jnp.dot(normed_b, w_up, preferred_element_type=jnp.float32)
        active = exact_gelu(hidden).astype(jnp.bfloat16)
        after = middle + lax.psum_scatter(
            jnp.dot(active, w_down, preferred_element_type=jnp.float32).astype(jnp.bfloat16),
            "mp",
            scatter_dimension=0,
            tiled=True,
        ).astype(jnp.float32)
        stored = None
        kept.append(
            (
                rows,
                normed_a,
                qkv,
                log_total,
                mixed,
                middle,
                normed_b,
                hidden,
                active,
                stored,
                pieces,
            )
        )
        rows = after
    activations = rows.astype(jnp.bfloat16)
    grad = cotangent.astype(jnp.float32) * live[:, None]
    reduced = [None] * layers
    for layer in reversed(range(layers)):
        (
            rows_in,
            normed_a,
            qkv,
            log_total,
            mixed,
            middle,
            normed_b,
            hidden,
            active,
            stored,
            pieces,
        ) = kept[layer]
        whole = (
            lax.all_gather(pieces[0], "dp", axis=0, tiled=True),
            lax.all_gather(pieces[1], "dp", axis=1, tiled=True),
            lax.all_gather(pieces[2], "dp", axis=0, tiled=True),
            lax.all_gather(pieces[3], "dp", axis=1, tiled=True),
        )
        w_qkv, w_out, w_up, w_down = whole
        local = w_qkv.shape[2]
        grad_down = spread_rows(grad.astype(jnp.bfloat16))
        g_down = jnp.einsum("tf,td->fd", active, grad_down, preferred_element_type=jnp.float32)
        d_active = jnp.einsum("td,fd->tf", grad_down, w_down, preferred_element_type=jnp.float32)
        gelu_value, gelu_back = jax.vjp(exact_gelu, hidden)
        d_hidden = gelu_back(d_active)[0].astype(jnp.bfloat16)
        g_up = jnp.einsum("td,tf->df", normed_b, d_hidden, preferred_element_type=jnp.float32)
        d_normed_b = lax.psum_scatter(
            jnp.einsum("tf,df->td", d_hidden, w_up, preferred_element_type=jnp.float32).astype(
                jnp.bfloat16
            ),
            "mp",
            scatter_dimension=0,
            tiled=True,
        ).astype(jnp.float32)
        d_middle, g_gain_b, g_shift_b = norm_back(
            middle, norms[layer, 2], norms[layer, 3], d_normed_b
        )
        grad_mid = grad + d_middle
        grad_out = spread_rows(grad_mid.astype(jnp.bfloat16))
        g_out = jnp.einsum("tc,td->cd", mixed, grad_out, preferred_element_type=jnp.float32)
        d_mixed = jnp.einsum(
            "td,cd->tc", grad_out, w_out, preferred_element_type=jnp.float32
        ).astype(jnp.bfloat16)
        d_qkv = attend_back(
            qkv, same, log_total, d_mixed.reshape(length, local // HEAD_DIM, HEAD_DIM)
        )
        d_qkv = d_qkv.reshape(length, 3 * local)
        g_qkv = jnp.einsum(
            "td,tc->dc", normed_a, d_qkv, preferred_element_type=jnp.float32
        ).reshape(D, 3, local)
        d_normed_a = lax.psum_scatter(
            jnp.einsum(
                "tc,dc->td", d_qkv, w_qkv.reshape(D, 3 * local), preferred_element_type=jnp.float32
            ).astype(jnp.bfloat16),
            "mp",
            scatter_dimension=0,
            tiled=True,
        ).astype(jnp.float32)
        d_input, g_gain_a, g_shift_a = norm_back(
            rows_in, norms[layer, 0], norms[layer, 1], d_normed_a
        )
        grad = grad_mid + d_input
        norm_terms = jnp.stack([g_gain_a, g_shift_a, g_gain_b, g_shift_b])
        reduced[layer] = (
            lax.psum_scatter(g_qkv, "dp", scatter_dimension=0, tiled=True),
            lax.psum_scatter(g_out, "dp", scatter_dimension=1, tiled=True),
            lax.psum_scatter(g_up, "dp", scatter_dimension=0, tiled=True),
            lax.psum_scatter(g_down, "dp", scatter_dimension=1, tiled=True),
            lax.psum(norm_terms, "mp"),
        )
    return activations, grad, [item[:4] for item in reduced], jnp.stack([item[4] for item in reduced])


def step_by_kernels(
    patches,
    cotangent,
    patch_counts,
    qkv_weight,
    out_weight,
    up_weight,
    down_weight,
    norms,
    qkv_rows,
    qkv_cols,
    out_rows,
    out_cols,
    up_rows,
    up_cols,
    down_rows,
    down_cols,
    norm_state,
):
    layers, depth, _, local = qkv_weight.shape
    n_dp = lax.axis_size("dp")
    nz, half, wide = n_dp // 4, patches.shape[0], up_weight.shape[2]
    length, slots = 2 * half, patch_counts.shape[0]
    ends = [0, 3 * local, 4 * local, 4 * local + wide, 4 * local + 2 * wide]
    cuts = tuple(zip(ends[:-1], ends[1:]))
    totals = tuple(2.0 * (high - low) for low, high in cuts)
    columns, n_groups = ends[-1], layers * ends[-1] // GROUP
    masters = (
        qkv_weight.transpose(0, 2, 1, 3),
        out_weight.transpose(0, 2, 1),
        up_weight,
        down_weight.transpose(0, 2, 1),
    )
    states_by_row = (qkv_rows, out_cols, up_rows, down_cols)
    states_by_column = (qkv_cols.transpose(1, 0, 2), out_rows, up_cols, down_rows)
    vmem, smem, hbm = [
        pl.BlockSpec(memory_space=space) for space in (pltpu.VMEM, pltpu.SMEM, pl.ANY)
    ]
    shape = jax.ShapeDtypeStruct
    whole = (nz, 2, 2, depth, columns)
    rows_f32, rows_bf16 = ((length, D), F32), ((length, D), BF16)
    kept = [
        rows_f32,
        rows_f32,
        rows_bf16,
        ((length, 3 * local), BF16),
        ((length, local), BF16),
        rows_bf16,
        ((length, wide), BF16),
        ((length, wide), BF16),
        ((8, length), F32),
    ]
    saved = [shape((layers,) + dims, kind) for dims, kind in kept]
    line = shape((1, 128), F32)
    sems = [
        pltpu.SemaphoreType.DMA((420,)),
        pltpu.SemaphoreType.DMA((420,)),
        pltpu.SemaphoreType.DMA((32,)),
    ]
    codes = [pltpu.VMEM((length, 128), BF16)] * 2
    swaps = [pltpu.VMEM((2, length, D), BF16)] * 2

    def around(dims, plane):
        return [pltpu.VMEM(dims, F32)] * 2 + [
            pltpu.VMEM((places,) + dims, F32) for places in (plane, nz)
        ]

    outs = pl.pallas_call(
        functools.partial(forward_kernel, n_dp, cuts, slots),
        out_shape=[shape((layers,) + whole, BF16)] + saved + [shape((half, D), BF16), line],
        in_specs=[smem] + [vmem] * 6,
        out_specs=[hbm] * (1 + len(saved)) + [vmem] * 2,
        scratch_shapes=[pltpu.VMEM(whole, BF16)] * layers
        + [pltpu.VMEM((layers,) + dims, kind) for dims, kind in kept]
        + [pltpu.VMEM((length, D), F32)]
        + swaps
        + codes
        + sems,
        compiler_params=pltpu.CompilerParams(
            collective_id=0, has_side_effects=True, vmem_limit_bytes=VMEM_BYTES
        ),
        name="forward",
    )(patch_counts, patches, *masters, norms)
    saved, activations, squares = outs[:-2], outs[-2], outs[-1]
    buffers = {}
    for width, order in PATHS[0] + PATHS[1]:
        sizes, refs = dict(z=nz, y=2, x=2), {}
        for axis in order[::-1]:
            sizes.pop(axis)
            dims = (nz,) if axis == "z" else ()
            dims += tuple(sizes.values()) + (depth, width)
            refs[axis] = pltpu.VMEM((n_groups // layers // 2,) + dims, BF16)
        buffers[order[::-1]] = refs
    small = around((1, columns), 4) + around((4, D), 4)
    grad, sums, rows, fresh, scalars, steps, norm_own = pl.pallas_call(
        functools.partial(backward_kernel, n_dp, cuts, totals, slots),
        out_shape=[
            shape((half, D), F32),
            shape((layers, depth, columns), F32),
            shape((128, 128), F32),
            shape((layers, 1, columns), F32),
            line,
            line,
            shape((128, 128), F32),
        ],
        in_specs=[smem] + [vmem] * 3 + [(vmem,) * 4] + [vmem] * 5 + [hbm] * len(saved),
        out_specs=[vmem] * 7,
        scratch_shapes=[pltpu.VMEM(whole, BF16)] * layers
        + [buffers]
        + [pltpu.VMEM(whole, BF16)]
        + [pltpu.VMEM(dims, kind) for dims, kind in kept[1:]]
        + [
            pltpu.VMEM((length, D), F32),
            pltpu.VMEM((length, D), BF16),
            pltpu.VMEM((D, length), BF16),
        ]
        + swaps
        + codes
        + [pltpu.VMEM((depth, 128), F32)] * 2
        + [pltpu.VMEM((128, 128), F32), pltpu.VMEM((D, 128), F32)]
        + [[small] * layers, around((8, 128), 8), around((8, 128), 8)]
        + sems,
        compiler_params=pltpu.CompilerParams(
            collective_id=1, has_side_effects=True, vmem_limit_bytes=VMEM_BYTES
        ),
        name="backward",
    )(
        patch_counts,
        cotangent,
        norms,
        squares,
        states_by_row,
        *states_by_column,
        norm_state,
        *saved,
    )
    like = lambda arrays, kind: [shape(array.shape, kind) for array in arrays]
    vectors = [shape(norm_state.shape, F32)]
    states = (
        qkv_rows, states_by_column[0], out_rows, out_cols,
        up_rows, up_cols, down_rows, down_cols,
    )
    results = [shape((half, D), BF16), shape((half, D), F32)]
    results += like(masters, F32) + vectors + like(masters, F32) + vectors + like(masters, BF16)
    results += like(states, F32)
    results += [shape((layers, 2, norm_state.shape[2]), F32)] * 2 + [shape((layers, 8), F32)]
    out = pl.pallas_call(
        functools.partial(apply_kernel, cuts, totals),
        out_shape=results,
        in_specs=[vmem] * 14,
        out_specs=[vmem] * len(results),
        scratch_shapes=[pltpu.VMEM((128, 128), F32)],
        compiler_params=pltpu.CompilerParams(vmem_limit_bytes=VMEM_BYTES),
        name="apply",
    )(
        activations, grad, sums, rows, fresh, scalars, steps, norm_own, *masters, norms, norm_state
    )
    out = list(out)
    for at in (2, 7, 12):
        out[at] = out[at].transpose(0, 2, 1, 3)
        out[at + 1] = out[at + 1].transpose(0, 2, 1)
        out[at + 3] = out[at + 3].transpose(0, 2, 1)
    out[17] = out[17].transpose(1, 0, 2)
    return tuple(out)


def kernels_fit(patches, qkv_weight):
    length = 2 * patches.shape[0]
    depth, local = qkv_weight.shape[1], qkv_weight.shape[3]
    return (
        lax.axis_size("mp") == 2
        and lax.axis_size("dp") % 4 == 0
        and depth % 16 == 0
        and length % TILE == 0
        and (4 * local) % GROUP == 0
    )


def per_device(*arrays):
    if kernels_fit(arrays[0], arrays[3]):
        return step_by_kernels(*arrays)
    return step_by_xla(*arrays)


def step_by_xla(
    patches,
    cotangent,
    patch_counts,
    qkv_weight,
    out_weight,
    up_weight,
    down_weight,
    norms,
    qkv_rows,
    qkv_cols,
    out_rows,
    out_cols,
    up_rows,
    up_cols,
    down_rows,
    down_cols,
    norm_state,
):
    layers = qkv_weight.shape[0]
    activations, grad, reduced, norm_terms = passes_by_xla(
        patches, cotangent, patch_counts, qkv_weight, out_weight, up_weight, down_weight, norms
    )
    col_axes = ("mp", "dp", "mp", "dp")
    row_counts = (D, D, D, FF)
    col_counts = (3 * D, D, FF, D)
    masters = (qkv_weight, out_weight, up_weight, down_weight)
    row_states = (qkv_rows, out_rows, up_rows, down_rows)
    col_states = (qkv_cols, out_cols, up_cols, down_cols)
    entries = [(layer, which) for layer in range(layers) for which in range(4)]
    grads = [reduced[layer][which] for layer, which in entries]
    row_olds = [row_states[which][layer] for layer, which in entries]
    col_olds = [col_states[which][layer] for layer, which in entries]
    width = norm_state.shape[2]
    row_parts, col_parts = ([], [])
    for position, (layer, which) in enumerate(entries):
        matrix = grads[position].reshape(grads[position].shape[0], -1)
        square = matrix * matrix + EPS_SQUARE
        row_parts.append(jnp.sum(square, axis=1))
        col_parts.append(jnp.sum(square, axis=0).reshape(col_olds[position].shape))
    model_side = tuple(
        [
            row_parts[position] if col_axes[which] == "mp" else col_parts[position]
            for position, (layer, which) in enumerate(entries)
        ]
    )
    data_side = tuple(
        (
            col_parts[position] if col_axes[which] == "mp" else row_parts[position]
            for position, (layer, which) in enumerate(entries)
        )
    ) + (norm_terms,)
    model_sums = jax.tree.map(
        lambda part: part.astype(jnp.float32), lax.psum(for_sending(model_side), "mp")
    )
    data_sums = lax.psum(data_side, "dp")
    norm_grad = lax.dynamic_slice_in_dim(
        data_sums[len(entries)], lax.axis_index("dp") * width, width, 2
    )
    row_sums = [
        model_sums[position] if col_axes[which] == "mp" else data_sums[position]
        for position, (layer, which) in enumerate(entries)
    ]
    col_sums = [
        data_sums[position] if col_axes[which] == "mp" else model_sums[position]
        for position, (layer, which) in enumerate(entries)
    ]
    row_news = [
        DECAY * row_olds[position] + (1.0 - DECAY) * row_sums[position] / col_counts[which]
        for position, (layer, which) in enumerate(entries)
    ]
    shares = jnp.stack(
        [
            jnp.sum(row_news[position]) / size_of(col_axes[which])
            for position, (layer, which) in enumerate(entries)
        ]
    )
    row_totals = lax.psum(shares, ("dp", "mp"))
    row_means = [
        row_totals[position] / row_counts[which] for position, (layer, which) in enumerate(entries)
    ]
    col_news = [
        DECAY * col_olds[position] + (1.0 - DECAY) * col_sums[position] / row_counts[which]
        for position, (layer, which) in enumerate(entries)
    ]
    directions, step_parts, weight_parts = ([], [], [])
    for position, (layer, which) in enumerate(entries):
        matrix = grads[position].reshape(grads[position].shape[0], -1)
        second = (
            row_news[position][:, None] * col_news[position].reshape(1, -1) / row_means[position]
        )
        direction = matrix * lax.rsqrt(second)
        directions.append(direction)
        step_parts.append(jnp.sum(direction * direction))
        master = masters[which][layer]
        weight_parts.append(jnp.sum(master * master))
    own_norms = lax.dynamic_slice_in_dim(norms, lax.axis_index("dp") * width, width, 2)
    norm_state_new = DECAY * norm_state + (1.0 - DECAY) * (norm_grad * norm_grad + EPS_SQUARE)
    norm_dirs = norm_grad * lax.rsqrt(norm_state_new)
    norm_parts = jnp.sum(norm_dirs * norm_dirs, axis=2) / lax.axis_size("mp")
    step_all = jnp.concatenate(
        [jnp.stack(step_parts).reshape(layers, 4), norm_parts], axis=1
    ).reshape(-1)
    step_total, weight_total = lax.psum((step_all, jnp.stack(weight_parts)), ("dp", "mp"))
    step_total = step_total.reshape(layers, 8)
    matrix_counts = jnp.asarray(
        [float(row_counts[which] * col_counts[which]) for which in range(4)], jnp.float32
    )
    update_rms = jnp.concatenate(
        [jnp.sqrt(step_total[:, :4] / matrix_counts[None, :]), jnp.sqrt(step_total[:, 4:] / D)],
        axis=1,
    )
    news = [[None] * layers for which in range(4)]
    rows_new = [[None] * layers for which in range(4)]
    cols_new = [[None] * layers for which in range(4)]
    for position, (layer, which) in enumerate(entries):
        master = masters[which][layer]
        scale = jnp.sqrt(weight_total[position] / (row_counts[which] * col_counts[which]) + 1e-06)
        clipped = directions[position] / jnp.maximum(1.0, update_rms[layer, which] / CLIP)
        news[which][layer] = master - RATE * scale * clipped.reshape(master.shape)
        rows_new[which][layer] = row_news[position]
        cols_new[which][layer] = col_news[position]
    norm_scale = jnp.sqrt(jnp.mean(norms * norms, axis=2) + 1e-06)
    norm_clipped = norm_dirs / jnp.maximum(1.0, update_rms[:, 4:] / CLIP)[:, :, None]
    norm_new = own_norms - RATE * norm_scale[:, :, None] * norm_clipped
    grad_out = [jnp.stack([reduced[layer][which] for layer in range(layers)]) for which in range(4)]
    new_out = [jnp.stack(news[which]) for which in range(4)]
    row_out = [jnp.stack(rows_new[which]) for which in range(4)]
    col_out = [jnp.stack(cols_new[which]) for which in range(4)]
    return (
        activations,
        grad,
        grad_out[0],
        grad_out[1],
        grad_out[2],
        grad_out[3],
        norm_grad,
        new_out[0],
        new_out[1],
        new_out[2],
        new_out[3],
        norm_new,
        new_out[0].astype(jnp.bfloat16),
        new_out[1].astype(jnp.bfloat16),
        new_out[2].astype(jnp.bfloat16),
        new_out[3].astype(jnp.bfloat16),
        row_out[0],
        col_out[0],
        row_out[1],
        col_out[1],
        row_out[2],
        col_out[2],
        row_out[3],
        col_out[3],
        norm_state_new[:, 0:2],
        norm_state_new[:, 2:4],
        update_rms,
    )


def solution(mesh):
    in_specs = (
        P(("dp", "mp"), None),
        P(("dp", "mp"), None),
        P("dp"),
        P(None, "dp", None, "mp"),
        P(None, "mp", "dp"),
        P(None, "dp", "mp"),
        P(None, "mp", "dp"),
        P(),
        P(None, "dp"),
        P(None, None, "mp"),
        P(None, "mp"),
        P(None, "dp"),
        P(None, "dp"),
        P(None, "mp"),
        P(None, "mp"),
        P(None, "dp"),
        P(None, None, "dp"),
    )
    out_specs = (
        P(("dp", "mp"), None),
        P(("dp", "mp"), None),
        P(None, "dp", None, "mp"),
        P(None, "mp", "dp"),
        P(None, "dp", "mp"),
        P(None, "mp", "dp"),
        P(None, None, "dp"),
        P(None, "dp", None, "mp"),
        P(None, "mp", "dp"),
        P(None, "dp", "mp"),
        P(None, "mp", "dp"),
        P(None, None, "dp"),
        P(None, "dp", None, "mp"),
        P(None, "mp", "dp"),
        P(None, "dp", "mp"),
        P(None, "mp", "dp"),
        P(None, "dp"),
        P(None, None, "mp"),
        P(None, "mp"),
        P(None, "dp"),
        P(None, "dp"),
        P(None, "mp"),
        P(None, "mp"),
        P(None, "dp"),
        P(None, None, "dp"),
        P(None, None, "dp"),
        P(),
    )
    return jax.shard_map(
        per_device, mesh=mesh, in_specs=in_specs, out_specs=out_specs, check_vma=False
    )
```

```python
import functools

import jax
import jax.numpy as jnp
from jax import lax
from jax.experimental import pallas as pl
from jax.experimental.pallas import tpu as pltpu
from jax.sharding import PartitionSpec as P

D = 768
HEAD_DIM = 64
FF = 3072


DECAY = 0.5
EPS_SQUARE = 1e-30
CLIP = 0.25
RATE = 2.0
MASKED = -1e30


def for_sending(value):
    return jax.tree.map(lambda a: a.astype(jnp.bfloat16) if a.dtype == jnp.float32 else a, value)


def layer_norm(rows, gain, shift):
    centre = rows - jnp.mean(rows, axis=-1, keepdims=True)
    spread = jnp.mean(centre * centre, axis=-1, keepdims=True)
    return centre * lax.rsqrt(spread + 1e-06) * gain + shift


def norm_back(rows, gain, shift, grad):
    result, back = jax.vjp(layer_norm, rows, gain, shift)
    return back(grad)


def exact_gelu(values):
    return jax.nn.gelu(values, approximate=False)


def segments(counts, length):
    bounds = jnp.cumsum(counts)
    places = jnp.arange(length, dtype=jnp.int32)
    image = jnp.sum((places[:, None] >= bounds[None, :]).astype(jnp.int32), axis=1)
    live = (places < bounds[-1]).astype(jnp.float32)
    return (image[:, None] == image[None, :], live)


def attention_scores(query, keys, same):
    scale = query.shape[-1] ** (-0.5)
    scores = jnp.einsum("qhd,khd->hqk", query, keys, preferred_element_type=jnp.float32) * scale
    return jnp.where(same[None], scores, MASKED)


def attend(qkv, same):
    scores = attention_scores(qkv[:, 0], qkv[:, 1], same)
    top = jnp.max(scores, axis=-1, keepdims=True)
    raised = jnp.exp(scores - top)
    total = jnp.sum(raised, axis=-1, keepdims=True)
    probs = (raised / total).astype(jnp.bfloat16)
    mixed = jnp.einsum("hqk,khd->qhd", probs, qkv[:, 2], preferred_element_type=jnp.float32)
    return (mixed.reshape(mixed.shape[0], -1), top + jnp.log(total))


def attend_back(qkv, same, log_total, grad_mixed):
    query, keys, values = (qkv[:, 0], qkv[:, 1], qkv[:, 2])
    scale = query.shape[-1] ** (-0.5)
    probs = jnp.exp(attention_scores(query, keys, same) - log_total)
    d_values = jnp.einsum(
        "hqk,qhd->khd", probs.astype(jnp.bfloat16), grad_mixed, preferred_element_type=jnp.float32
    )
    d_probs = jnp.einsum("qhd,khd->hqk", grad_mixed, values, preferred_element_type=jnp.float32)
    d_scores = (probs * (d_probs - jnp.sum(probs * d_probs, axis=-1, keepdims=True))).astype(
        jnp.bfloat16
    )
    d_query = jnp.einsum("hqk,khd->qhd", d_scores, keys, preferred_element_type=jnp.float32) * scale
    d_keys = jnp.einsum("hqk,qhd->khd", d_scores, query, preferred_element_type=jnp.float32) * scale
    return jnp.stack([d_query, d_keys, d_values], axis=1).astype(jnp.bfloat16)


def spread_rows(values):
    return lax.all_gather(values, "mp", axis=0, tiled=True)


def size_of(name):
    return lax.axis_size("dp") if name == "dp" else lax.axis_size("mp")


TILE = 112
VMEM_BYTES = 64 << 20
LAG = 3
GROUP = 384
PATHS = (((128, "zyx"), (256, "xzy")), ((128, "zxy"), (256, "yzx")))
BIG = 1e30
MESH = pl.DeviceIdType.MESH
F32 = jnp.float32
BF16 = jnp.bfloat16
NN = ((1,), (0,))
NT = ((1,), (1,))
PLANE = [(dy, dx, dc) for dy in range(2) for dx in range(2) for dc in range(2)][1:]


def dot(left, right, dims):
    return lax.dot_general(left, right, (dims, ((), ())), preferred_element_type=F32)


class Place:
    def __init__(self, n_dp):
        self.nz = n_dp // 4
        me = lax.axis_index("dp")
        self.core = lax.axis_index("mp")
        self.z, self.y, self.x = me // 4, (me // 2) % 2, me % 2

    def at(self, z, y, x, core):
        return (z * 4 + y * 2 + x, core)

    def over_x(self):
        return self.at(self.z, self.y, 1 - self.x, self.core)

    def over_y(self):
        return self.at(self.z, 1 - self.y, self.x, self.core)

    def over_z(self, step):
        return self.at((self.z + step) % self.nz, self.y, self.x, self.core)

    def over_core(self):
        return self.at(self.z, self.y, self.x, 1 - self.core)

    def near(self, dy, dx, dc):
        return self.at(self.z, (self.y + dy) % 2, (self.x + dx) % 2, (self.core + dc) % 2)

    def barrier(self):
        sem = pltpu.get_barrier_semaphore()
        others = [self.near(dy, dx, dc) for dy, dx, dc in PLANE]
        others += [self.over_z(step) for step in range(1, self.nz)]
        for other in others:
            pl.semaphore_signal(sem, inc=1, device_id=other, device_id_type=MESH)
        pl.semaphore_wait(sem, len(others))


class Sender:
    def __init__(self, send_sems, recv_sems):
        self.send_sems, self.recv_sems = send_sems, recv_sems
        self.count = 0
        self.sent = []

    def make(self, src, dst, device, number=None):
        at = self.count
        self.count += 1
        return pltpu.make_async_remote_copy(
            src_ref=src,
            dst_ref=dst,
            send_sem=self.send_sems.at[at],
            recv_sem=self.recv_sems.at[at if number is None else number],
            device_id=device,
            device_id_type=MESH,
        )

    def start(self, src, dst, device):
        copy = self.make(src, dst, device)
        copy.start()
        self.sent.append(copy)
        return copy

    def drain(self):
        for copy in self.sent:
            copy.wait_send()
        self.sent = []


def parts_of(layer, low, turn):
    parts = []
    for width, order in PATHS[turn % 2]:
        parts.append((layer, low, low + width, order))
        low += width
    return parts


class Links:
    def __init__(self, place, sender):
        self.p, self.sender = place, sender
        self.inner = jnp.logical_or(place.z == 1, place.z == 2)
        self.copies = {}
        self.only_inner, self.only_outer = [], []

    def over_z_bit(self, bit):
        return self.p.at(self.p.z ^ bit, self.p.y, self.p.x, self.p.core)

    def steps(self, order):
        return order.replace("z", "zf")

    def over(self, axis):
        return self.p.over_x() if axis == "x" else self.p.over_y()

    def drain(self):
        @pl.when(self.inner)
        def _():
            for copy in self.only_inner:
                copy.wait_send()

        @pl.when(jnp.logical_not(self.inner))
        def _():
            for copy in self.only_outer:
                copy.wait_send()


class Gather(Links):
    def __init__(self, place, sender, weights, groups):
        super().__init__(place, sender)
        self.weights, self.groups = weights, groups
        self.tick_at = 0

    def view(self, part, done, z=None):
        layer, low, high, order = part
        p = self.p
        at_z = slice(None) if "z" in done else (p.z if z is None else z)
        at_y = slice(None) if "y" in done else p.y
        at_x = slice(None) if "x" in done else p.x
        return self.weights[layer].at[at_z, at_y, at_x, :, low:high]

    def stage(self, part, at):
        steps = self.steps(part[3])
        axis, done = steps[at], steps[:at].replace("f", "")
        before = self.copies.get((part, at - 1), ())
        if axis == "f":
            near, far, third, number = before
            far.wait_recv()
            piece = self.view(part, done.replace("z", ""), self.p.z ^ 2)
            onward = self.sender.make(piece, piece, self.over_z_bit(1), number)

            @pl.when(self.inner)
            def _():
                onward.start()

            self.only_inner.append(onward)
            self.copies[part, at] = [near, third]
            return
        for copy in before:
            copy.wait_recv()
        piece = self.view(part, done)
        if axis == "z":
            near = self.sender.start(piece, piece, self.over_z_bit(1))
            far = self.sender.start(piece, piece, self.over_z_bit(2))
            number = self.sender.count
            third = self.sender.make(piece, piece, self.over_z_bit(3))

            @pl.when(self.inner)
            def _():
                third.start()

            self.only_inner.append(third)
            self.copies[part, at] = (near, far, third, number)
        else:
            self.copies[part, at] = [self.sender.start(piece, piece, self.over(axis))]

    def tick(self):
        t = self.tick_at
        self.tick_at += 1
        for at in range(4):
            if 0 <= t - at < len(self.groups):
                for part in self.groups[t - at]:
                    self.stage(part, at)

    def poll(self):
        if self.tick_at < len(self.groups) + 3:
            self.tick()

    def ready(self, k):
        while self.tick_at < min(k + 4 + 1, len(self.groups) + 3):
            self.tick()
        for part in self.groups[k]:
            for copy in self.copies.pop((part, 3), ()):
                copy.wait_recv()


class Rounds:
    def __init__(self, place, sender):
        self.p, self.sender = place, sender

    def plane(self, term, slots, cores=False):
        p = self.p
        at = p.y * 2 + p.x
        at = at * 2 + p.core if cores else at
        slots[at] = term[...]
        return [
            self.sender.start(term, slots.at[at], p.near(dy, dx, dc))
            for dy, dx, dc in PLANE
            if cores or not dc
        ]

    def along_z(self, term, slots):
        p = self.p
        slots[p.z] = term[...]
        return [self.sender.start(term, slots.at[p.z], p.over_z(step)) for step in range(1, p.nz)]


def slot_sum(copies, slots):
    for copy in copies:
        copy.wait_recv()
    total = slots[0]
    for at in range(1, slots.shape[0]):
        total = total + slots[at]
    return total


class Scatter(Links):
    def __init__(
        self, place, sender, grads, groups, buffers, result, cuts, by_row, by_column
    ):
        super().__init__(place, sender)
        self.grads, self.groups, self.buffers, self.result = grads, groups, buffers, result
        self.cuts, self.by_row, self.by_column = cuts, by_row, by_column
        self.started, self.offered, self.clock, self.paced = 0, 0, 0, 0
        self.flying = {}

    def view(self, part, done, z=None, y=None, x=None):
        layer, low, high, order = part
        p = self.p
        at_z = slice(None) if z is None and "z" not in done else (p.z if z is None else z)
        at_y = slice(None) if y is None and "y" not in done else (p.y if y is None else y)
        at_x = slice(None) if x is None and "x" not in done else (p.x if x is None else x)
        return self.grads[layer].at[at_z, at_y, at_x, :, low:high]

    def add(self, into, term):
        into[...] = (into[...].astype(F32) + term[...].astype(F32)).astype(BF16)

    def put(self, part, into, value, last):
        if last:
            layer, low, high, _ = part
            self.result[layer, :, low:high] = value
        else:
            into[...] = value.astype(BF16)

    def buffer(self, k, at, name):
        ref = self.buffers[self.groups[k][at][3]][name]
        return ref.at[(k // 2) % ref.shape[0]]

    def absorb(self, k, at, step):
        part = self.groups[k][at]
        steps = self.steps(part[3])
        if step == 0:
            return ""
        axis, done = steps[step - 1], steps[: step - 1].replace("f", "")
        copies = self.copies.pop((k, at, step - 1))
        last = step == len(steps)
        if axis in "xy":
            copies[0].wait_recv()
            total = self.view(part, done + axis)
            value = total[...].astype(F32) + self.buffer(k, at, axis)[...].astype(F32)
            self.put(part, total, value, last)
        elif axis == "f":
            near, far, third = copies
            done = done.replace("z", "")
            total = self.view(part, done + "z")
            slots = self.buffer(k, at, "z")
            near.wait_recv()
            far.wait_recv()
            value = total[...].astype(F32) + slots[0].astype(F32) + slots[1].astype(F32)
            self.put(part, total, value, last)

            @pl.when(self.inner)
            def _():
                third.wait_recv()
                self.put(part, total, value + slots[2].astype(F32), last)

            done = done + "z"
            return done
        return done + axis

    def stage(self, k, at, step):
        part = self.groups[k][at]
        steps = self.steps(part[3])
        p = self.p
        if step < len(steps) and steps[step] == "f":
            near, far, third, relay, far_number = self.copies.pop((k, at, step - 1))
            done = steps[: step - 1]
            slots = self.buffer(k, at, "z")
            piece = self.view(part, done, z=p.z ^ 2)
            onward = self.sender.make(piece, slots.at[1], self.over_z_bit(2), far_number)

            @pl.when(self.inner)
            def _():
                relay.wait_recv()
                self.add(piece, slots.at[3])
                onward.start()

            self.only_inner.append(onward)
            self.copies[k, at, step] = (near, far, third)
            return
        done = self.absorb(k, at, step)
        if step == len(steps):
            self.measure(part)
            return
        axis = steps[step]
        if axis == "z":
            slots = self.buffer(k, at, "z")
            near = self.sender.start(
                self.view(part, done, z=p.z ^ 1), slots.at[0], self.over_z_bit(1)
            )
            far_number = self.sender.count
            far = self.sender.make(
                self.view(part, done, z=p.z ^ 2), slots.at[1], self.over_z_bit(2)
            )
            across = self.view(part, done, z=p.z ^ 3)
            third = self.sender.make(across, slots.at[2], self.over_z_bit(3))
            relay = self.sender.make(across, slots.at[3], self.over_z_bit(1))

            @pl.when(self.inner)
            def _():
                third.start()

            @pl.when(jnp.logical_not(self.inner))
            def _():
                relay.start()
                far.start()

            self.only_inner.append(third)
            self.only_outer += [relay, far]
            self.copies[k, at, step] = (near, far, third, relay, far_number)
        else:
            flip = {axis: 1 - (p.x if axis == "x" else p.y)}
            self.copies[k, at, step] = [
                self.sender.start(
                    self.view(part, done, **flip), self.buffer(k, at, axis), self.over(axis)
                )
            ]

    def measure(self, part):
        layer, low, high, _ = part
        total = self.result[layer, :, low:high]
        squares = total * total + EPS_SQUARE
        self.by_column[layer][:, low:high] = jnp.sum(squares, axis=0, keepdims=True)
        lane = lax.broadcasted_iota(jnp.int32, (1, 128), 1)
        for which, (first, end) in enumerate(self.cuts):
            if first <= low < end:
                term = jnp.sum(squares, axis=1, keepdims=True)
                self.by_row[...] += jnp.where(lane == layer * 4 + which, term, 0.0)

    def start(self):
        k = self.started
        self.started += 1
        for at in range(len(self.groups[k])):
            self.stage(k, at, 0)
        self.flying[k] = (1, self.clock)

    def offer(self):
        self.offered += 1

    def burst(self):
        while self.started < min(self.offered, 1):
            self.start()

    def poll(self, lag=LAG):
        self.clock += 1
        for k in list(self.flying):
            step, since = self.flying[k]
            if self.clock - since < lag:
                continue
            for at in range(len(self.groups[k])):
                self.stage(k, at, step)
            if step == 4:
                del self.flying[k]
            else:
                self.flying[k] = (step + 1, self.clock)
        if self.started < self.offered and len(self.flying) < 12:
            if lag == 1 or self.clock - self.paced >= 1:
                self.paced = self.clock
                self.start()


def row_tiles(length, body):
    def step(i, carry):
        body(pl.ds(pl.multiple_of(i * TILE, TILE), TILE))
        return carry

    lax.fori_loop(0, length // TILE, step, 0)


def normalised(rows):
    centre = rows - jnp.mean(rows, axis=-1, keepdims=True)
    spread = jnp.mean(centre * centre, axis=-1, keepdims=True)
    rise = lax.rsqrt(spread + 1e-06)
    return centre * rise, rise


def encode_segments(counts, slots, qe, ke):
    length = qe.shape[0]
    place = lax.broadcasted_iota(jnp.int32, (length, 128), 0)
    lane = lax.broadcasted_iota(jnp.int32, (length, 128), 1) % HEAD_DIM
    image = jnp.zeros((length, 128), jnp.int32)
    total = jnp.int32(0)
    for slot in range(slots):
        total = total + counts[slot]
        image = image + (place >= total).astype(jnp.int32)
    hit = image == lane
    ke[...] = jnp.where(hit, 1.0, 0.0).astype(BF16)
    qe[...] = jnp.where(jnp.logical_or(hit, lane > slots), 0.0, -BIG).astype(BF16)


def attention_forward(qkv, qe, ke, log_total, mixed, between):
    length, width = mixed.shape
    lane = lax.broadcasted_iota(jnp.int32, (length, 128), 1)

    def pair(at, carry):
        low = pl.multiple_of(at * 128, 128)
        query = qkv[:, pl.ds(low, 128)] * jnp.asarray(0.125, BF16)
        keys = qkv[:, pl.ds(width + low, 128)]
        values = qkv[:, pl.ds(2 * width + low, 128)].T
        outs = []
        for half in range(2):
            own = (lane < HEAD_DIM) if half == 0 else (lane >= HEAD_DIM)
            q = jnp.where(own, query, qe[...])
            k = jnp.where(own, keys, ke[...])
            scores = dot(k, q, NT)
            top = jnp.max(scores, axis=0, keepdims=True)
            raised = jnp.exp(scores - top)
            total = jnp.sum(raised, axis=0, keepdims=True)
            rows = slice(half * HEAD_DIM, (half + 1) * HEAD_DIM)
            outs.append(dot(values[rows], raised.astype(BF16), NN) / total)
            log_total[pl.ds(at * 2 + half, 1), :] = top + jnp.log(total)
        mixed[:, pl.ds(low, 128)] = jnp.concatenate(outs, axis=0).T.astype(BF16)
        return carry

    for at in range(width // 128):
        lax.fori_loop(at, at + 1, pair, 0)
        between()


def attention_backward(qkv, qe, ke, log_total, d_mixed, between):
    length, width = d_mixed.shape
    lane = lax.broadcasted_iota(jnp.int32, (length, 128), 1)

    def pair(at, carry):
        low = pl.multiple_of(at * 128, 128)
        query = qkv[:, pl.ds(low, 128)] * jnp.asarray(0.125, BF16)
        keys = qkv[:, pl.ds(width + low, 128)]
        values = qkv[:, pl.ds(2 * width + low, 128)]
        d_out = d_mixed[:, pl.ds(low, 128)]
        keys_t = keys.T
        d_query, d_keys, d_values = [], [], []
        for half in range(2):
            own = (lane < HEAD_DIM) if half == 0 else (lane >= HEAD_DIM)
            q = jnp.where(own, query, qe[...])
            k = jnp.where(own, keys, ke[...])
            v = jnp.where(own, values, jnp.zeros_like(values))
            probs = jnp.exp(dot(k, q, NT) - log_total[pl.ds(at * 2 + half, 1), :])
            d_probs = dot(v, d_out, NT)
            mean = jnp.sum(probs * d_probs, axis=0, keepdims=True)
            d_scores = (probs * (d_probs - mean)).astype(BF16)
            d_values.append(dot(probs.astype(BF16), d_out, NN))
            d_keys.append(dot(d_scores, query, NN))
            rows = slice(half * HEAD_DIM, (half + 1) * HEAD_DIM)
            d_query.append(dot(keys_t[rows], d_scores, NN))
        first = lane < HEAD_DIM
        d_q = jnp.concatenate(d_query, axis=0).T * 0.125
        qkv[:, pl.ds(low, 128)] = d_q.astype(BF16)
        qkv[:, pl.ds(width + low, 128)] = jnp.where(first, *d_keys).astype(BF16)
        qkv[:, pl.ds(2 * width + low, 128)] = jnp.where(first, *d_values).astype(BF16)
        return carry

    for at in range(width // 128):
        lax.fori_loop(at, at + 1, pair, 0)
        between()


class Exchange:
    def __init__(self, place, sender, out, into):
        self.p, self.sender, self.out, self.into = place, sender, out, into
        self.turn = 0
        self.copies = {}
        length = out.shape[1]
        cut = (length // TILE + 1) // 2 * TILE
        self.chunks = ((0, cut), (cut, length))

    def send(self, compute):
        slot = self.turn % 2
        for copy in self.copies.get(slot, ()):
            copy.wait_send()
            self.sender.sent = [item for item in self.sender.sent if item is not copy]
        self.copies[slot] = []
        for low, high in self.chunks:
            self.out[slot, low:high, :] = compute(low, high).astype(BF16)
            piece = self.out.at[slot, low:high, :]
            self.copies[slot].append(
                self.sender.start(piece, self.into.at[slot, low:high, :], self.p.over_core())
            )

    def swap_halves(self, compute, meanwhile, body):
        slot = self.turn % 2
        for copy in self.copies.get(slot, ()):
            copy.wait_send()
            self.sender.sent = [item for item in self.sender.sent if item is not copy]
        length = self.out.shape[1]
        count = (length // TILE + 1) // 2 * TILE
        first = (length // 2 // TILE) * TILE
        core = self.p.core
        theirs = pl.ds(pl.multiple_of((1 - core) * first, TILE), count)
        self.out[slot, theirs, :] = compute(theirs).astype(BF16)
        copy = self.sender.start(
            self.out.at[slot, theirs, :], self.into.at[slot, theirs, :], self.p.over_core()
        )
        mine = pl.ds(pl.multiple_of(core * first, TILE), count)
        own = compute(mine).astype(BF16).astype(F32)
        meanwhile()
        copy.wait_recv()
        body(mine, own + self.into[slot, mine, :].astype(F32))

    def take(self, body, between=lambda: None):
        slot = self.turn % 2
        self.turn += 1
        for (low, high), copy in zip(self.chunks, self.copies[slot]):
            copy.wait_recv()

            def step(i, carry, low=low):
                rows = pl.ds(pl.multiple_of(low + i * TILE, TILE), TILE)
                total = self.out[slot, rows, :].astype(F32) + self.into[slot, rows, :].astype(F32)
                body(rows, total)
                return carry

            lax.fori_loop(0, (high - low) // TILE, step, 0)
            if high != self.chunks[-1][1]:
                between()


def grand_total(value):
    return jnp.sum(jnp.sum(value, axis=1, keepdims=True), axis=0, keepdims=True)


def store(grads, low, value):
    cols = slice(low, low + value.shape[1])
    grads[:, :, :, :, cols] = value.astype(BF16).reshape(grads.shape[:4] + value.shape[1:])


def flat(w, low, high):
    value = w[:, :, :, :, low:high]
    return value.reshape(-1, high - low)


def gelu_and_slope(hidden):
    cdf = 0.5 * (1.0 + lax.erf(hidden * (0.5**0.5)))
    slope = cdf + hidden * (jnp.exp(-0.5 * hidden * hidden) * 0.3989422804014327)
    return hidden * cdf, slope


def forward_kernel(
    n_dp, cuts, slots,
    counts, patches, cotangent, qkv_w, out_w, up_w, down_w, norms,
    o_weights, o_rows, o_middle, o_normed_a, o_qkv, o_mixed, o_normed_b, o_active, o_slope, o_log,
    o_rounded, o_grads, o_result, o_squares,
    w0, w1, grads, rounded, turned, rows, middle, normed_a, qkv, mixed, normed_b, active, slope, log_total, final,
    x_out, x_in, qe, ke, send_sems, recv_sems, local_sems,
):
    layers, half = 2, patches.shape[0]
    length = 2 * half
    c_qkv, c_out, c_up, c_down = cuts
    p = Place(n_dp)
    sender = Sender(send_sems, recv_sems)
    local = []

    def move(src, dst):
        copy = pltpu.make_async_copy(src, dst, local_sems.at[len(local)])
        copy.start()
        local.append(copy)
        return copy

    weights = (w0, w1)
    local_heads = qkv_w.shape[3]

    def master(layer, which):
        if which == 0:
            return [qkv_w[layer, part] for part in range(3)]
        return [(out_w, up_w, down_w)[which - 1][layer]]

    def place_pieces(layer):
        for which, (low, _) in enumerate(cuts):
            for part, value in enumerate(master(layer, which)):
                cols = slice(low + part * local_heads, low + part * local_heads + value.shape[1])
                weights[layer][p.z, p.y, p.x, :, cols] = value.astype(BF16)

    place_pieces(0)
    p.barrier()
    starts = [(l, low) for l in range(layers) for low in range(0, c_down[1], GROUP)]
    groups = [parts_of(l, low, turn) for turn, (l, low) in enumerate(starts)]
    per = len(groups) // layers
    gather = Gather(p, sender, weights, groups)
    gather.tick()
    own_rows = pl.ds(pl.multiple_of(p.core * half, half), half)
    rows[0, own_rows, :] = patches[...].astype(F32)
    swap = sender.start(rows.at[0, own_rows, :], rows.at[0, own_rows, :], p.over_core())
    place_pieces(1)
    gather.tick()
    total = jnp.int32(0)
    for slot in range(slots):
        total = total + counts[slot]
    place = lax.broadcasted_iota(jnp.int32, (half, 1), 0) + p.core * half
    final[own_rows, :] = jnp.where(place < total, cotangent[...].astype(F32), 0.0)
    swap_back = sender.start(final.at[own_rows, :], final.at[own_rows, :], p.over_core())
    encode_segments(counts, slots, qe, ke)
    gather.tick()
    swap.wait_recv()
    exchange = Exchange(p, sender, x_out, x_in)

    def norm_into(target, layer, which, at, value):
        hat, _ = normalised(value)
        gain, shift = norms[layer, which : which + 1, :], norms[layer, which + 1 : which + 2, :]
        target[layer, at, :] = (hat * gain + shift).astype(BF16)

    row_tiles(length, lambda at: norm_into(normed_a, 0, 0, at, rows[0, at, :]))
    saves = [(rows, o_rows, 0), (normed_a, o_normed_a, 0)]
    gather.tick()
    swap_back.wait_recv()
    swap_back.wait_send()
    sender.sent = [item for item in sender.sent if item is not swap_back]

    def round_step(at):
        rounded[at, :] = final[at, :].astype(BF16)

    row_tiles(length, round_step)
    move(rounded, o_rounded)

    def save(*items):
        for src, dst, layer in items:
            move(src.at[layer], dst.at[layer])

    save(*saves)
    for layer in range(layers):
        w, base = weights[layer], per * layer
        for k in range(c_qkv[1] // GROUP):
            gather.ready(base + k)
            cols = slice(k * GROUP, (k + 1) * GROUP)
            value = dot(normed_a[layer], flat(w, cols.start, cols.stop), NN)
            qkv[layer, :, cols] = value.astype(BF16)
        attention_forward(
            qkv.at[layer], qe, ke, log_total.at[layer], mixed.at[layer], gather.poll
        )
        save((qkv, o_qkv, layer), (log_total, o_log, layer), (mixed, o_mixed, layer))
        gather.ready(base + c_out[0] // GROUP)
        w_out = flat(w, *c_out)
        exchange.send(lambda low, high: dot(mixed[layer, low:high, :], w_out, NT))
        gather.poll()

        def mid_step(at, total):
            value = rows[layer, at, :] + total
            middle[layer, at, :] = value
            norm_into(normed_b, layer, 2, at, value)

        exchange.take(mid_step)
        save((middle, o_middle, layer), (normed_b, o_normed_b, layer))
        for k in range(c_up[0] // GROUP, c_up[1] // GROUP):
            gather.ready(base + k)
            low = k * GROUP
            cols = slice(low - c_up[0], low - c_up[0] + GROUP)
            hidden = dot(normed_b[layer], flat(w, low, low + GROUP), NN)
            act, rise = gelu_and_slope(hidden)
            active[layer, :, cols] = act.astype(BF16)
            slope[layer, :, cols] = rise.astype(BF16)
        last_layer = layer + 1 == layers
        if last_layer:
            turned[...] = rounded[...].T
            for low in range(c_down[0], c_down[1], GROUP):
                cols = slice(low - c_down[0], low - c_down[0] + GROUP)
                store(grads, low - c_up[0], dot(turned[...], active[layer, :, cols], NN))
                gather.poll()
            turned[...] = normed_b[layer].T
            cols = slice(c_down[0] - c_up[0], c_down[1] - c_up[0])
            move(grads.at[:, :, :, :, cols], o_grads.at[:, :, :, :, cols])
            cols = slice(0, c_up[1])
            move(w.at[:, :, :, :, cols], o_weights.at[layer, :, :, :, :, cols])
        else:
            save((active, o_active, layer), (slope, o_slope, layer))

        def mlp_back(low):
            cols = slice(low - c_down[0], low - c_down[0] + GROUP)
            d_active = dot(rounded[...], flat(w, low, low + GROUP), NN)
            d_hidden = (d_active * slope[layer, :, cols].astype(F32)).astype(BF16)
            slope[layer, :, cols] = d_hidden
            store(grads, cols.start, dot(turned[...], d_hidden, NN))
            move(grads.at[:, :, :, :, cols], o_grads.at[:, :, :, :, cols])
            move(slope.at[layer, :, cols], o_slope.at[layer, :, cols])

        for k in range(c_down[0] // GROUP, c_down[1] // GROUP - 1):
            gather.ready(base + k)
            low = k * GROUP
            if last_layer:
                mlp_back(low)
            cols = slice(low - c_down[0], low - c_down[0] + GROUP)
            term = dot(active[layer, :, cols], flat(w, low, low + GROUP), NT)
            if k * GROUP == c_down[0]:
                final[...] = term
            else:
                final[...] += term
        gather.ready(base + c_down[1] // GROUP - 1)
        w_down = flat(w, c_down[1] - GROUP, c_down[1])
        cols = slice(c_down[1] - c_down[0] - GROUP, c_down[1] - c_down[0])
        if layer + 1 < layers:
            exchange.send(
                lambda low, high: final[low:high, :]
                + dot(active[layer, low:high, cols], w_down, NT)
            )
            move(w, o_weights.at[layer])
            gather.poll()

            def next_step(at, total):
                value = middle[layer, at, :] + total
                rows[layer + 1, at, :] = value
                norm_into(normed_a, layer + 1, 0, at, value)

            exchange.take(next_step)
            save((rows, o_rows, layer + 1), (normed_a, o_normed_a, layer + 1))
        else:
            def last_step(at, total):
                final[at, :] = middle[layer, at, :] + total

            exchange.swap_halves(
                lambda at: final[at, :] + dot(active[layer, at, cols], w_down, NT),
                lambda: mlp_back(c_down[1] - GROUP),
                last_step,
            )
    o_result[...] = final[own_rows, :].astype(BF16)
    sender.drain()
    gather.drain()
    lane = lax.broadcasted_iota(jnp.int32, (1, 128), 1)
    squares = jnp.zeros((1, 128), F32)
    for layer in range(layers):
        for which in range(4):
            total = sum(grand_total(value * value) for value in master(layer, which))
            squares = squares + jnp.where(lane == layer * 4 + which, total, 0.0)
    o_squares[...] = squares
    for copy in local:
        copy.wait()


def backward_kernel(
    n_dp, cuts, totals, slots,
    counts, norms, squares, row_states, qkv_c, out_c, up_c, down_c, norm_state,
    i_weights, i_rows, i_middle, i_normed_a, i_qkv, i_mixed, i_normed_b, i_active, i_slope, i_log,
    i_rounded, i_grads, o_input, o_pieces, o_rows, o_columns, o_scalars, o_steps, o_own,
    g0, g1, buffers,
    w, kept, normed_a, qkv, mixed, normed_b, active, slope, log_total,
    grad, rounded, turned, x_out, x_in, qe, ke, by_row, row_in, square, tall, small, few, last,
    send_sems, recv_sems, local_sems,
):
    layers, half = 2, o_input.shape[0]
    length = 2 * half
    c_qkv, c_out, c_up, c_down = cuts
    p = Place(n_dp)
    sender = Sender(send_sems, recv_sems)
    count = [0]

    def load(src, dst):
        copy = pltpu.make_async_copy(src, dst, local_sems.at[count[0]])
        count[0] += 1
        copy.start()
        return copy

    def load_mlp(l):
        cols = slice(c_up[0], c_down[1])
        return dict(
            active=load(i_active.at[l], active),
            slope=load(i_slope.at[l], slope),
            weights=load(i_weights.at[l, :, :, :, :, cols], w.at[:, :, :, :, cols]),
            normed_b=load(i_normed_b.at[l], normed_b),
        )

    def load_attention(l):
        cols = slice(c_qkv[0], c_out[1])
        return dict(
            mixed=load(i_mixed.at[l], mixed),
            weights=load(i_weights.at[l, :, :, :, :, cols], w.at[:, :, :, :, cols]),
            qkv=load(i_qkv.at[l], qkv),
            log=load(i_log.at[l], log_total),
            normed_a=load(i_normed_a.at[l], normed_a),
        )

    top = layers - 1
    cols = slice(c_up[0], c_down[1])
    ready = load(i_grads, (g0, g1)[top].at[:, :, :, :, cols])
    up_cols = slice(*c_up)
    mlp = dict(
        slope=load(i_slope.at[top], slope),
        weights=load(i_weights.at[top, :, :, :, :, up_cols], w.at[:, :, :, :, up_cols]),
        rounded=load(i_rounded, rounded),
        middle=load(i_middle.at[top], kept),
    )
    att = load_attention(top)
    p.barrier()
    own_rows = pl.ds(pl.multiple_of(p.core * half, half), half)
    encode_segments(counts, slots, qe, ke)
    norm_sums = [small[layer][4] for layer in range(layers)]
    by_row[...] = jnp.zeros_like(by_row)
    for sums in norm_sums:
        sums[...] = jnp.zeros_like(sums)
    exchange = Exchange(p, sender, x_out, x_in)
    grads = (g0, g1)
    starts = list(range(c_down[0], c_down[1], GROUP)) + list(range(c_up[0], c_up[1], GROUP))
    starts += list(range(c_out[0], c_out[1], GROUP)) + list(range(c_qkv[0], c_qkv[1], GROUP))
    starts = [(l, low) for l in reversed(range(layers)) for low in starts]
    groups = [
        [(layer, a, b, order[::-1]) for layer, a, b, order in parts_of(l, low, turn)]
        for turn, (l, low) in enumerate(starts)
    ]
    columns_of_layer = [small[layer][0] for layer in range(layers)]
    scatter = Scatter(
        p, sender, grads, groups, buffers, o_pieces, cuts, by_row, columns_of_layer
    )
    ready.wait()
    for _ in range(2 * (c_up[1] - c_up[0]) // GROUP):
        scatter.offer()
    scatter.burst()
    mlp["rounded"].wait()

    def norm_step(layer, which, at, total):
        hat, rise = normalised(kept[at, :])
        norm_sums[layer][which : which + 1, :] += jnp.sum(total * hat, axis=0, keepdims=True)
        norm_sums[layer][which + 1 : which + 2, :] += jnp.sum(total, axis=0, keepdims=True)
        d_hat = total * norms[layer, which : which + 1, :]
        flat_mean = jnp.mean(d_hat, axis=-1, keepdims=True)
        hat_mean = jnp.mean(d_hat * hat, axis=-1, keepdims=True)
        value = grad[at, :] + rise * (d_hat - flat_mean - hat * hat_mean)
        grad[at, :] = value
        rounded[at, :] = value.astype(BF16)

    def widen_step(at):
        grad[at, :] = rounded[at, :].astype(F32)

    row_tiles(length, widen_step)
    for layer in reversed(range(layers)):
        if layer < top:
            turned[...] = rounded[...].T
            mlp["active"].wait()
            for low in range(c_down[0], c_down[1], GROUP):
                cols = slice(low - c_down[0], low - c_down[0] + GROUP)
                store(grads[layer], low, dot(turned[...], active[:, cols], NN))
                scatter.offer()
                if low % (2 * GROUP):
                    scatter.poll()
            mlp["weights"].wait()
            mlp["slope"].wait()
            for low in range(c_down[0], c_down[1], GROUP):
                cols = slice(low - c_down[0], low - c_down[0] + GROUP)
                d_active = dot(rounded[...], flat(w, low, low + GROUP), NN)
                slope[:, cols] = (d_active * slope[:, cols].astype(F32)).astype(BF16)
                if low % (2 * GROUP):
                    scatter.poll()
        else:
            mlp["weights"].wait()
            mlp["slope"].wait()
        w_up = flat(w, *c_up)
        exchange.send(lambda low, high: dot(slope[low:high, :], w_up, NT))
        scatter.poll()
        if layer < top:
            mlp["normed_b"].wait()
            turned[...] = normed_b[...].T
            for low in range(c_up[0], c_up[1], GROUP):
                cols = slice(low - c_up[0], low - c_up[0] + GROUP)
                store(grads[layer], low, dot(turned[...], slope[:, cols], NN))
                scatter.offer()
                if low % (2 * GROUP):
                    scatter.poll()
        mlp["middle"].wait()
        exchange.take(lambda at, total: norm_step(layer, 2, at, total), scatter.poll)
        rows_load = load(i_rows.at[layer], kept)
        if layer:
            mlp = load_mlp(layer - 1)
        scatter.poll()
        turned[...] = rounded[...].T
        att["mixed"].wait()
        store(grads[layer], c_out[0], dot(turned[...], mixed[...], NN))
        scatter.offer()
        att["weights"].wait()
        mixed[...] = dot(rounded[...], flat(w, *c_out), NN).astype(BF16)
        scatter.poll()
        att["qkv"].wait()
        att["log"].wait()
        attention_backward(qkv, qe, ke, log_total, mixed, scatter.poll)
        w_qkv = flat(w, *c_qkv)
        exchange.send(lambda low, high: dot(qkv[low:high, :], w_qkv, NT))
        att["normed_a"].wait()
        turned[...] = normed_a[...].T
        for low in range(c_qkv[0], c_qkv[1], GROUP):
            store(grads[layer], low, dot(turned[...], qkv[:, low : low + GROUP], NN))
            scatter.offer()
        scatter.poll()
        rows_load.wait()
        exchange.take(lambda at, total: norm_step(layer, 0, at, total), scatter.poll)
        if layer:
            mlp["middle"] = load(i_middle.at[layer - 1], kept)
            att = load_attention(layer - 1)
        scatter.poll()
    o_input[...] = grad[own_rows, :]
    rounds = Rounds(p, sender)
    in_plane, in_z = {}, {}

    def small_plane(layer):
        col, _, col_plane, _, norm, _, norm_plane, _ = small[layer]
        in_plane[layer] = (rounds.plane(col, col_plane), rounds.plane(norm, norm_plane))

    def small_z(layer):
        _, col, col_plane, col_z, _, norm, norm_plane, norm_z = small[layer]
        col[...] = slot_sum(in_plane[layer][0], col_plane)
        first = rounds.along_z(col, col_z)
        norm[...] = slot_sum(in_plane[layer][1], norm_plane)
        in_z[layer] = (first, rounds.along_z(norm, norm_z))

    while scatter.flying or scatter.started < len(groups):
        scatter.poll(1)
        if in_plane and not in_z:
            small_z(1)
        if not in_plane and min(scatter.flying, default=len(groups)) >= len(groups) // 2:
            small_plane(1)
    if not in_z:
        small_z(1)
    scatter.drain()
    small_plane(0)
    lane = lax.broadcasted_iota(jnp.int32, (1, 128), 1)
    entries = [(layer, which) for layer in range(layers) for which in range(4)]
    columns_of = (None, out_c, up_c, down_c)

    def old_columns(layer, which):
        if which == 0:
            return jnp.concatenate([qkv_c[part, layer : layer + 1, :] for part in range(3)], axis=1)
        return columns_of[which][layer : layer + 1, :]

    swap = sender.start(by_row, row_in, p.over_core())
    square[...] = jnp.zeros_like(square)
    olds = jnp.zeros((1, 128), F32)
    for at, (layer, which) in enumerate(entries):
        old = row_states[which][layer : layer + 1, :]
        square[at : at + 1, 0 : old.shape[1]] = old
        share = 0.5
        if which % 2:
            old, share = old_columns(layer, which), 1.0 / n_dp
        olds = olds + jnp.where(lane == 16 + at, jnp.sum(old, axis=1, keepdims=True) * share, 0.0)
    depth = o_pieces.shape[1]
    width = norm_state.shape[2]
    few_term, few_mid, few_plane, few_z = few
    sums = jnp.sum(by_row[...], axis=0, keepdims=True) + olds + pltpu.roll(squares[...], 8, 1)
    few_term[...] = jnp.broadcast_to(sums, few_term.shape)
    few_plane_copies = rounds.plane(few_term, few_plane, True)
    old_rows = square[...].T[0:depth, :]
    small_z(0)
    few_mid[...] = slot_sum(few_plane_copies, few_plane)
    few_z_copies = rounds.along_z(few_mid, few_z)
    swap.wait_recv()
    counts_of = jnp.ones((1, 128), F32)
    for at, (layer, which) in enumerate(entries):
        counts_of = jnp.where(lane == at, 1.0 / totals[which], counts_of)
    new_rows = DECAY * old_rows + (1.0 - DECAY) * (by_row[...] + row_in[...]) * counts_of
    square[...] = jnp.zeros_like(square)
    square[0:depth, :] = new_rows
    o_rows[...] = square[...].T
    by_row_rise = lax.rsqrt(new_rows)
    columns = []
    for layer in range(layers):
        columns.append(slot_sum(in_z[layer][0], small[layer][3]))
    norm_totals = [slot_sum(in_z[layer][1], small[layer][7]) for layer in range(layers)]
    scalars = slot_sum(few_z_copies, few_z)[0:1, :]
    o_scalars[...] = scalars
    steps = jnp.zeros((1, 128), F32)
    for at, (layer, which) in enumerate(entries):
        low, high = cuts[which]
        fresh = columns[layer][:, low:high]
        new_cols = DECAY * old_columns(layer, which) + (1.0 - DECAY) / D * fresh
        o_columns[layer, :, low:high] = new_cols
        mean = row_mean(scalars, at, which, totals)
        by_col = lax.rsqrt(new_cols)
        step = o_pieces[layer, :, low:high] * by_row_rise[:, at : at + 1] * by_col
        steps = steps + jnp.where(lane == at, grand_total(step * step) * mean, 0.0)
    both = norm_totals + [norms[layer] for layer in range(layers)]
    both.append(jnp.zeros((128 - 16, D), F32))
    tall[...] = jnp.concatenate(both, axis=0).T
    me = p.z * 4 + p.y * 2 + p.x
    square[0:depth, :] = tall[pl.ds(pl.multiple_of(me * depth, 8), depth), :]
    o_own[...] = square[...].T
    for layer in range(layers):
        mine = o_own[layer * 4 : layer * 4 + 4, 0:width]
        state = DECAY * norm_state[layer] + (1.0 - DECAY) * (mine * mine + EPS_SQUARE)
        sizes = jnp.sum(mine * mine / state, axis=1, keepdims=True) * 0.5
        for kind in range(4):
            steps = steps + jnp.where(lane == 8 + layer * 4 + kind, sizes[kind : kind + 1], 0.0)
    last_term, last_mid, last_plane, last_z = last
    last_term[...] = jnp.broadcast_to(steps, last_term.shape)
    last_copies = rounds.plane(last_term, last_plane, True)
    last_mid[...] = slot_sum(last_copies, last_plane)
    last_copies = rounds.along_z(last_mid, last_z)
    o_steps[...] = slot_sum(last_copies, last_z)[0:1, :]
    sender.drain()


def row_mean(scalars, at, which, totals):
    count = totals[3] if which == 3 else D
    mean = DECAY * scalars[:, 16 + at : 17 + at] / count
    return mean + (1.0 - DECAY) * scalars[:, at : at + 1] / (D * totals[which])


def apply_kernel(
    cuts, totals,
    result, grad, sums, rows, columns, scalars, steps, own, qkv_w, out_w, up_w, down_w, norms,
    norm_state,
    o_result, o_grad, g_qkv, g_out, g_up, g_down, g_norm, n_qkv, n_out, n_up, n_down, n_norm,
    k_qkv, k_out, k_up, k_down,
    qkv_rn, qkv_cn, out_rn, out_cn, up_rn, up_cn, down_rn, down_cn, moments_a, moments_f, rms,
    square,
):
    layers, depth = sums.shape[0], sums.shape[1]
    width, local = norm_state.shape[2], qkv_w.shape[3]
    o_result[...] = result[...]
    o_grad[...] = grad[...]
    lane = lax.broadcasted_iota(jnp.int32, (1, 128), 1)
    entries = [(layer, which) for layer in range(layers) for which in range(4)]
    means = jnp.ones((1, 128), F32)
    for at, (layer, which) in enumerate(entries):
        means = jnp.where(lane == at, 1.0 / (D * totals[which]), means)
        means = jnp.where(lane == 8 + at, 1.0 / D, means)
    size = jnp.sqrt(steps[...] * means)
    shrink = 1.0 / jnp.maximum(1.0, size / CLIP)
    row_news = (qkv_rn, out_cn, up_rn, down_cn)
    square[...] = rows[...].T
    by_row = lax.rsqrt(square[0:depth, :])
    for layer in range(layers):
        rms[layer : layer + 1, 0:4] = size[:, layer * 4 : layer * 4 + 4]
        rms[layer : layer + 1, 4:8] = size[:, 8 + layer * 4 : 12 + layer * 4]
        vectors = norms[layer]
        scale = jnp.sqrt(jnp.mean(vectors * vectors, axis=1, keepdims=True) + 1e-06)
        shrinks = jnp.concatenate(
            [shrink[:, 8 + layer * 4 + kind : 9 + layer * 4 + kind] for kind in range(4)], axis=0
        )
        mine = own[layer * 4 : layer * 4 + 4, 0:width]
        state = DECAY * norm_state[layer] + (1.0 - DECAY) * (mine * mine + EPS_SQUARE)
        g_norm[layer] = mine
        moments_a[layer] = state[0:2]
        moments_f[layer] = state[2:4]
        before = own[8 + layer * 4 : 12 + layer * 4, 0:width]
        n_norm[layer] = before - RATE * scale * (mine * lax.rsqrt(state) * shrinks)
    for at, (layer, which) in enumerate(entries):
        row_news[which][layer : layer + 1, :] = rows[at : at + 1, 0:depth]
        scale = jnp.sqrt(scalars[:, 8 + at : 9 + at] / (D * totals[which]) + 1e-06)
        factor = RATE * scale * shrink[:, at : at + 1]
        factor = factor * jnp.sqrt(row_mean(scalars[...], at, which, totals))
        factor = factor * by_row[:, at : at + 1]
        for part in range(3 if which == 0 else 1):
            low, high = cuts[which]
            if which == 0:
                low, high = part * local, part * local + local
                refs = [ref.at[layer, part] for ref in (qkv_w, g_qkv, n_qkv, k_qkv)]
                qkv_cn[part, layer : layer + 1, :] = columns[layer, :, low:high]
            else:
                table = (
                    (out_w, g_out, n_out, k_out),
                    (up_w, g_up, n_up, k_up),
                    (down_w, g_down, n_down, k_down),
                )
                refs = [ref.at[layer] for ref in table[which - 1]]
                new_ref = (out_rn, up_cn, down_rn)[which - 1]
                new_ref[layer : layer + 1, :] = columns[layer, :, low:high]
            grad_piece = sums[layer, :, low:high]
            new = refs[0][...] - grad_piece * factor * lax.rsqrt(columns[layer, :, low:high])
            refs[1][...] = grad_piece
            refs[2][...] = new
            refs[3][...] = new.astype(BF16)


def passes_by_xla(
    patches,
    cotangent,
    patch_counts,
    qkv_weight,
    out_weight,
    up_weight,
    down_weight,
    norms,
):
    layers = qkv_weight.shape[0]
    half = patches.shape[0]
    length = half * lax.axis_size("mp")
    same, live_all = segments(patch_counts, length)
    live = lax.dynamic_slice_in_dim(live_all, lax.axis_index("mp") * half, half)
    rows = patches.astype(jnp.float32)
    kept = []
    for layer in range(layers):
        pieces = (
            qkv_weight[layer].astype(jnp.bfloat16),
            out_weight[layer].astype(jnp.bfloat16),
            up_weight[layer].astype(jnp.bfloat16),
            down_weight[layer].astype(jnp.bfloat16),
        )
        whole = (
            lax.all_gather(pieces[0], "dp", axis=0, tiled=True),
            lax.all_gather(pieces[1], "dp", axis=1, tiled=True),
            lax.all_gather(pieces[2], "dp", axis=0, tiled=True),
            lax.all_gather(pieces[3], "dp", axis=1, tiled=True),
        )
        w_qkv, w_out, w_up, w_down = whole
        local = w_qkv.shape[2]
        normed_a = spread_rows(
            layer_norm(rows, norms[layer, 0], norms[layer, 1]).astype(jnp.bfloat16)
        )
        qkv = jnp.dot(normed_a, w_qkv.reshape(D, 3 * local), preferred_element_type=jnp.float32)
        qkv = qkv.astype(jnp.bfloat16).reshape(length, 3, local // HEAD_DIM, HEAD_DIM)
        mixed, log_total = attend(qkv, same)
        mixed = mixed.astype(jnp.bfloat16)
        middle = rows + lax.psum_scatter(
            jnp.dot(mixed, w_out, preferred_element_type=jnp.float32).astype(jnp.bfloat16),
            "mp",
            scatter_dimension=0,
            tiled=True,
        ).astype(jnp.float32)
        normed_b = spread_rows(
            layer_norm(middle, norms[layer, 2], norms[layer, 3]).astype(jnp.bfloat16)
        )
        hidden = jnp.dot(normed_b, w_up, preferred_element_type=jnp.float32)
        active = exact_gelu(hidden).astype(jnp.bfloat16)
        after = middle + lax.psum_scatter(
            jnp.dot(active, w_down, preferred_element_type=jnp.float32).astype(jnp.bfloat16),
            "mp",
            scatter_dimension=0,
            tiled=True,
        ).astype(jnp.float32)
        stored = None
        kept.append(
            (
                rows,
                normed_a,
                qkv,
                log_total,
                mixed,
                middle,
                normed_b,
                hidden,
                active,
                stored,
                pieces,
            )
        )
        rows = after
    activations = rows.astype(jnp.bfloat16)
    grad = cotangent.astype(jnp.float32) * live[:, None]
    reduced = [None] * layers
    for layer in reversed(range(layers)):
        (
            rows_in,
            normed_a,
            qkv,
            log_total,
            mixed,
            middle,
            normed_b,
            hidden,
            active,
            stored,
            pieces,
        ) = kept[layer]
        whole = (
            lax.all_gather(pieces[0], "dp", axis=0, tiled=True),
            lax.all_gather(pieces[1], "dp", axis=1, tiled=True),
            lax.all_gather(pieces[2], "dp", axis=0, tiled=True),
            lax.all_gather(pieces[3], "dp", axis=1, tiled=True),
        )
        w_qkv, w_out, w_up, w_down = whole
        local = w_qkv.shape[2]
        grad_down = spread_rows(grad.astype(jnp.bfloat16))
        g_down = jnp.einsum("tf,td->fd", active, grad_down, preferred_element_type=jnp.float32)
        d_active = jnp.einsum("td,fd->tf", grad_down, w_down, preferred_element_type=jnp.float32)
        gelu_value, gelu_back = jax.vjp(exact_gelu, hidden)
        d_hidden = gelu_back(d_active)[0].astype(jnp.bfloat16)
        g_up = jnp.einsum("td,tf->df", normed_b, d_hidden, preferred_element_type=jnp.float32)
        d_normed_b = lax.psum_scatter(
            jnp.einsum("tf,df->td", d_hidden, w_up, preferred_element_type=jnp.float32).astype(
                jnp.bfloat16
            ),
            "mp",
            scatter_dimension=0,
            tiled=True,
        ).astype(jnp.float32)
        d_middle, g_gain_b, g_shift_b = norm_back(
            middle, norms[layer, 2], norms[layer, 3], d_normed_b
        )
        grad_mid = grad + d_middle
        grad_out = spread_rows(grad_mid.astype(jnp.bfloat16))
        g_out = jnp.einsum("tc,td->cd", mixed, grad_out, preferred_element_type=jnp.float32)
        d_mixed = jnp.einsum(
            "td,cd->tc", grad_out, w_out, preferred_element_type=jnp.float32
        ).astype(jnp.bfloat16)
        d_qkv = attend_back(
            qkv, same, log_total, d_mixed.reshape(length, local // HEAD_DIM, HEAD_DIM)
        )
        d_qkv = d_qkv.reshape(length, 3 * local)
        g_qkv = jnp.einsum(
            "td,tc->dc", normed_a, d_qkv, preferred_element_type=jnp.float32
        ).reshape(D, 3, local)
        d_normed_a = lax.psum_scatter(
            jnp.einsum(
                "tc,dc->td", d_qkv, w_qkv.reshape(D, 3 * local), preferred_element_type=jnp.float32
            ).astype(jnp.bfloat16),
            "mp",
            scatter_dimension=0,
            tiled=True,
        ).astype(jnp.float32)
        d_input, g_gain_a, g_shift_a = norm_back(
            rows_in, norms[layer, 0], norms[layer, 1], d_normed_a
        )
        grad = grad_mid + d_input
        norm_terms = jnp.stack([g_gain_a, g_shift_a, g_gain_b, g_shift_b])
        reduced[layer] = (
            lax.psum_scatter(g_qkv, "dp", scatter_dimension=0, tiled=True),
            lax.psum_scatter(g_out, "dp", scatter_dimension=1, tiled=True),
            lax.psum_scatter(g_up, "dp", scatter_dimension=0, tiled=True),
            lax.psum_scatter(g_down, "dp", scatter_dimension=1, tiled=True),
            lax.psum(norm_terms, "mp"),
        )
    return activations, grad, [item[:4] for item in reduced], jnp.stack([item[4] for item in reduced])


def step_by_kernels(
    patches,
    cotangent,
    patch_counts,
    qkv_weight,
    out_weight,
    up_weight,
    down_weight,
    norms,
    qkv_rows,
    qkv_cols,
    out_rows,
    out_cols,
    up_rows,
    up_cols,
    down_rows,
    down_cols,
    norm_state,
):
    layers, depth, _, local = qkv_weight.shape
    n_dp = lax.axis_size("dp")
    nz, half, wide = n_dp // 4, patches.shape[0], up_weight.shape[2]
    length, slots = 2 * half, patch_counts.shape[0]
    ends = [0, 3 * local, 4 * local, 4 * local + wide, 4 * local + 2 * wide]
    cuts = tuple(zip(ends[:-1], ends[1:]))
    totals = tuple(2.0 * (high - low) for low, high in cuts)
    columns, n_groups = ends[-1], layers * ends[-1] // GROUP
    masters = (
        qkv_weight.transpose(0, 2, 1, 3),
        out_weight.transpose(0, 2, 1),
        up_weight,
        down_weight.transpose(0, 2, 1),
    )
    states_by_row = (qkv_rows, out_cols, up_rows, down_cols)
    states_by_column = (qkv_cols.transpose(1, 0, 2), out_rows, up_cols, down_rows)
    vmem, smem, hbm = [
        pl.BlockSpec(memory_space=space) for space in (pltpu.VMEM, pltpu.SMEM, pl.ANY)
    ]
    shape = jax.ShapeDtypeStruct
    whole = (nz, 2, 2, depth, columns)
    mlp_part = (nz, 2, 2, depth, 2 * wide)
    rows_f32, rows_bf16 = ((length, D), F32), ((length, D), BF16)
    kept = [
        rows_f32,
        rows_f32,
        rows_bf16,
        ((length, 3 * local), BF16),
        ((length, local), BF16),
        rows_bf16,
        ((length, wide), BF16),
        ((length, wide), BF16),
        ((8, length), F32),
    ]
    saved = [shape((layers,) + dims, kind) for dims, kind in kept]
    line = shape((1, 128), F32)
    sems = [
        pltpu.SemaphoreType.DMA((420,)),
        pltpu.SemaphoreType.DMA((420,)),
        pltpu.SemaphoreType.DMA((48,)),
    ]
    codes = [pltpu.VMEM((length, 128), BF16)] * 2
    swaps = [pltpu.VMEM((2, length, D), BF16)] * 2

    def around(dims, plane):
        return [pltpu.VMEM(dims, F32)] * 2 + [
            pltpu.VMEM((places,) + dims, F32) for places in (plane, nz)
        ]

    outs = pl.pallas_call(
        functools.partial(forward_kernel, n_dp, cuts, slots),
        out_shape=[shape((layers,) + whole, BF16)]
        + saved
        + [shape((length, D), BF16), shape(mlp_part, BF16), shape((half, D), BF16), line],
        in_specs=[smem] + [vmem] * 7,
        out_specs=[hbm] * (3 + len(saved)) + [vmem] * 2,
        scratch_shapes=[pltpu.VMEM(whole, BF16)] * layers
        + [
            pltpu.VMEM(mlp_part, BF16),
            pltpu.VMEM((length, D), BF16),
            pltpu.VMEM((D, length), BF16),
        ]
        + [pltpu.VMEM((layers,) + dims, kind) for dims, kind in kept]
        + [pltpu.VMEM((length, D), F32)]
        + swaps
        + codes
        + sems,
        compiler_params=pltpu.CompilerParams(
            collective_id=0, has_side_effects=True, vmem_limit_bytes=VMEM_BYTES
        ),
        name="forward",
    )(patch_counts, patches, cotangent, *masters, norms)
    saved, activations, squares = outs[:-2], outs[-2], outs[-1]
    buffers = {}
    for width, order in PATHS[0] + PATHS[1]:
        sizes, refs = dict(z=nz, y=2, x=2), {}
        for axis in order[::-1]:
            sizes.pop(axis)
            dims = (nz,) if axis == "z" else ()
            dims += tuple(sizes.values()) + (depth, width)
            refs[axis] = pltpu.VMEM((n_groups // layers // 2,) + dims, BF16)
        buffers[order[::-1]] = refs
    small = around((1, columns), 4) + around((4, D), 4)
    grad, sums, rows, fresh, scalars, steps, norm_own = pl.pallas_call(
        functools.partial(backward_kernel, n_dp, cuts, totals, slots),
        out_shape=[
            shape((half, D), F32),
            shape((layers, depth, columns), F32),
            shape((128, 128), F32),
            shape((layers, 1, columns), F32),
            line,
            line,
            shape((128, 128), F32),
        ],
        in_specs=[smem] + [vmem] * 2 + [(vmem,) * 4] + [vmem] * 5 + [hbm] * len(saved),
        out_specs=[vmem] * 7,
        scratch_shapes=[pltpu.VMEM(whole, BF16)] * layers
        + [buffers]
        + [pltpu.VMEM(whole, BF16)]
        + [pltpu.VMEM(dims, kind) for dims, kind in kept[1:]]
        + [
            pltpu.VMEM((length, D), F32),
            pltpu.VMEM((length, D), BF16),
            pltpu.VMEM((D, length), BF16),
        ]
        + swaps
        + codes
        + [pltpu.VMEM((depth, 128), F32)] * 2
        + [pltpu.VMEM((128, 128), F32), pltpu.VMEM((D, 128), F32)]
        + [[small] * layers, around((8, 128), 8), around((8, 128), 8)]
        + sems,
        compiler_params=pltpu.CompilerParams(
            collective_id=1, has_side_effects=True, vmem_limit_bytes=VMEM_BYTES
        ),
        name="backward",
    )(
        patch_counts,
        norms,
        squares,
        states_by_row,
        *states_by_column,
        norm_state,
        *saved,
    )
    like = lambda arrays, kind: [shape(array.shape, kind) for array in arrays]
    vectors = [shape(norm_state.shape, F32)]
    states = (
        qkv_rows, states_by_column[0], out_rows, out_cols,
        up_rows, up_cols, down_rows, down_cols,
    )
    results = [shape((half, D), BF16), shape((half, D), F32)]
    results += like(masters, F32) + vectors + like(masters, F32) + vectors + like(masters, BF16)
    results += like(states, F32)
    results += [shape((layers, 2, norm_state.shape[2]), F32)] * 2 + [shape((layers, 8), F32)]
    out = pl.pallas_call(
        functools.partial(apply_kernel, cuts, totals),
        out_shape=results,
        in_specs=[vmem] * 14,
        out_specs=[vmem] * len(results),
        scratch_shapes=[pltpu.VMEM((128, 128), F32)],
        compiler_params=pltpu.CompilerParams(vmem_limit_bytes=VMEM_BYTES),
        name="apply",
    )(
        activations, grad, sums, rows, fresh, scalars, steps, norm_own, *masters, norms, norm_state
    )
    out = list(out)
    for at in (2, 7, 12):
        out[at] = out[at].transpose(0, 2, 1, 3)
        out[at + 1] = out[at + 1].transpose(0, 2, 1)
        out[at + 3] = out[at + 3].transpose(0, 2, 1)
    out[17] = out[17].transpose(1, 0, 2)
    return tuple(out)


def kernels_fit(patches, qkv_weight):
    length = 2 * patches.shape[0]
    depth, local = qkv_weight.shape[1], qkv_weight.shape[3]
    return (
        lax.axis_size("mp") == 2
        and lax.axis_size("dp") % 4 == 0
        and depth % 16 == 0
        and length % TILE == 0
        and (4 * local) % GROUP == 0
    )


def per_device(*arrays):
    if kernels_fit(arrays[0], arrays[3]):
        return step_by_kernels(*arrays)
    return step_by_xla(*arrays)


def step_by_xla(
    patches,
    cotangent,
    patch_counts,
    qkv_weight,
    out_weight,
    up_weight,
    down_weight,
    norms,
    qkv_rows,
    qkv_cols,
    out_rows,
    out_cols,
    up_rows,
    up_cols,
    down_rows,
    down_cols,
    norm_state,
):
    layers = qkv_weight.shape[0]
    activations, grad, reduced, norm_terms = passes_by_xla(
        patches, cotangent, patch_counts, qkv_weight, out_weight, up_weight, down_weight, norms
    )
    col_axes = ("mp", "dp", "mp", "dp")
    row_counts = (D, D, D, FF)
    col_counts = (3 * D, D, FF, D)
    masters = (qkv_weight, out_weight, up_weight, down_weight)
    row_states = (qkv_rows, out_rows, up_rows, down_rows)
    col_states = (qkv_cols, out_cols, up_cols, down_cols)
    entries = [(layer, which) for layer in range(layers) for which in range(4)]
    grads = [reduced[layer][which] for layer, which in entries]
    row_olds = [row_states[which][layer] for layer, which in entries]
    col_olds = [col_states[which][layer] for layer, which in entries]
    width = norm_state.shape[2]
    row_parts, col_parts = ([], [])
    for position, (layer, which) in enumerate(entries):
        matrix = grads[position].reshape(grads[position].shape[0], -1)
        square = matrix * matrix + EPS_SQUARE
        row_parts.append(jnp.sum(square, axis=1))
        col_parts.append(jnp.sum(square, axis=0).reshape(col_olds[position].shape))
    model_side = tuple(
        [
            row_parts[position] if col_axes[which] == "mp" else col_parts[position]
            for position, (layer, which) in enumerate(entries)
        ]
    )
    data_side = tuple(
        (
            col_parts[position] if col_axes[which] == "mp" else row_parts[position]
            for position, (layer, which) in enumerate(entries)
        )
    ) + (norm_terms,)
    model_sums = jax.tree.map(
        lambda part: part.astype(jnp.float32), lax.psum(for_sending(model_side), "mp")
    )
    data_sums = lax.psum(data_side, "dp")
    norm_grad = lax.dynamic_slice_in_dim(
        data_sums[len(entries)], lax.axis_index("dp") * width, width, 2
    )
    row_sums = [
        model_sums[position] if col_axes[which] == "mp" else data_sums[position]
        for position, (layer, which) in enumerate(entries)
    ]
    col_sums = [
        data_sums[position] if col_axes[which] == "mp" else model_sums[position]
        for position, (layer, which) in enumerate(entries)
    ]
    row_news = [
        DECAY * row_olds[position] + (1.0 - DECAY) * row_sums[position] / col_counts[which]
        for position, (layer, which) in enumerate(entries)
    ]
    shares = jnp.stack(
        [
            jnp.sum(row_news[position]) / size_of(col_axes[which])
            for position, (layer, which) in enumerate(entries)
        ]
    )
    row_totals = lax.psum(shares, ("dp", "mp"))
    row_means = [
        row_totals[position] / row_counts[which] for position, (layer, which) in enumerate(entries)
    ]
    col_news = [
        DECAY * col_olds[position] + (1.0 - DECAY) * col_sums[position] / row_counts[which]
        for position, (layer, which) in enumerate(entries)
    ]
    directions, step_parts, weight_parts = ([], [], [])
    for position, (layer, which) in enumerate(entries):
        matrix = grads[position].reshape(grads[position].shape[0], -1)
        second = (
            row_news[position][:, None] * col_news[position].reshape(1, -1) / row_means[position]
        )
        direction = matrix * lax.rsqrt(second)
        directions.append(direction)
        step_parts.append(jnp.sum(direction * direction))
        master = masters[which][layer]
        weight_parts.append(jnp.sum(master * master))
    own_norms = lax.dynamic_slice_in_dim(norms, lax.axis_index("dp") * width, width, 2)
    norm_state_new = DECAY * norm_state + (1.0 - DECAY) * (norm_grad * norm_grad + EPS_SQUARE)
    norm_dirs = norm_grad * lax.rsqrt(norm_state_new)
    norm_parts = jnp.sum(norm_dirs * norm_dirs, axis=2) / lax.axis_size("mp")
    step_all = jnp.concatenate(
        [jnp.stack(step_parts).reshape(layers, 4), norm_parts], axis=1
    ).reshape(-1)
    step_total, weight_total = lax.psum((step_all, jnp.stack(weight_parts)), ("dp", "mp"))
    step_total = step_total.reshape(layers, 8)
    matrix_counts = jnp.asarray(
        [float(row_counts[which] * col_counts[which]) for which in range(4)], jnp.float32
    )
    update_rms = jnp.concatenate(
        [jnp.sqrt(step_total[:, :4] / matrix_counts[None, :]), jnp.sqrt(step_total[:, 4:] / D)],
        axis=1,
    )
    news = [[None] * layers for which in range(4)]
    rows_new = [[None] * layers for which in range(4)]
    cols_new = [[None] * layers for which in range(4)]
    for position, (layer, which) in enumerate(entries):
        master = masters[which][layer]
        scale = jnp.sqrt(weight_total[position] / (row_counts[which] * col_counts[which]) + 1e-06)
        clipped = directions[position] / jnp.maximum(1.0, update_rms[layer, which] / CLIP)
        news[which][layer] = master - RATE * scale * clipped.reshape(master.shape)
        rows_new[which][layer] = row_news[position]
        cols_new[which][layer] = col_news[position]
    norm_scale = jnp.sqrt(jnp.mean(norms * norms, axis=2) + 1e-06)
    norm_clipped = norm_dirs / jnp.maximum(1.0, update_rms[:, 4:] / CLIP)[:, :, None]
    norm_new = own_norms - RATE * norm_scale[:, :, None] * norm_clipped
    grad_out = [jnp.stack([reduced[layer][which] for layer in range(layers)]) for which in range(4)]
    new_out = [jnp.stack(news[which]) for which in range(4)]
    row_out = [jnp.stack(rows_new[which]) for which in range(4)]
    col_out = [jnp.stack(cols_new[which]) for which in range(4)]
    return (
        activations,
        grad,
        grad_out[0],
        grad_out[1],
        grad_out[2],
        grad_out[3],
        norm_grad,
        new_out[0],
        new_out[1],
        new_out[2],
        new_out[3],
        norm_new,
        new_out[0].astype(jnp.bfloat16),
        new_out[1].astype(jnp.bfloat16),
        new_out[2].astype(jnp.bfloat16),
        new_out[3].astype(jnp.bfloat16),
        row_out[0],
        col_out[0],
        row_out[1],
        col_out[1],
        row_out[2],
        col_out[2],
        row_out[3],
        col_out[3],
        norm_state_new[:, 0:2],
        norm_state_new[:, 2:4],
        update_rms,
    )


def solution(mesh):
    in_specs = (
        P(("dp", "mp"), None),
        P(("dp", "mp"), None),
        P("dp"),
        P(None, "dp", None, "mp"),
        P(None, "mp", "dp"),
        P(None, "dp", "mp"),
        P(None, "mp", "dp"),
        P(),
        P(None, "dp"),
        P(None, None, "mp"),
        P(None, "mp"),
        P(None, "dp"),
        P(None, "dp"),
        P(None, "mp"),
        P(None, "mp"),
        P(None, "dp"),
        P(None, None, "dp"),
    )
    out_specs = (
        P(("dp", "mp"), None),
        P(("dp", "mp"), None),
        P(None, "dp", None, "mp"),
        P(None, "mp", "dp"),
        P(None, "dp", "mp"),
        P(None, "mp", "dp"),
        P(None, None, "dp"),
        P(None, "dp", None, "mp"),
        P(None, "mp", "dp"),
        P(None, "dp", "mp"),
        P(None, "mp", "dp"),
        P(None, None, "dp"),
        P(None, "dp", None, "mp"),
        P(None, "mp", "dp"),
        P(None, "dp", "mp"),
        P(None, "mp", "dp"),
        P(None, "dp"),
        P(None, None, "mp"),
        P(None, "mp"),
        P(None, "dp"),
        P(None, "dp"),
        P(None, "mp"),
        P(None, "mp"),
        P(None, "dp"),
        P(None, None, "dp"),
        P(None, None, "dp"),
        P(),
    )
    return jax.shard_map(
        per_device, mesh=mesh, in_specs=in_specs, out_specs=out_specs, check_vma=False
    )
```

```python
import functools

import jax
import jax.numpy as jnp
from jax import lax
from jax.experimental import pallas as pl
from jax.experimental.pallas import tpu as pltpu
from jax.sharding import PartitionSpec as P

D = 768
HEAD_DIM = 64
FF = 3072


DECAY = 0.5
EPS_SQUARE = 1e-30
CLIP = 0.25
RATE = 2.0
MASKED = -1e30


def for_sending(value):
    return jax.tree.map(lambda a: a.astype(jnp.bfloat16) if a.dtype == jnp.float32 else a, value)


def layer_norm(rows, gain, shift):
    centre = rows - jnp.mean(rows, axis=-1, keepdims=True)
    spread = jnp.mean(centre * centre, axis=-1, keepdims=True)
    return centre * lax.rsqrt(spread + 1e-06) * gain + shift


def norm_back(rows, gain, shift, grad):
    result, back = jax.vjp(layer_norm, rows, gain, shift)
    return back(grad)


def exact_gelu(values):
    return jax.nn.gelu(values, approximate=False)


def segments(counts, length):
    bounds = jnp.cumsum(counts)
    places = jnp.arange(length, dtype=jnp.int32)
    image = jnp.sum((places[:, None] >= bounds[None, :]).astype(jnp.int32), axis=1)
    live = (places < bounds[-1]).astype(jnp.float32)
    return (image[:, None] == image[None, :], live)


def attention_scores(query, keys, same):
    scale = query.shape[-1] ** (-0.5)
    scores = jnp.einsum("qhd,khd->hqk", query, keys, preferred_element_type=jnp.float32) * scale
    return jnp.where(same[None], scores, MASKED)


def attend(qkv, same):
    scores = attention_scores(qkv[:, 0], qkv[:, 1], same)
    top = jnp.max(scores, axis=-1, keepdims=True)
    raised = jnp.exp(scores - top)
    total = jnp.sum(raised, axis=-1, keepdims=True)
    probs = (raised / total).astype(jnp.bfloat16)
    mixed = jnp.einsum("hqk,khd->qhd", probs, qkv[:, 2], preferred_element_type=jnp.float32)
    return (mixed.reshape(mixed.shape[0], -1), top + jnp.log(total))


def attend_back(qkv, same, log_total, grad_mixed):
    query, keys, values = (qkv[:, 0], qkv[:, 1], qkv[:, 2])
    scale = query.shape[-1] ** (-0.5)
    probs = jnp.exp(attention_scores(query, keys, same) - log_total)
    d_values = jnp.einsum(
        "hqk,qhd->khd", probs.astype(jnp.bfloat16), grad_mixed, preferred_element_type=jnp.float32
    )
    d_probs = jnp.einsum("qhd,khd->hqk", grad_mixed, values, preferred_element_type=jnp.float32)
    d_scores = (probs * (d_probs - jnp.sum(probs * d_probs, axis=-1, keepdims=True))).astype(
        jnp.bfloat16
    )
    d_query = jnp.einsum("hqk,khd->qhd", d_scores, keys, preferred_element_type=jnp.float32) * scale
    d_keys = jnp.einsum("hqk,qhd->khd", d_scores, query, preferred_element_type=jnp.float32) * scale
    return jnp.stack([d_query, d_keys, d_values], axis=1).astype(jnp.bfloat16)


def spread_rows(values):
    return lax.all_gather(values, "mp", axis=0, tiled=True)


def size_of(name):
    return lax.axis_size("dp") if name == "dp" else lax.axis_size("mp")


TILE = 112
VMEM_BYTES = 64 << 20
LAG = 3
GROUP = 384
PATHS = (((128, "zyx"), (256, "xzy")), ((128, "zxy"), (256, "yzx")))
BIG = 1e30
MESH = pl.DeviceIdType.MESH
F32 = jnp.float32
BF16 = jnp.bfloat16
NN = ((1,), (0,))
NT = ((1,), (1,))
PLANE = [(dy, dx, dc) for dy in range(2) for dx in range(2) for dc in range(2)][1:]


def dot(left, right, dims):
    return lax.dot_general(left, right, (dims, ((), ())), preferred_element_type=F32)


class Place:
    def __init__(self, n_dp):
        self.nz = n_dp // 4
        me = lax.axis_index("dp")
        self.core = lax.axis_index("mp")
        self.z, self.y, self.x = me // 4, (me // 2) % 2, me % 2

    def at(self, z, y, x, core):
        return (z * 4 + y * 2 + x, core)

    def over_x(self):
        return self.at(self.z, self.y, 1 - self.x, self.core)

    def over_y(self):
        return self.at(self.z, 1 - self.y, self.x, self.core)

    def over_z(self, step):
        return self.at((self.z + step) % self.nz, self.y, self.x, self.core)

    def over_core(self):
        return self.at(self.z, self.y, self.x, 1 - self.core)

    def near(self, dy, dx, dc):
        return self.at(self.z, (self.y + dy) % 2, (self.x + dx) % 2, (self.core + dc) % 2)

    def greet(self):
        sem = pltpu.get_barrier_semaphore()
        others = [self.near(dy, dx, dc) for dy, dx, dc in PLANE]
        others += [self.over_z(step) for step in range(1, self.nz)]
        for other in others:
            pl.semaphore_signal(sem, inc=1, device_id=other, device_id_type=MESH)
        return lambda: pl.semaphore_wait(sem, len(others))


class Sender:
    def __init__(self, send_sems, recv_sems):
        self.send_sems, self.recv_sems = send_sems, recv_sems
        self.count = 0
        self.sent = []

    def make(self, src, dst, device, number=None):
        at = self.count
        self.count += 1
        return pltpu.make_async_remote_copy(
            src_ref=src,
            dst_ref=dst,
            send_sem=self.send_sems.at[at],
            recv_sem=self.recv_sems.at[at if number is None else number],
            device_id=device,
            device_id_type=MESH,
        )

    def start(self, src, dst, device):
        copy = self.make(src, dst, device)
        copy.start()
        self.sent.append(copy)
        return copy

    def drain(self):
        for copy in self.sent:
            copy.wait_send()
        self.sent = []


def parts_of(layer, low, turn):
    parts = []
    for width, order in PATHS[turn % 2]:
        parts.append((layer, low, low + width, order))
        low += width
    return parts


class Links:
    def __init__(self, place, sender):
        self.p, self.sender = place, sender
        self.inner = jnp.logical_or(place.z == 1, place.z == 2)
        self.copies = {}
        self.only_inner, self.only_outer = [], []

    def over_z_bit(self, bit):
        return self.p.at(self.p.z ^ bit, self.p.y, self.p.x, self.p.core)

    def steps(self, order):
        return order.replace("z", "zf")

    def over(self, axis):
        return self.p.over_x() if axis == "x" else self.p.over_y()

    def drain(self):
        @pl.when(self.inner)
        def _():
            for copy in self.only_inner:
                copy.wait_send()

        @pl.when(jnp.logical_not(self.inner))
        def _():
            for copy in self.only_outer:
                copy.wait_send()


class Gather(Links):
    def __init__(self, place, sender, weights, groups):
        super().__init__(place, sender)
        self.weights, self.groups = weights, groups
        self.started, self.clock = 0, 0
        self.flying = {}

    def view(self, part, done, z=None):
        layer, low, high, order = part
        p = self.p
        at_z = slice(None) if "z" in done else (p.z if z is None else z)
        at_y = slice(None) if "y" in done else p.y
        at_x = slice(None) if "x" in done else p.x
        return self.weights[layer].at[at_z, at_y, at_x, :, low:high]

    def stage(self, part, at):
        steps = self.steps(part[3])
        axis, done = steps[at], steps[:at].replace("f", "")
        before = self.copies.get((part, at - 1), ())
        if axis == "f":
            near, far, third, number = before
            far.wait_recv()
            piece = self.view(part, done.replace("z", ""), self.p.z ^ 2)
            onward = self.sender.make(piece, piece, self.over_z_bit(1), number)

            @pl.when(self.inner)
            def _():
                onward.start()

            self.only_inner.append(onward)
            self.copies[part, at] = [near, third]
            return
        for copy in before:
            copy.wait_recv()
        piece = self.view(part, done)
        if axis == "z":
            near = self.sender.start(piece, piece, self.over_z_bit(1))
            far = self.sender.start(piece, piece, self.over_z_bit(2))
            number = self.sender.count
            third = self.sender.make(piece, piece, self.over_z_bit(3))

            @pl.when(self.inner)
            def _():
                third.start()

            self.only_inner.append(third)
            self.copies[part, at] = (near, far, third, number)
        else:
            self.copies[part, at] = [self.sender.start(piece, piece, self.over(axis))]

    def poll(self, lag=1):
        self.clock += 1
        waiting = sorted(self.flying, reverse=True)
        if self.started < len(self.groups):
            for part in self.groups[self.started]:
                self.stage(part, 0)
            self.flying[self.started] = (1, self.clock)
            self.started += 1
        for k in waiting:
            step, since = self.flying[k]
            if step == 4 or self.clock - since < lag:
                continue
            for part in self.groups[k]:
                self.stage(part, step)
            self.flying[k] = (step + 1, self.clock)

    def ready(self, k):
        while k >= self.started or (k in self.flying and self.flying[k][0] < 4):
            self.poll(1)
        if k in self.flying:
            if self.flying[k][1] == self.clock and k + 1 < len(self.groups):
                self.poll(1)
            del self.flying[k]
            for part in self.groups[k]:
                for copy in self.copies.pop((part, 3)):
                    copy.wait_recv()


class Rounds:
    def __init__(self, place, sender):
        self.p, self.sender = place, sender

    def plane(self, term, slots, cores=False):
        p = self.p
        at = p.y * 2 + p.x
        at = at * 2 + p.core if cores else at
        slots[at] = term[...]
        return [
            self.sender.start(term, slots.at[at], p.near(dy, dx, dc))
            for dy, dx, dc in PLANE
            if cores or not dc
        ]

    def along_z(self, term, slots):
        p = self.p
        slots[p.z] = term[...]
        return [self.sender.start(term, slots.at[p.z], p.over_z(step)) for step in range(1, p.nz)]


def slot_sum(copies, slots):
    for copy in copies:
        copy.wait_recv()
    total = slots[0]
    for at in range(1, slots.shape[0]):
        total = total + slots[at]
    return total


class Scatter(Links):
    def __init__(
        self, place, sender, grads, groups, buffers, result, cuts, by_row, by_column
    ):
        super().__init__(place, sender)
        self.grads, self.groups, self.buffers, self.result = grads, groups, buffers, result
        self.cuts, self.by_row, self.by_column = cuts, by_row, by_column
        self.started, self.offered, self.clock = 0, 0, 0
        self.flying = {}

    def view(self, part, done, z=None, y=None, x=None):
        layer, low, high, order = part
        p = self.p
        at_z = slice(None) if z is None and "z" not in done else (p.z if z is None else z)
        at_y = slice(None) if y is None and "y" not in done else (p.y if y is None else y)
        at_x = slice(None) if x is None and "x" not in done else (p.x if x is None else x)
        return self.grads[layer].at[at_z, at_y, at_x, :, low:high]

    def add(self, into, term):
        into[...] = (into[...].astype(F32) + term[...].astype(F32)).astype(BF16)

    def put(self, part, into, value, last):
        if last:
            layer, low, high, _ = part
            self.result[layer, :, low:high] = value
        else:
            into[...] = value.astype(BF16)

    def buffer(self, k, at, name):
        ref = self.buffers[self.groups[k][at][3]][name]
        return ref.at[(k // 2) % ref.shape[0]]

    def absorb(self, k, at, step):
        part = self.groups[k][at]
        steps = self.steps(part[3])
        if step == 0:
            return ""
        axis, done = steps[step - 1], steps[: step - 1].replace("f", "")
        copies = self.copies.pop((k, at, step - 1))
        last = step == len(steps)
        if axis in "xy":
            copies[0].wait_recv()
            total = self.view(part, done + axis)
            value = total[...].astype(F32) + self.buffer(k, at, axis)[...].astype(F32)
            self.put(part, total, value, last)
        elif axis == "f":
            near, far, third = copies
            done = done.replace("z", "")
            total = self.view(part, done + "z")
            slots = self.buffer(k, at, "z")
            near.wait_recv()
            far.wait_recv()
            value = total[...].astype(F32) + slots[0].astype(F32) + slots[1].astype(F32)
            self.put(part, total, value, last)

            @pl.when(self.inner)
            def _():
                third.wait_recv()
                self.put(part, total, value + slots[2].astype(F32), last)

            done = done + "z"
            return done
        return done + axis

    def stage(self, k, at, step):
        part = self.groups[k][at]
        steps = self.steps(part[3])
        p = self.p
        if step < len(steps) and steps[step] == "f":
            near, far, third, relay, far_number = self.copies.pop((k, at, step - 1))
            done = steps[: step - 1]
            slots = self.buffer(k, at, "z")
            piece = self.view(part, done, z=p.z ^ 2)
            onward = self.sender.make(piece, slots.at[1], self.over_z_bit(2), far_number)

            @pl.when(self.inner)
            def _():
                relay.wait_recv()
                self.add(piece, slots.at[3])
                onward.start()

            self.only_inner.append(onward)
            self.copies[k, at, step] = (near, far, third)
            return
        done = self.absorb(k, at, step)
        if step == len(steps):
            self.measure(part)
            return
        axis = steps[step]
        if axis == "z":
            slots = self.buffer(k, at, "z")
            near = self.sender.start(
                self.view(part, done, z=p.z ^ 1), slots.at[0], self.over_z_bit(1)
            )
            far_number = self.sender.count
            far = self.sender.make(
                self.view(part, done, z=p.z ^ 2), slots.at[1], self.over_z_bit(2)
            )
            across = self.view(part, done, z=p.z ^ 3)
            third = self.sender.make(across, slots.at[2], self.over_z_bit(3))
            relay = self.sender.make(across, slots.at[3], self.over_z_bit(1))

            @pl.when(self.inner)
            def _():
                third.start()

            @pl.when(jnp.logical_not(self.inner))
            def _():
                relay.start()
                far.start()

            self.only_inner.append(third)
            self.only_outer += [relay, far]
            self.copies[k, at, step] = (near, far, third, relay, far_number)
        else:
            flip = {axis: 1 - (p.x if axis == "x" else p.y)}
            self.copies[k, at, step] = [
                self.sender.start(
                    self.view(part, done, **flip), self.buffer(k, at, axis), self.over(axis)
                )
            ]

    def measure(self, part):
        layer, low, high, _ = part
        total = self.result[layer, :, low:high]
        squares = total * total + EPS_SQUARE
        self.by_column[layer][:, low:high] = jnp.sum(squares, axis=0, keepdims=True)
        lane = lax.broadcasted_iota(jnp.int32, (1, 128), 1)
        for which, (first, end) in enumerate(self.cuts):
            if first <= low < end:
                term = jnp.sum(squares, axis=1, keepdims=True)
                self.by_row[...] += jnp.where(lane == layer * 4 + which, term, 0.0)

    def start(self):
        k = self.started
        self.started += 1
        for at in range(len(self.groups[k])):
            self.stage(k, at, 0)
        self.flying[k] = (1, self.clock)

    def offer(self):
        self.offered += 1

    def burst(self):
        while self.started < min(self.offered, 1):
            self.start()

    def poll(self, lag=LAG):
        self.clock += 1
        for k in list(self.flying):
            step, since = self.flying[k]
            if self.clock - since < lag:
                continue
            for at in range(len(self.groups[k])):
                self.stage(k, at, step)
            if step == 4:
                del self.flying[k]
            else:
                self.flying[k] = (step + 1, self.clock)
        if self.started < self.offered and len(self.flying) < 12:
            self.start()


def row_tiles(length, body):
    def step(i, carry):
        body(pl.ds(pl.multiple_of(i * TILE, TILE), TILE))
        return carry

    lax.fori_loop(0, length // TILE, step, 0)


def normalised(rows):
    centre = rows - jnp.mean(rows, axis=-1, keepdims=True)
    spread = jnp.mean(centre * centre, axis=-1, keepdims=True)
    rise = lax.rsqrt(spread + 1e-06)
    return centre * rise, rise


def encode_segments(counts, slots, qe, ke):
    length = qe.shape[0]
    place = lax.broadcasted_iota(jnp.int32, (length, 128), 0)
    lane = lax.broadcasted_iota(jnp.int32, (length, 128), 1) % HEAD_DIM
    image = jnp.zeros((length, 128), jnp.int32)
    total = jnp.int32(0)
    for slot in range(slots):
        total = total + counts[slot]
        image = image + (place >= total).astype(jnp.int32)
    hit = image == lane
    ke[...] = jnp.where(hit, 1.0, 0.0).astype(BF16)
    qe[...] = jnp.where(jnp.logical_or(hit, lane > slots), 0.0, -BIG).astype(BF16)


def attention_forward(qkv, qe, ke, log_total, mixed, between):
    length, width = mixed.shape
    lane = lax.broadcasted_iota(jnp.int32, (length, 128), 1)

    def pair(at, carry):
        low = pl.multiple_of(at * 128, 128)
        query = qkv[:, pl.ds(low, 128)] * jnp.asarray(0.125, BF16)
        keys = qkv[:, pl.ds(width + low, 128)]
        values = qkv[:, pl.ds(2 * width + low, 128)].T
        outs = []
        for half in range(2):
            own = (lane < HEAD_DIM) if half == 0 else (lane >= HEAD_DIM)
            q = jnp.where(own, query, qe[...])
            k = jnp.where(own, keys, ke[...])
            scores = dot(k, q, NT)
            top = jnp.max(scores, axis=0, keepdims=True)
            raised = jnp.exp(scores - top)
            total = jnp.sum(raised, axis=0, keepdims=True)
            rows = slice(half * HEAD_DIM, (half + 1) * HEAD_DIM)
            outs.append(dot(values[rows], raised.astype(BF16), NN) / total)
            log_total[pl.ds(at * 2 + half, 1), :] = top + jnp.log(total)
        mixed[:, pl.ds(low, 128)] = jnp.concatenate(outs, axis=0).T.astype(BF16)
        return carry

    for at in range(width // 128):
        lax.fori_loop(at, at + 1, pair, 0)
        between()


def attention_backward(qkv, qe, ke, log_total, d_mixed, between):
    length, width = d_mixed.shape
    lane = lax.broadcasted_iota(jnp.int32, (length, 128), 1)

    def pair(at, carry):
        low = pl.multiple_of(at * 128, 128)
        query = qkv[:, pl.ds(low, 128)] * jnp.asarray(0.125, BF16)
        keys = qkv[:, pl.ds(width + low, 128)]
        values = qkv[:, pl.ds(2 * width + low, 128)]
        d_out = d_mixed[:, pl.ds(low, 128)]
        keys_t = keys.T
        d_query, d_keys, d_values = [], [], []
        for half in range(2):
            own = (lane < HEAD_DIM) if half == 0 else (lane >= HEAD_DIM)
            q = jnp.where(own, query, qe[...])
            k = jnp.where(own, keys, ke[...])
            v = jnp.where(own, values, jnp.zeros_like(values))
            probs = jnp.exp(dot(k, q, NT) - log_total[pl.ds(at * 2 + half, 1), :])
            d_probs = dot(v, d_out, NT)
            mean = jnp.sum(probs * d_probs, axis=0, keepdims=True)
            d_scores = (probs * (d_probs - mean)).astype(BF16)
            d_values.append(dot(probs.astype(BF16), d_out, NN))
            d_keys.append(dot(d_scores, query, NN))
            rows = slice(half * HEAD_DIM, (half + 1) * HEAD_DIM)
            d_query.append(dot(keys_t[rows], d_scores, NN))
        first = lane < HEAD_DIM
        d_q = jnp.concatenate(d_query, axis=0).T * 0.125
        qkv[:, pl.ds(low, 128)] = d_q.astype(BF16)
        qkv[:, pl.ds(width + low, 128)] = jnp.where(first, *d_keys).astype(BF16)
        qkv[:, pl.ds(2 * width + low, 128)] = jnp.where(first, *d_values).astype(BF16)
        return carry

    for at in range(width // 128):
        lax.fori_loop(at, at + 1, pair, 0)
        between()


class Exchange:
    def __init__(self, place, sender, out, into):
        self.p, self.sender, self.out, self.into = place, sender, out, into
        self.turn = 0
        self.copies = {}
        length = out.shape[1]
        cut = (length // TILE + 1) // 2 * TILE
        self.chunks = ((0, cut), (cut, length))

    def send(self, compute):
        slot = self.turn % 2
        for copy in self.copies.get(slot, ()):
            copy.wait_send()
            self.sender.sent = [item for item in self.sender.sent if item is not copy]
        self.copies[slot] = []
        for low, high in self.chunks:
            self.out[slot, low:high, :] = compute(low, high).astype(BF16)
            piece = self.out.at[slot, low:high, :]
            self.copies[slot].append(
                self.sender.start(piece, self.into.at[slot, low:high, :], self.p.over_core())
            )

    def swap_halves(self, compute, meanwhile, body):
        slot = self.turn % 2
        for copy in self.copies.get(slot, ()):
            copy.wait_send()
            self.sender.sent = [item for item in self.sender.sent if item is not copy]
        length = self.out.shape[1]
        count = (length // TILE + 1) // 2 * TILE
        first = (length // 2 // TILE) * TILE
        core = self.p.core
        theirs = pl.ds(pl.multiple_of((1 - core) * first, TILE), count)
        self.out[slot, theirs, :] = compute(theirs).astype(BF16)
        copy = self.sender.start(
            self.out.at[slot, theirs, :], self.into.at[slot, theirs, :], self.p.over_core()
        )
        mine = pl.ds(pl.multiple_of(core * first, TILE), count)
        own = compute(mine).astype(BF16).astype(F32)
        meanwhile()
        copy.wait_recv()
        body(mine, own + self.into[slot, mine, :].astype(F32))

    def take(self, body, between=lambda: None):
        slot = self.turn % 2
        self.turn += 1
        for (low, high), copy in zip(self.chunks, self.copies[slot]):
            copy.wait_recv()

            def step(i, carry, low=low):
                rows = pl.ds(pl.multiple_of(low + i * TILE, TILE), TILE)
                total = self.out[slot, rows, :].astype(F32) + self.into[slot, rows, :].astype(F32)
                body(rows, total)
                return carry

            lax.fori_loop(0, (high - low) // TILE, step, 0)
            if high != self.chunks[-1][1]:
                between()


def grand_total(value):
    return jnp.sum(jnp.sum(value, axis=1, keepdims=True), axis=0, keepdims=True)


def store(grads, low, value):
    cols = slice(low, low + value.shape[1])
    grads[:, :, :, :, cols] = value.astype(BF16).reshape(grads.shape[:4] + value.shape[1:])


def flat(w, low, high):
    value = w[:, :, :, :, low:high]
    return value.reshape(-1, high - low)


def gelu_and_slope(hidden):
    cdf = 0.5 * (1.0 + lax.erf(hidden * (0.5**0.5)))
    slope = cdf + hidden * (jnp.exp(-0.5 * hidden * hidden) * 0.3989422804014327)
    return hidden * cdf, slope


def forward_kernel(
    n_dp, cuts, slots,
    counts, patches, cotangent, qkv_w, out_w, up_w, down_w, norms,
    o_weights, o_rows, o_middle, o_normed_a, o_qkv, o_mixed, o_normed_b, o_active, o_slope, o_log,
    o_rounded, o_grads, o_result, o_squares,
    w0, w1, grads, rounded, turned, rows, middle, normed_a, qkv, mixed, normed_b, active, slope, log_total, final,
    x_out, x_in, qe, ke, send_sems, recv_sems, local_sems,
):
    layers, half = 2, patches.shape[0]
    length = 2 * half
    c_qkv, c_out, c_up, c_down = cuts
    p = Place(n_dp)
    wait_for_all = p.greet()
    sender = Sender(send_sems, recv_sems)
    local = []

    def move(src, dst):
        copy = pltpu.make_async_copy(src, dst, local_sems.at[len(local)])
        copy.start()
        local.append(copy)
        return copy

    weights = (w0, w1)
    local_heads = qkv_w.shape[3]

    def master(layer, which):
        if which == 0:
            return [qkv_w[layer, part] for part in range(3)]
        return [(out_w, up_w, down_w)[which - 1][layer]]

    def place_pieces(layer):
        for which, (low, _) in enumerate(cuts):
            for part, value in enumerate(master(layer, which)):
                cols = slice(low + part * local_heads, low + part * local_heads + value.shape[1])
                weights[layer][p.z, p.y, p.x, :, cols] = value.astype(BF16)

    place_pieces(0)
    wait_for_all()
    starts = [(l, low) for l in range(layers) for low in range(0, c_down[1], GROUP)]
    groups = [parts_of(l, low, turn) for turn, (l, low) in enumerate(starts)]
    per = len(groups) // layers
    gather = Gather(p, sender, weights, groups)
    gather.poll()
    own_rows = pl.ds(pl.multiple_of(p.core * half, half), half)
    rows[0, own_rows, :] = patches[...].astype(F32)
    swap = sender.start(rows.at[0, own_rows, :], rows.at[0, own_rows, :], p.over_core())
    place_pieces(1)
    gather.poll()
    total = jnp.int32(0)
    for slot in range(slots):
        total = total + counts[slot]
    place = lax.broadcasted_iota(jnp.int32, (half, 1), 0) + p.core * half
    final[own_rows, :] = jnp.where(place < total, cotangent[...].astype(F32), 0.0)
    swap_back = sender.start(final.at[own_rows, :], final.at[own_rows, :], p.over_core())
    encode_segments(counts, slots, qe, ke)
    gather.poll()
    swap.wait_recv()
    exchange = Exchange(p, sender, x_out, x_in)

    def norm_into(target, layer, which, at, value):
        hat, _ = normalised(value)
        gain, shift = norms[layer, which : which + 1, :], norms[layer, which + 1 : which + 2, :]
        target[layer, at, :] = (hat * gain + shift).astype(BF16)

    row_tiles(length, lambda at: norm_into(normed_a, 0, 0, at, rows[0, at, :]))
    gather.poll()
    lane = lax.broadcasted_iota(jnp.int32, (1, 128), 1)
    squares = jnp.zeros((1, 128), F32)
    for layer in range(layers):
        for which in range(4):
            total = sum(grand_total(value * value) for value in master(layer, which))
            squares = squares + jnp.where(lane == layer * 4 + which, total, 0.0)
    o_squares[...] = squares
    saves = [(rows, o_rows, 0), (normed_a, o_normed_a, 0)]
    gather.poll()
    swap_back.wait_recv()
    swap_back.wait_send()
    sender.sent = [item for item in sender.sent if item is not swap_back]

    def round_step(at):
        rounded[at, :] = final[at, :].astype(BF16)

    row_tiles(length, round_step)
    move(rounded, o_rounded)

    def save(*items):
        for src, dst, layer in items:
            move(src.at[layer], dst.at[layer])

    save(*saves)
    for layer in range(layers):
        w, base = weights[layer], per * layer
        for k in range(c_qkv[1] // GROUP):
            gather.ready(base + k)
            cols = slice(k * GROUP, (k + 1) * GROUP)
            value = dot(normed_a[layer], flat(w, cols.start, cols.stop), NN)
            qkv[layer, :, cols] = value.astype(BF16)
        attention_forward(
            qkv.at[layer], qe, ke, log_total.at[layer], mixed.at[layer], gather.poll
        )
        save((qkv, o_qkv, layer), (log_total, o_log, layer), (mixed, o_mixed, layer))
        gather.ready(base + c_out[0] // GROUP)
        w_out = flat(w, *c_out)
        exchange.send(lambda low, high: dot(mixed[layer, low:high, :], w_out, NT))
        gather.poll()

        def mid_step(at, total):
            value = rows[layer, at, :] + total
            middle[layer, at, :] = value
            norm_into(normed_b, layer, 2, at, value)

        exchange.take(mid_step, gather.poll)
        save((middle, o_middle, layer), (normed_b, o_normed_b, layer))
        gather.poll()
        for k in range(c_up[0] // GROUP, c_up[1] // GROUP):
            gather.ready(base + k)
            low = k * GROUP
            cols = slice(low - c_up[0], low - c_up[0] + GROUP)
            hidden = dot(normed_b[layer], flat(w, low, low + GROUP), NN)
            act, rise = gelu_and_slope(hidden)
            active[layer, :, cols] = act.astype(BF16)
            slope[layer, :, cols] = rise.astype(BF16)
        last_layer = layer + 1 == layers
        if last_layer:
            turned[...] = rounded[...].T
            for low in range(c_down[0], c_down[1], GROUP):
                cols = slice(low - c_down[0], low - c_down[0] + GROUP)
                store(grads, low - c_up[0], dot(turned[...], active[layer, :, cols], NN))
                gather.poll()
            turned[...] = normed_b[layer].T
            cols = slice(c_down[0] - c_up[0], c_down[1] - c_up[0])
            move(grads.at[:, :, :, :, cols], o_grads.at[:, :, :, :, cols])
            cols = slice(0, c_up[1])
            move(w.at[:, :, :, :, cols], o_weights.at[layer, :, :, :, :, cols])
        else:
            save((active, o_active, layer), (slope, o_slope, layer))

        def mlp_back(low):
            cols = slice(low - c_down[0], low - c_down[0] + GROUP)
            d_active = dot(rounded[...], flat(w, low, low + GROUP), NN)
            d_hidden = (d_active * slope[layer, :, cols].astype(F32)).astype(BF16)
            slope[layer, :, cols] = d_hidden
            store(grads, cols.start, dot(turned[...], d_hidden, NN))
            move(grads.at[:, :, :, :, cols], o_grads.at[:, :, :, :, cols])
            move(slope.at[layer, :, cols], o_slope.at[layer, :, cols])

        for k in range(c_down[0] // GROUP, c_down[1] // GROUP - 1):
            gather.ready(base + k)
            low = k * GROUP
            if last_layer:
                mlp_back(low)
            cols = slice(low - c_down[0], low - c_down[0] + GROUP)
            term = dot(active[layer, :, cols], flat(w, low, low + GROUP), NT)
            if k * GROUP == c_down[0]:
                final[...] = term
            else:
                final[...] += term
        gather.ready(base + c_down[1] // GROUP - 1)
        w_down = flat(w, c_down[1] - GROUP, c_down[1])
        cols = slice(c_down[1] - c_down[0] - GROUP, c_down[1] - c_down[0])
        if layer + 1 < layers:
            exchange.send(
                lambda low, high: final[low:high, :]
                + dot(active[layer, low:high, cols], w_down, NT)
            )
            move(w, o_weights.at[layer])
            gather.poll()

            def next_step(at, total):
                value = middle[layer, at, :] + total
                rows[layer + 1, at, :] = value
                norm_into(normed_a, layer + 1, 0, at, value)

            exchange.take(next_step, gather.poll)
            save((rows, o_rows, layer + 1), (normed_a, o_normed_a, layer + 1))
            gather.poll()
        else:
            def last_step(at, total):
                final[at, :] = middle[layer, at, :] + total

            exchange.swap_halves(
                lambda at: final[at, :] + dot(active[layer, at, cols], w_down, NT),
                lambda: mlp_back(c_down[1] - GROUP),
                last_step,
            )
    o_result[...] = final[own_rows, :].astype(BF16)
    sender.drain()
    gather.drain()
    for copy in local:
        copy.wait()


def backward_kernel(
    n_dp, cuts, totals, slots,
    counts, norms, squares, row_states, qkv_c, out_c, up_c, down_c, norm_state,
    i_weights, i_rows, i_middle, i_normed_a, i_qkv, i_mixed, i_normed_b, i_active, i_slope, i_log,
    i_rounded, i_grads, o_input, o_sums, o_rows, o_columns, o_scalars, o_steps, o_own,
    g0, g1, buffers,
    w, kept, normed_a, qkv, mixed, normed_b, active, slope, log_total,
    o_pieces, grad, rounded, turned, x_out, x_in, qe, ke, by_row, row_in, square, small, few, last,
    send_sems, recv_sems, local_sems,
):
    layers, half = 2, o_input.shape[0]
    length = 2 * half
    c_qkv, c_out, c_up, c_down = cuts
    p = Place(n_dp)
    wait_for_all = p.greet()
    sender = Sender(send_sems, recv_sems)
    count, outward = [0], []

    def load(src, dst):
        copy = pltpu.make_async_copy(src, dst, local_sems.at[count[0]])
        count[0] += 1
        copy.start()
        outward.append(copy)
        return copy

    def load_mlp(l):
        cols = slice(c_up[0], c_down[1])
        return dict(
            active=load(i_active.at[l], active),
            slope=load(i_slope.at[l], slope),
            weights=load(i_weights.at[l, :, :, :, :, cols], w.at[:, :, :, :, cols]),
            normed_b=load(i_normed_b.at[l], normed_b),
        )

    def load_attention(l):
        cols = slice(c_qkv[0], c_out[1])
        return dict(
            mixed=load(i_mixed.at[l], mixed),
            weights=load(i_weights.at[l, :, :, :, :, cols], w.at[:, :, :, :, cols]),
            qkv=load(i_qkv.at[l], qkv),
            log=load(i_log.at[l], log_total),
            normed_a=load(i_normed_a.at[l], normed_a),
        )

    top = layers - 1
    readies = []
    for low, high in (c_down, c_up):
        cols = slice(low - c_up[0], high - c_up[0])
        readies.append(
            load(i_grads.at[:, :, :, :, cols], (g0, g1)[top].at[:, :, :, :, low:high])
        )
    up_cols = slice(*c_up)
    mlp = dict(
        slope=load(i_slope.at[top], slope),
        weights=load(i_weights.at[top, :, :, :, :, up_cols], w.at[:, :, :, :, up_cols]),
        rounded=load(i_rounded, rounded),
        middle=load(i_middle.at[top], kept),
    )
    att = load_attention(top)
    own_rows = pl.ds(pl.multiple_of(p.core * half, half), half)
    encode_segments(counts, slots, qe, ke)
    norm_sums = [small[layer][4] for layer in range(layers)]
    by_row[...] = jnp.zeros_like(by_row)
    for sums in norm_sums:
        sums[...] = jnp.zeros_like(sums)
    exchange = Exchange(p, sender, x_out, x_in)
    grads = (g0, g1)
    starts = list(range(c_down[0], c_down[1], GROUP)) + list(range(c_up[0], c_up[1], GROUP))
    starts += list(range(c_out[0], c_out[1], GROUP)) + list(range(c_qkv[0], c_qkv[1], GROUP))
    starts = [(l, low) for l in reversed(range(layers)) for low in starts]
    groups = [
        [(layer, a, b, order[::-1]) for layer, a, b, order in parts_of(l, low, turn)]
        for turn, (l, low) in enumerate(starts)
    ]
    columns_of_layer = [small[layer][0] for layer in range(layers)]
    scatter = Scatter(
        p, sender, grads, groups, buffers, o_pieces, cuts, by_row, columns_of_layer
    )
    wait_for_all()
    for ready in readies:
        ready.wait()
        for _ in range((c_up[1] - c_up[0]) // GROUP):
            scatter.offer()
        if scatter.started == 0:
            scatter.poll()
    mlp["rounded"].wait()

    def norm_step(layer, which, at, total):
        hat, rise = normalised(kept[at, :])
        norm_sums[layer][which : which + 1, :] += jnp.sum(total * hat, axis=0, keepdims=True)
        norm_sums[layer][which + 1 : which + 2, :] += jnp.sum(total, axis=0, keepdims=True)
        d_hat = total * norms[layer, which : which + 1, :]
        flat_mean = jnp.mean(d_hat, axis=-1, keepdims=True)
        hat_mean = jnp.mean(d_hat * hat, axis=-1, keepdims=True)
        value = grad[at, :] + rise * (d_hat - flat_mean - hat * hat_mean)
        grad[at, :] = value
        rounded[at, :] = value.astype(BF16)

    def widen_step(at):
        grad[at, :] = rounded[at, :].astype(F32)

    row_tiles(length, widen_step)
    scatter.poll()
    for layer in reversed(range(layers)):
        if layer < top:
            turned[...] = rounded[...].T
            mlp["active"].wait()
            for low in range(c_down[0], c_down[1], GROUP):
                cols = slice(low - c_down[0], low - c_down[0] + GROUP)
                store(grads[layer], low, dot(turned[...], active[:, cols], NN))
                scatter.offer()
                if low % (2 * GROUP):
                    scatter.poll()
            mlp["weights"].wait()
            mlp["slope"].wait()
            for low in range(c_down[0], c_down[1], GROUP):
                cols = slice(low - c_down[0], low - c_down[0] + GROUP)
                d_active = dot(rounded[...], flat(w, low, low + GROUP), NN)
                slope[:, cols] = (d_active * slope[:, cols].astype(F32)).astype(BF16)
                if low % (2 * GROUP):
                    scatter.poll()
        else:
            mlp["weights"].wait()
            mlp["slope"].wait()
        w_up = flat(w, *c_up)
        exchange.send(lambda low, high: dot(slope[low:high, :], w_up, NT))
        scatter.poll()
        if layer < top:
            mlp["normed_b"].wait()
            turned[...] = normed_b[...].T
            for low in range(c_up[0], c_up[1], GROUP):
                cols = slice(low - c_up[0], low - c_up[0] + GROUP)
                store(grads[layer], low, dot(turned[...], slope[:, cols], NN))
                scatter.offer()
                if low % (2 * GROUP):
                    scatter.poll()
        mlp["middle"].wait()
        exchange.take(lambda at, total: norm_step(layer, 2, at, total), scatter.poll)
        rows_load = load(i_rows.at[layer], kept)
        if layer:
            mlp = load_mlp(layer - 1)
        scatter.poll()
        turned[...] = rounded[...].T
        att["mixed"].wait()
        store(grads[layer], c_out[0], dot(turned[...], mixed[...], NN))
        scatter.offer()
        att["weights"].wait()
        mixed[...] = dot(rounded[...], flat(w, *c_out), NN).astype(BF16)
        scatter.poll()
        att["qkv"].wait()
        att["log"].wait()
        attention_backward(qkv, qe, ke, log_total, mixed, scatter.poll)
        w_qkv = flat(w, *c_qkv)
        exchange.send(lambda low, high: dot(qkv[low:high, :], w_qkv, NT))
        att["normed_a"].wait()
        turned[...] = normed_a[...].T
        for low in range(c_qkv[0], c_qkv[1], GROUP):
            store(grads[layer], low, dot(turned[...], qkv[:, low : low + GROUP], NN))
            scatter.offer()
        scatter.poll()
        rows_load.wait()
        exchange.take(lambda at, total: norm_step(layer, 0, at, total), scatter.poll)
        if layer:
            mlp["middle"] = load(i_middle.at[layer - 1], kept)
            att = load_attention(layer - 1)
        scatter.poll()
    load(grad.at[own_rows, :], o_input)
    rounds = Rounds(p, sender)
    in_plane, in_z = {}, {}

    def small_plane(layer):
        col, _, col_plane, _, norm, _, norm_plane, _ = small[layer]
        in_plane[layer] = (rounds.plane(col, col_plane), rounds.plane(norm, norm_plane))

    def small_z(layer):
        _, col, col_plane, col_z, _, norm, norm_plane, norm_z = small[layer]
        col[...] = slot_sum(in_plane[layer][0], col_plane)
        first = rounds.along_z(col, col_z)
        norm[...] = slot_sum(in_plane[layer][1], norm_plane)
        in_z[layer] = (first, rounds.along_z(norm, norm_z))

    while scatter.flying or scatter.started < len(groups):
        scatter.poll(1)
        if in_plane and not in_z:
            small_z(1)
        if not in_plane and min(scatter.flying, default=len(groups)) >= len(groups) // 2:
            small_plane(1)
    if not in_z:
        small_z(1)
    scatter.drain()
    small_plane(0)
    load(o_pieces, o_sums)
    lane = lax.broadcasted_iota(jnp.int32, (1, 128), 1)
    entries = [(layer, which) for layer in range(layers) for which in range(4)]
    columns_of = (None, out_c, up_c, down_c)

    def old_columns(layer, which):
        if which == 0:
            return jnp.concatenate([qkv_c[part, layer : layer + 1, :] for part in range(3)], axis=1)
        return columns_of[which][layer : layer + 1, :]

    swap = sender.start(by_row, row_in, p.over_core())
    square[...] = jnp.zeros_like(square)
    olds = jnp.zeros((1, 128), F32)
    for at, (layer, which) in enumerate(entries):
        old = row_states[which][layer : layer + 1, :]
        square[at : at + 1, 0 : old.shape[1]] = old
        share = 0.5
        if which % 2:
            old, share = old_columns(layer, which), 1.0 / n_dp
        olds = olds + jnp.where(lane == 16 + at, jnp.sum(old, axis=1, keepdims=True) * share, 0.0)
    depth = o_pieces.shape[1]
    width = norm_state.shape[2]
    few_term, few_mid, few_plane, few_z = few
    sums = jnp.sum(by_row[...], axis=0, keepdims=True) + olds + pltpu.roll(squares[...], 8, 1)
    few_term[...] = jnp.broadcast_to(sums, few_term.shape)
    few_plane_copies = rounds.plane(few_term, few_plane, True)
    old_rows = square[...].T[0:depth, :]
    small_z(0)
    few_mid[...] = slot_sum(few_plane_copies, few_plane)
    few_z_copies = rounds.along_z(few_mid, few_z)
    swap.wait_recv()
    counts_of = jnp.ones((1, 128), F32)
    for at, (layer, which) in enumerate(entries):
        counts_of = jnp.where(lane == at, 1.0 / totals[which], counts_of)
    new_rows = DECAY * old_rows + (1.0 - DECAY) * (by_row[...] + row_in[...]) * counts_of
    square[...] = jnp.zeros_like(square)
    square[0:depth, :] = new_rows
    o_rows[...] = square[...].T
    by_row_rise = lax.rsqrt(new_rows)
    columns = []
    for layer in range(layers):
        columns.append(slot_sum(in_z[layer][0], small[layer][3]))
    norm_totals = [slot_sum(in_z[layer][1], small[layer][7]) for layer in range(layers)]
    scalars = slot_sum(few_z_copies, few_z)[0:1, :]
    o_scalars[...] = scalars
    steps = jnp.zeros((1, 128), F32)
    for at, (layer, which) in enumerate(entries):
        low, high = cuts[which]
        fresh = columns[layer][:, low:high]
        new_cols = DECAY * old_columns(layer, which) + (1.0 - DECAY) / D * fresh
        o_columns[layer, :, low:high] = new_cols
        mean = row_mean(scalars, at, which, totals)
        by_col = lax.rsqrt(new_cols)
        step = o_pieces[layer, :, low:high] * by_row_rise[:, at : at + 1] * by_col
        steps = steps + jnp.where(lane == at, grand_total(step * step) * mean, 0.0)
    both = norm_totals + [norms[layer] for layer in range(layers)]
    me = p.z * 4 + p.y * 2 + p.x
    at_row = lax.broadcasted_iota(jnp.int32, (D, 128), 0)
    at_col = lax.broadcasted_iota(jnp.int32, (D, 128), 1)
    pick = jnp.where(at_row == at_col + me * depth, 1.0, 0.0)
    o_own[0:16, :] = lax.dot_general(
        jnp.concatenate(both, axis=0),
        pick,
        (NN, ((), ())),
        precision=lax.Precision.HIGHEST,
        preferred_element_type=F32,
    )
    for layer in range(layers):
        mine = o_own[layer * 4 : layer * 4 + 4, 0:width]
        state = DECAY * norm_state[layer] + (1.0 - DECAY) * (mine * mine + EPS_SQUARE)
        sizes = jnp.sum(mine * mine / state, axis=1, keepdims=True) * 0.5
        for kind in range(4):
            steps = steps + jnp.where(lane == 8 + layer * 4 + kind, sizes[kind : kind + 1], 0.0)
    last_term, last_mid, last_plane, last_z = last
    last_term[...] = jnp.broadcast_to(steps, last_term.shape)
    last_copies = rounds.plane(last_term, last_plane, True)
    last_mid[...] = slot_sum(last_copies, last_plane)
    last_copies = rounds.along_z(last_mid, last_z)
    o_steps[...] = slot_sum(last_copies, last_z)[0:1, :]
    sender.drain()
    for copy in outward[-2:]:
        copy.wait()


def row_mean(scalars, at, which, totals):
    count = totals[3] if which == 3 else D
    mean = DECAY * scalars[:, 16 + at : 17 + at] / count
    return mean + (1.0 - DECAY) * scalars[:, at : at + 1] / (D * totals[which])


def apply_kernel(
    cuts, totals,
    result, grad, sums, rows, columns, scalars, steps, own, qkv_w, out_w, up_w, down_w, norms,
    norm_state,
    o_result, o_grad, g_qkv, g_out, g_up, g_down, g_norm, n_qkv, n_out, n_up, n_down, n_norm,
    k_qkv, k_out, k_up, k_down,
    qkv_rn, qkv_cn, out_rn, out_cn, up_rn, up_cn, down_rn, down_cn, moments_a, moments_f, rms,
    square,
):
    layers, depth = sums.shape[0], sums.shape[1]
    width, local = norm_state.shape[2], qkv_w.shape[3]
    o_result[...] = result[...]
    o_grad[...] = grad[...]
    lane = lax.broadcasted_iota(jnp.int32, (1, 128), 1)
    entries = [(layer, which) for layer in range(layers) for which in range(4)]
    means = jnp.ones((1, 128), F32)
    for at, (layer, which) in enumerate(entries):
        means = jnp.where(lane == at, 1.0 / (D * totals[which]), means)
        means = jnp.where(lane == 8 + at, 1.0 / D, means)
    size = jnp.sqrt(steps[...] * means)
    shrink = 1.0 / jnp.maximum(1.0, size / CLIP)
    row_news = (qkv_rn, out_cn, up_rn, down_cn)
    square[...] = rows[...].T
    by_row = lax.rsqrt(square[0:depth, :])
    for layer in range(layers):
        rms[layer : layer + 1, 0:4] = size[:, layer * 4 : layer * 4 + 4]
        rms[layer : layer + 1, 4:8] = size[:, 8 + layer * 4 : 12 + layer * 4]
        vectors = norms[layer]
        scale = jnp.sqrt(jnp.mean(vectors * vectors, axis=1, keepdims=True) + 1e-06)
        shrinks = jnp.concatenate(
            [shrink[:, 8 + layer * 4 + kind : 9 + layer * 4 + kind] for kind in range(4)], axis=0
        )
        mine = own[layer * 4 : layer * 4 + 4, 0:width]
        state = DECAY * norm_state[layer] + (1.0 - DECAY) * (mine * mine + EPS_SQUARE)
        g_norm[layer] = mine
        moments_a[layer] = state[0:2]
        moments_f[layer] = state[2:4]
        before = own[8 + layer * 4 : 12 + layer * 4, 0:width]
        n_norm[layer] = before - RATE * scale * (mine * lax.rsqrt(state) * shrinks)
    for at, (layer, which) in enumerate(entries):
        row_news[which][layer : layer + 1, :] = rows[at : at + 1, 0:depth]
        scale = jnp.sqrt(scalars[:, 8 + at : 9 + at] / (D * totals[which]) + 1e-06)
        factor = RATE * scale * shrink[:, at : at + 1]
        factor = factor * jnp.sqrt(row_mean(scalars[...], at, which, totals))
        factor = factor * by_row[:, at : at + 1]
        for part in range(3 if which == 0 else 1):
            low, high = cuts[which]
            if which == 0:
                low, high = part * local, part * local + local
                refs = [ref.at[layer, part] for ref in (qkv_w, g_qkv, n_qkv, k_qkv)]
                qkv_cn[part, layer : layer + 1, :] = columns[layer, :, low:high]
            else:
                table = (
                    (out_w, g_out, n_out, k_out),
                    (up_w, g_up, n_up, k_up),
                    (down_w, g_down, n_down, k_down),
                )
                refs = [ref.at[layer] for ref in table[which - 1]]
                new_ref = (out_rn, up_cn, down_rn)[which - 1]
                new_ref[layer : layer + 1, :] = columns[layer, :, low:high]
            grad_piece = sums[layer, :, low:high]
            new = refs[0][...] - grad_piece * factor * lax.rsqrt(columns[layer, :, low:high])
            refs[1][...] = grad_piece
            refs[2][...] = new
            refs[3][...] = new.astype(BF16)


def passes_by_xla(
    patches,
    cotangent,
    patch_counts,
    qkv_weight,
    out_weight,
    up_weight,
    down_weight,
    norms,
):
    layers = qkv_weight.shape[0]
    half = patches.shape[0]
    length = half * lax.axis_size("mp")
    same, live_all = segments(patch_counts, length)
    live = lax.dynamic_slice_in_dim(live_all, lax.axis_index("mp") * half, half)
    rows = patches.astype(jnp.float32)
    kept = []
    for layer in range(layers):
        pieces = (
            qkv_weight[layer].astype(jnp.bfloat16),
            out_weight[layer].astype(jnp.bfloat16),
            up_weight[layer].astype(jnp.bfloat16),
            down_weight[layer].astype(jnp.bfloat16),
        )
        whole = (
            lax.all_gather(pieces[0], "dp", axis=0, tiled=True),
            lax.all_gather(pieces[1], "dp", axis=1, tiled=True),
            lax.all_gather(pieces[2], "dp", axis=0, tiled=True),
            lax.all_gather(pieces[3], "dp", axis=1, tiled=True),
        )
        w_qkv, w_out, w_up, w_down = whole
        local = w_qkv.shape[2]
        normed_a = spread_rows(
            layer_norm(rows, norms[layer, 0], norms[layer, 1]).astype(jnp.bfloat16)
        )
        qkv = jnp.dot(normed_a, w_qkv.reshape(D, 3 * local), preferred_element_type=jnp.float32)
        qkv = qkv.astype(jnp.bfloat16).reshape(length, 3, local // HEAD_DIM, HEAD_DIM)
        mixed, log_total = attend(qkv, same)
        mixed = mixed.astype(jnp.bfloat16)
        middle = rows + lax.psum_scatter(
            jnp.dot(mixed, w_out, preferred_element_type=jnp.float32).astype(jnp.bfloat16),
            "mp",
            scatter_dimension=0,
            tiled=True,
        ).astype(jnp.float32)
        normed_b = spread_rows(
            layer_norm(middle, norms[layer, 2], norms[layer, 3]).astype(jnp.bfloat16)
        )
        hidden = jnp.dot(normed_b, w_up, preferred_element_type=jnp.float32)
        active = exact_gelu(hidden).astype(jnp.bfloat16)
        after = middle + lax.psum_scatter(
            jnp.dot(active, w_down, preferred_element_type=jnp.float32).astype(jnp.bfloat16),
            "mp",
            scatter_dimension=0,
            tiled=True,
        ).astype(jnp.float32)
        stored = None
        kept.append(
            (
                rows,
                normed_a,
                qkv,
                log_total,
                mixed,
                middle,
                normed_b,
                hidden,
                active,
                stored,
                pieces,
            )
        )
        rows = after
    activations = rows.astype(jnp.bfloat16)
    grad = cotangent.astype(jnp.float32) * live[:, None]
    reduced = [None] * layers
    for layer in reversed(range(layers)):
        (
            rows_in,
            normed_a,
            qkv,
            log_total,
            mixed,
            middle,
            normed_b,
            hidden,
            active,
            stored,
            pieces,
        ) = kept[layer]
        whole = (
            lax.all_gather(pieces[0], "dp", axis=0, tiled=True),
            lax.all_gather(pieces[1], "dp", axis=1, tiled=True),
            lax.all_gather(pieces[2], "dp", axis=0, tiled=True),
            lax.all_gather(pieces[3], "dp", axis=1, tiled=True),
        )
        w_qkv, w_out, w_up, w_down = whole
        local = w_qkv.shape[2]
        grad_down = spread_rows(grad.astype(jnp.bfloat16))
        g_down = jnp.einsum("tf,td->fd", active, grad_down, preferred_element_type=jnp.float32)
        d_active = jnp.einsum("td,fd->tf", grad_down, w_down, preferred_element_type=jnp.float32)
        gelu_value, gelu_back = jax.vjp(exact_gelu, hidden)
        d_hidden = gelu_back(d_active)[0].astype(jnp.bfloat16)
        g_up = jnp.einsum("td,tf->df", normed_b, d_hidden, preferred_element_type=jnp.float32)
        d_normed_b = lax.psum_scatter(
            jnp.einsum("tf,df->td", d_hidden, w_up, preferred_element_type=jnp.float32).astype(
                jnp.bfloat16
            ),
            "mp",
            scatter_dimension=0,
            tiled=True,
        ).astype(jnp.float32)
        d_middle, g_gain_b, g_shift_b = norm_back(
            middle, norms[layer, 2], norms[layer, 3], d_normed_b
        )
        grad_mid = grad + d_middle
        grad_out = spread_rows(grad_mid.astype(jnp.bfloat16))
        g_out = jnp.einsum("tc,td->cd", mixed, grad_out, preferred_element_type=jnp.float32)
        d_mixed = jnp.einsum(
            "td,cd->tc", grad_out, w_out, preferred_element_type=jnp.float32
        ).astype(jnp.bfloat16)
        d_qkv = attend_back(
            qkv, same, log_total, d_mixed.reshape(length, local // HEAD_DIM, HEAD_DIM)
        )
        d_qkv = d_qkv.reshape(length, 3 * local)
        g_qkv = jnp.einsum(
            "td,tc->dc", normed_a, d_qkv, preferred_element_type=jnp.float32
        ).reshape(D, 3, local)
        d_normed_a = lax.psum_scatter(
            jnp.einsum(
                "tc,dc->td", d_qkv, w_qkv.reshape(D, 3 * local), preferred_element_type=jnp.float32
            ).astype(jnp.bfloat16),
            "mp",
            scatter_dimension=0,
            tiled=True,
        ).astype(jnp.float32)
        d_input, g_gain_a, g_shift_a = norm_back(
            rows_in, norms[layer, 0], norms[layer, 1], d_normed_a
        )
        grad = grad_mid + d_input
        norm_terms = jnp.stack([g_gain_a, g_shift_a, g_gain_b, g_shift_b])
        reduced[layer] = (
            lax.psum_scatter(g_qkv, "dp", scatter_dimension=0, tiled=True),
            lax.psum_scatter(g_out, "dp", scatter_dimension=1, tiled=True),
            lax.psum_scatter(g_up, "dp", scatter_dimension=0, tiled=True),
            lax.psum_scatter(g_down, "dp", scatter_dimension=1, tiled=True),
            lax.psum(norm_terms, "mp"),
        )
    return activations, grad, [item[:4] for item in reduced], jnp.stack([item[4] for item in reduced])


def step_by_kernels(
    patches,
    cotangent,
    patch_counts,
    qkv_weight,
    out_weight,
    up_weight,
    down_weight,
    norms,
    qkv_rows,
    qkv_cols,
    out_rows,
    out_cols,
    up_rows,
    up_cols,
    down_rows,
    down_cols,
    norm_state,
):
    layers, depth, _, local = qkv_weight.shape
    n_dp = lax.axis_size("dp")
    nz, half, wide = n_dp // 4, patches.shape[0], up_weight.shape[2]
    length, slots = 2 * half, patch_counts.shape[0]
    ends = [0, 3 * local, 4 * local, 4 * local + wide, 4 * local + 2 * wide]
    cuts = tuple(zip(ends[:-1], ends[1:]))
    totals = tuple(2.0 * (high - low) for low, high in cuts)
    columns, n_groups = ends[-1], layers * ends[-1] // GROUP
    masters = (
        qkv_weight.transpose(0, 2, 1, 3),
        out_weight.transpose(0, 2, 1),
        up_weight,
        down_weight.transpose(0, 2, 1),
    )
    states_by_row = (qkv_rows, out_cols, up_rows, down_cols)
    states_by_column = (qkv_cols.transpose(1, 0, 2), out_rows, up_cols, down_rows)
    vmem, smem, hbm = [
        pl.BlockSpec(memory_space=space) for space in (pltpu.VMEM, pltpu.SMEM, pl.ANY)
    ]
    shape = jax.ShapeDtypeStruct
    whole = (nz, 2, 2, depth, columns)
    mlp_part = (nz, 2, 2, depth, 2 * wide)
    rows_f32, rows_bf16 = ((length, D), F32), ((length, D), BF16)
    kept = [
        rows_f32,
        rows_f32,
        rows_bf16,
        ((length, 3 * local), BF16),
        ((length, local), BF16),
        rows_bf16,
        ((length, wide), BF16),
        ((length, wide), BF16),
        ((8, length), F32),
    ]
    saved = [shape((layers,) + dims, kind) for dims, kind in kept]
    line = shape((1, 128), F32)
    sems = [
        pltpu.SemaphoreType.DMA((420,)),
        pltpu.SemaphoreType.DMA((420,)),
        pltpu.SemaphoreType.DMA((48,)),
    ]
    codes = [pltpu.VMEM((length, 128), BF16)] * 2
    swaps = [pltpu.VMEM((2, length, D), BF16)] * 2

    def around(dims, plane):
        return [pltpu.VMEM(dims, F32)] * 2 + [
            pltpu.VMEM((places,) + dims, F32) for places in (plane, nz)
        ]

    outs = pl.pallas_call(
        functools.partial(forward_kernel, n_dp, cuts, slots),
        out_shape=[shape((layers,) + whole, BF16)]
        + saved
        + [shape((length, D), BF16), shape(mlp_part, BF16), shape((half, D), BF16), line],
        in_specs=[smem] + [vmem] * 7,
        out_specs=[hbm] * (3 + len(saved)) + [vmem] * 2,
        scratch_shapes=[pltpu.VMEM(whole, BF16)] * layers
        + [
            pltpu.VMEM(mlp_part, BF16),
            pltpu.VMEM((length, D), BF16),
            pltpu.VMEM((D, length), BF16),
        ]
        + [pltpu.VMEM((layers,) + dims, kind) for dims, kind in kept]
        + [pltpu.VMEM((length, D), F32)]
        + swaps
        + codes
        + sems,
        compiler_params=pltpu.CompilerParams(
            collective_id=0, has_side_effects=True, vmem_limit_bytes=VMEM_BYTES
        ),
        name="forward",
    )(patch_counts, patches, cotangent, *masters, norms)
    saved, activations, squares = outs[:-2], outs[-2], outs[-1]
    buffers = {}
    for width, order in PATHS[0] + PATHS[1]:
        sizes, refs = dict(z=nz, y=2, x=2), {}
        for axis in order[::-1]:
            sizes.pop(axis)
            dims = (nz,) if axis == "z" else ()
            dims += tuple(sizes.values()) + (depth, width)
            slots_of = n_groups // layers // 2 + (2 if axis == "z" else 0)
            refs[axis] = pltpu.VMEM((slots_of,) + dims, BF16)
        buffers[order[::-1]] = refs
    small = around((1, columns), 4) + around((4, D), 4)
    grad, sums, rows, fresh, scalars, steps, norm_own = pl.pallas_call(
        functools.partial(backward_kernel, n_dp, cuts, totals, slots),
        out_shape=[
            shape((half, D), F32),
            shape((layers, depth, columns), F32),
            shape((128, 128), F32),
            shape((layers, 1, columns), F32),
            line,
            line,
            shape((16, 128), F32),
        ],
        in_specs=[smem] + [vmem] * 2 + [(vmem,) * 4] + [vmem] * 5 + [hbm] * len(saved),
        out_specs=[hbm] * 2 + [vmem] * 5,
        scratch_shapes=[pltpu.VMEM(whole, BF16)] * layers
        + [buffers]
        + [pltpu.VMEM(whole, BF16)]
        + [pltpu.VMEM(dims, kind) for dims, kind in kept[1:]]
        + [
            pltpu.VMEM((layers, depth, columns), F32),
            pltpu.VMEM((length, D), F32),
            pltpu.VMEM((length, D), BF16),
            pltpu.VMEM((D, length), BF16),
        ]
        + swaps
        + codes
        + [pltpu.VMEM((depth, 128), F32)] * 2
        + [pltpu.VMEM((128, 128), F32)]
        + [[small] * layers, around((8, 128), 8), around((8, 128), 8)]
        + sems,
        compiler_params=pltpu.CompilerParams(
            collective_id=1, has_side_effects=True, vmem_limit_bytes=VMEM_BYTES
        ),
        name="backward",
    )(
        patch_counts,
        norms,
        squares,
        states_by_row,
        *states_by_column,
        norm_state,
        *saved,
    )
    like = lambda arrays, kind: [shape(array.shape, kind) for array in arrays]
    vectors = [shape(norm_state.shape, F32)]
    states = (
        qkv_rows, states_by_column[0], out_rows, out_cols,
        up_rows, up_cols, down_rows, down_cols,
    )
    results = [shape((half, D), BF16), shape((half, D), F32)]
    results += like(masters, F32) + vectors + like(masters, F32) + vectors + like(masters, BF16)
    results += like(states, F32)
    results += [shape((layers, 2, norm_state.shape[2]), F32)] * 2 + [shape((layers, 8), F32)]
    out = pl.pallas_call(
        functools.partial(apply_kernel, cuts, totals),
        out_shape=results,
        in_specs=[vmem] * 14,
        out_specs=[vmem] * len(results),
        scratch_shapes=[pltpu.VMEM((128, 128), F32)],
        compiler_params=pltpu.CompilerParams(vmem_limit_bytes=VMEM_BYTES),
        name="apply",
    )(
        activations, grad, sums, rows, fresh, scalars, steps, norm_own, *masters, norms, norm_state
    )
    out = list(out)
    for at in (2, 7, 12):
        out[at] = out[at].transpose(0, 2, 1, 3)
        out[at + 1] = out[at + 1].transpose(0, 2, 1)
        out[at + 3] = out[at + 3].transpose(0, 2, 1)
    out[17] = out[17].transpose(1, 0, 2)
    return tuple(out)


def kernels_fit(patches, qkv_weight):
    length = 2 * patches.shape[0]
    depth, local = qkv_weight.shape[1], qkv_weight.shape[3]
    return (
        lax.axis_size("mp") == 2
        and lax.axis_size("dp") % 4 == 0
        and depth % 16 == 0
        and length % TILE == 0
        and (4 * local) % GROUP == 0
    )


def per_device(*arrays):
    if kernels_fit(arrays[0], arrays[3]):
        return step_by_kernels(*arrays)
    return step_by_xla(*arrays)


def step_by_xla(
    patches,
    cotangent,
    patch_counts,
    qkv_weight,
    out_weight,
    up_weight,
    down_weight,
    norms,
    qkv_rows,
    qkv_cols,
    out_rows,
    out_cols,
    up_rows,
    up_cols,
    down_rows,
    down_cols,
    norm_state,
):
    layers = qkv_weight.shape[0]
    activations, grad, reduced, norm_terms = passes_by_xla(
        patches, cotangent, patch_counts, qkv_weight, out_weight, up_weight, down_weight, norms
    )
    col_axes = ("mp", "dp", "mp", "dp")
    row_counts = (D, D, D, FF)
    col_counts = (3 * D, D, FF, D)
    masters = (qkv_weight, out_weight, up_weight, down_weight)
    row_states = (qkv_rows, out_rows, up_rows, down_rows)
    col_states = (qkv_cols, out_cols, up_cols, down_cols)
    entries = [(layer, which) for layer in range(layers) for which in range(4)]
    grads = [reduced[layer][which] for layer, which in entries]
    row_olds = [row_states[which][layer] for layer, which in entries]
    col_olds = [col_states[which][layer] for layer, which in entries]
    width = norm_state.shape[2]
    row_parts, col_parts = ([], [])
    for position, (layer, which) in enumerate(entries):
        matrix = grads[position].reshape(grads[position].shape[0], -1)
        square = matrix * matrix + EPS_SQUARE
        row_parts.append(jnp.sum(square, axis=1))
        col_parts.append(jnp.sum(square, axis=0).reshape(col_olds[position].shape))
    model_side = tuple(
        [
            row_parts[position] if col_axes[which] == "mp" else col_parts[position]
            for position, (layer, which) in enumerate(entries)
        ]
    )
    data_side = tuple(
        (
            col_parts[position] if col_axes[which] == "mp" else row_parts[position]
            for position, (layer, which) in enumerate(entries)
        )
    ) + (norm_terms,)
    model_sums = jax.tree.map(
        lambda part: part.astype(jnp.float32), lax.psum(for_sending(model_side), "mp")
    )
    data_sums = lax.psum(data_side, "dp")
    norm_grad = lax.dynamic_slice_in_dim(
        data_sums[len(entries)], lax.axis_index("dp") * width, width, 2
    )
    row_sums = [
        model_sums[position] if col_axes[which] == "mp" else data_sums[position]
        for position, (layer, which) in enumerate(entries)
    ]
    col_sums = [
        data_sums[position] if col_axes[which] == "mp" else model_sums[position]
        for position, (layer, which) in enumerate(entries)
    ]
    row_news = [
        DECAY * row_olds[position] + (1.0 - DECAY) * row_sums[position] / col_counts[which]
        for position, (layer, which) in enumerate(entries)
    ]
    shares = jnp.stack(
        [
            jnp.sum(row_news[position]) / size_of(col_axes[which])
            for position, (layer, which) in enumerate(entries)
        ]
    )
    row_totals = lax.psum(shares, ("dp", "mp"))
    row_means = [
        row_totals[position] / row_counts[which] for position, (layer, which) in enumerate(entries)
    ]
    col_news = [
        DECAY * col_olds[position] + (1.0 - DECAY) * col_sums[position] / row_counts[which]
        for position, (layer, which) in enumerate(entries)
    ]
    directions, step_parts, weight_parts = ([], [], [])
    for position, (layer, which) in enumerate(entries):
        matrix = grads[position].reshape(grads[position].shape[0], -1)
        second = (
            row_news[position][:, None] * col_news[position].reshape(1, -1) / row_means[position]
        )
        direction = matrix * lax.rsqrt(second)
        directions.append(direction)
        step_parts.append(jnp.sum(direction * direction))
        master = masters[which][layer]
        weight_parts.append(jnp.sum(master * master))
    own_norms = lax.dynamic_slice_in_dim(norms, lax.axis_index("dp") * width, width, 2)
    norm_state_new = DECAY * norm_state + (1.0 - DECAY) * (norm_grad * norm_grad + EPS_SQUARE)
    norm_dirs = norm_grad * lax.rsqrt(norm_state_new)
    norm_parts = jnp.sum(norm_dirs * norm_dirs, axis=2) / lax.axis_size("mp")
    step_all = jnp.concatenate(
        [jnp.stack(step_parts).reshape(layers, 4), norm_parts], axis=1
    ).reshape(-1)
    step_total, weight_total = lax.psum((step_all, jnp.stack(weight_parts)), ("dp", "mp"))
    step_total = step_total.reshape(layers, 8)
    matrix_counts = jnp.asarray(
        [float(row_counts[which] * col_counts[which]) for which in range(4)], jnp.float32
    )
    update_rms = jnp.concatenate(
        [jnp.sqrt(step_total[:, :4] / matrix_counts[None, :]), jnp.sqrt(step_total[:, 4:] / D)],
        axis=1,
    )
    news = [[None] * layers for which in range(4)]
    rows_new = [[None] * layers for which in range(4)]
    cols_new = [[None] * layers for which in range(4)]
    for position, (layer, which) in enumerate(entries):
        master = masters[which][layer]
        scale = jnp.sqrt(weight_total[position] / (row_counts[which] * col_counts[which]) + 1e-06)
        clipped = directions[position] / jnp.maximum(1.0, update_rms[layer, which] / CLIP)
        news[which][layer] = master - RATE * scale * clipped.reshape(master.shape)
        rows_new[which][layer] = row_news[position]
        cols_new[which][layer] = col_news[position]
    norm_scale = jnp.sqrt(jnp.mean(norms * norms, axis=2) + 1e-06)
    norm_clipped = norm_dirs / jnp.maximum(1.0, update_rms[:, 4:] / CLIP)[:, :, None]
    norm_new = own_norms - RATE * norm_scale[:, :, None] * norm_clipped
    grad_out = [jnp.stack([reduced[layer][which] for layer in range(layers)]) for which in range(4)]
    new_out = [jnp.stack(news[which]) for which in range(4)]
    row_out = [jnp.stack(rows_new[which]) for which in range(4)]
    col_out = [jnp.stack(cols_new[which]) for which in range(4)]
    return (
        activations,
        grad,
        grad_out[0],
        grad_out[1],
        grad_out[2],
        grad_out[3],
        norm_grad,
        new_out[0],
        new_out[1],
        new_out[2],
        new_out[3],
        norm_new,
        new_out[0].astype(jnp.bfloat16),
        new_out[1].astype(jnp.bfloat16),
        new_out[2].astype(jnp.bfloat16),
        new_out[3].astype(jnp.bfloat16),
        row_out[0],
        col_out[0],
        row_out[1],
        col_out[1],
        row_out[2],
        col_out[2],
        row_out[3],
        col_out[3],
        norm_state_new[:, 0:2],
        norm_state_new[:, 2:4],
        update_rms,
    )


def solution(mesh):
    in_specs = (
        P(("dp", "mp"), None),
        P(("dp", "mp"), None),
        P("dp"),
        P(None, "dp", None, "mp"),
        P(None, "mp", "dp"),
        P(None, "dp", "mp"),
        P(None, "mp", "dp"),
        P(),
        P(None, "dp"),
        P(None, None, "mp"),
        P(None, "mp"),
        P(None, "dp"),
        P(None, "dp"),
        P(None, "mp"),
        P(None, "mp"),
        P(None, "dp"),
        P(None, None, "dp"),
    )
    out_specs = (
        P(("dp", "mp"), None),
        P(("dp", "mp"), None),
        P(None, "dp", None, "mp"),
        P(None, "mp", "dp"),
        P(None, "dp", "mp"),
        P(None, "mp", "dp"),
        P(None, None, "dp"),
        P(None, "dp", None, "mp"),
        P(None, "mp", "dp"),
        P(None, "dp", "mp"),
        P(None, "mp", "dp"),
        P(None, None, "dp"),
        P(None, "dp", None, "mp"),
        P(None, "mp", "dp"),
        P(None, "dp", "mp"),
        P(None, "mp", "dp"),
        P(None, "dp"),
        P(None, None, "mp"),
        P(None, "mp"),
        P(None, "dp"),
        P(None, "dp"),
        P(None, "mp"),
        P(None, "mp"),
        P(None, "dp"),
        P(None, None, "dp"),
        P(None, None, "dp"),
        P(),
    )
    return jax.shard_map(
        per_device, mesh=mesh, in_specs=in_specs, out_specs=out_specs, check_vma=False
    )
```
